32 devices in a mesh: stream: 16 (over z, x, core), shard: 2 (over y).
Axes of the slice: x: 2, y: 2, z: 4, core: 2. Of those that a mesh axis runs over, the one named last changes fastest.
Arguments:
- tokens: bfloat16 [32, 768, 512], P(('stream', 'shard')), may hold values from -6 to 6
- memory: bfloat16 [32, 512, 512], P(('stream', 'shard')), may hold values from -6 to 6
- cmemory: bfloat16 [32, 512, 512], P(('stream', 'shard')), may hold values from -6 to 6
- doc_ids: int32 [32, 1792], P(('stream', 'shard')), may hold values from 0 to 7, never falling along the last dimension, each value on 1 to 448 neighbouring positions
- cotangent: bfloat16 [32, 768, 512], P(('stream', 'shard')), may hold values from -6 to 6
- qkv_weight: float32 [512, 1536], P('shard'), may hold values from -0.25 to 0.25
- out_weight: float32 [512, 512], P('shard'), may hold values from -2 to 2
- up_weight: float32 [512, 2048], P('shard'), may hold values from -0.25 to 0.25
- down_weight: float32 [2048, 512], P('shard'), may hold values from -0.125 to 0.125
- conv_weight: float32 [1536, 512], P('shard'), may hold values from -0.15625 to 0.15625
- norm_params: float32 [512, 4], P('shard'), may hold values from -0.6 to 1.4, as said below
- qkv_moment: float32 [512, 1536], P('shard'), may hold values from -48 to 48
- out_moment: float32 [512, 512], P('shard'), may hold values from -14 to 14
- up_moment: float32 [512, 2048], P('shard'), may hold values from -28 to 28
- down_moment: float32 [2048, 512], P('shard'), may hold values from -56 to 56
- norm_moment: float32 [512, 4], P('shard'), may hold values from -96 to 96
- qkv_average: float32 [512, 1536], P('shard'), may hold values from -0.25 to 0.25
- out_average: float32 [512, 512], P('shard'), may hold values from -2 to 2
- up_average: float32 [512, 2048], P('shard'), may hold values from -0.25 to 0.25
- down_average: float32 [2048, 512], P('shard'), may hold values from -0.125 to 0.125
- norm_average: float32 [512, 4], P('shard'), may hold values from -0.6 to 1.4, as said below
Outputs:
- output: bfloat16 [32, 768, 512], P(('stream', 'shard'))
- new_memory: bfloat16 [32, 512, 512], P(('stream', 'shard'))
- new_cmemory: bfloat16 [32, 512, 512], P(('stream', 'shard'))
- token_grad: bfloat16 [32, 768, 512], P(('stream', 'shard'))
- qkv_grad: float32 [512, 1536], P('shard')
- out_grad: float32 [512, 512], P('shard')
- up_grad: float32 [512, 2048], P('shard')
- down_grad: float32 [2048, 512], P('shard')
- norm_grad: float32 [512, 4], P('shard')
- qkv_momentum: float32 [512, 1536], P('shard')
- out_momentum: float32 [512, 512], P('shard')
- up_momentum: float32 [512, 2048], P('shard')
- down_momentum: float32 [2048, 512], P('shard')
- norm_momentum: float32 [512, 4], P('shard')
- qkv_smooth: float32 [512, 1536], P('shard')
- out_smooth: float32 [512, 512], P('shard')
- up_smooth: float32 [512, 2048], P('shard')
- down_smooth: float32 [2048, 512], P('shard')
- norm_smooth: float32 [512, 4], P('shard')
- qkv_updated: float32 [512, 1536], P('shard')
- out_updated: float32 [512, 512], P('shard')
- up_updated: float32 [512, 2048], P('shard')
- down_updated: float32 [2048, 512], P('shard')
- norm_updated: float32 [512, 4], P('shard')
- lifted_grads: float32 [512, 2], P('shard')
The draws below stay inside these ranges and needn't reach their ends.
Inputs may be any that keep to these rules, and one draw needn't show every extreme that they name: `doc_ids`: each stream's row names the documents of its 512 compressed slots, then its 512 memory slots, then its 768 segment tokens; ids never fall along a row. `norm_params`: columns 0 and 2 hold gains, columns 1 and 3 shifts. `norm_average`: columns 0 and 2 hold gains, columns 1 and 3 shifts.
All inputs are finite; a program needn't handle non-finite values.
Results may differ from the reference program's by a relative error of at most 0.012.
The reference program's roundings to bfloat16 on the way count: a program that leaves them out, or rounds other values in their place, can miss the bound.
Values may be sent and summed in bfloat16 or wider, within the bound.
A program may use at most 192 MiB of HBM per device.

```python
import math
import jax
import jax.numpy as jnp
import numpy as np
from jax import lax

D = 512
HEADS = 8
FF = 2048
S = 768
M = 512
C = 512
STREAMS = 32
TOKENS = 24576


def norm_table(gains, shifts):
    return jnp.stack([gains[:, 0], shifts[:, 0], gains[:, 1], shifts[:, 1]], axis=1)


def draw_norm_params(key, part):
    key = jax.random.fold_in(key, 11)
    gain_key, shift_key = jax.random.split(key)
    gains = jax.random.uniform(gain_key, (D, 2), jnp.float32, 0.6, 1.4)
    shifts = 0.3 * jax.random.truncated_normal(shift_key, -2.0, 2.0, (D, 2), jnp.float32)
    return norm_table(gains, shifts)


def draw_norm_average(key, part):
    key = jax.random.fold_in(key, 12)
    gain_key, shift_key = jax.random.split(key)
    gains = jax.random.uniform(gain_key, (D, 2), jnp.float32, 0.6, 1.4)
    shifts = 0.3 * jax.random.truncated_normal(shift_key, -2.0, 2.0, (D, 2), jnp.float32)
    return norm_table(gains, shifts)


def block_levels(rng, shape, cuts, smallest, high):
    factor_of = 1.0
    for position, shards_of in cuts:
        heights = jax.random.uniform(jax.random.fold_in(jax.random.fold_in(rng, 6), position), (shards_of,), jnp.float32, smallest / len(cuts), high / len(cuts))
        factor_of = factor_of * jnp.repeat(jnp.exp(heights), shape[position] // shards_of).reshape((-1,) + (1,) * (len(shape) - 1 - position))
    return factor_of


def split_up(number_of, total, reach, slope):
    loads = [(1 << 20) // math.isqrt(rank ** slope) + 1 for rank in range(2, number_of + 1)]
    surplus, holding = total - reach - (number_of - 1), [1] * (number_of - 1)
    while surplus > 0:
        candidates = [i for i in range(number_of - 1) if holding[i] < reach]
        mass, remaining = sum([loads[i] for i in candidates]), surplus
        for i in candidates:
            addition = min(reach - holding[i], max(1, remaining * loads[i] // mass), surplus)
            holding[i] = holding[i] + addition
            surplus = surplus - addition
    return np.array([reach] + holding)


def ragged_sizes(own_key, amount, total, most, slope):
    if amount == 2:
        one = jax.random.randint(own_key, (), max(1, total - most), min(most, total - 1) + 1)
        return jnp.stack([one, total - one])
    tallies = jnp.asarray(split_up(amount, total, most, slope), jnp.int32)
    pairs = (amount - 1) // 2
    source_of, taker = tallies[1:1 + 2 * pairs:2], tallies[2:2 + 2 * pairs:2]
    margin = jnp.minimum(source_of - 1, most - taker)
    passed = jax.random.randint(jax.random.fold_in(own_key, 1), (pairs,), 0, 1 << 20) % (margin + 1)
    tallies = tallies.at[1:1 + 2 * pairs:2].set(source_of - passed).at[2:2 + 2 * pairs:2].set(taker + passed)
    return tallies[jax.random.permutation(jax.random.fold_in(own_key, 2), amount)]


def scatter_about(rng, shape, deviation, bound, pieces=(), kind=jnp.bfloat16):
    entries = deviation * jax.random.normal(rng, shape, jnp.float32)
    if pieces:
        entries = entries * block_levels(rng, shape, pieces, -0.22, 0.18)
    return jnp.clip(entries, -bound, bound).astype(kind)


def setup_inputs(seed: int = 0) -> dict:
    splits = jax.random.split(jax.random.key(seed), 22)
    tokens = scatter_about(splits[0], (STREAMS, S, D), 1.0, 6.0, ((0, 32),))
    memory = scatter_about(splits[1], (STREAMS, M, D), 1.0, 6.0, ((0, 32),))
    cmemory = scatter_about(splits[2], (STREAMS, C, D), 1.0, 6.0, ((0, 32),))
    doc_ids = jax.vmap(lambda own: jnp.searchsorted(jnp.cumsum(ragged_sizes(own, 8, C + M + S, (C + M + S) // 4, 2)), jnp.arange(C + M + S), side="right"))(jax.random.split(splits[3], STREAMS)).reshape((STREAMS, C + M + S)).astype(jnp.int32)
    cotangent = scatter_about(splits[4], (STREAMS, S, D), 1.0, 6.0, ((0, 32),))
    qkv_weight = scatter_about(splits[5], (D, 3 * D), D ** -0.5, 0.25, ((0, 2),), jnp.float32)
    out_weight = scatter_about(splits[6], (D, D), (max(D // 64, 1)) ** -0.5, 2.0, ((0, 2),), jnp.float32)
    up_weight = scatter_about(splits[7], (D, FF), D ** -0.5, 0.25, ((0, 2),), jnp.float32)
    down_weight = scatter_about(splits[8], (FF, D), FF ** -0.5, 0.125, ((0, 2),), jnp.float32)
    conv_weight = scatter_about(splits[9], (3 * D, D), (3 * D) ** -0.5, 0.15625, ((0, 2),), jnp.float32)
    norm_params = draw_norm_params(jax.random.fold_in(splits[21], 71), 0)
    qkv_moment = scatter_about(splits[11], (D, 3 * D), (0.05 * TOKENS ** 0.5), 48.0, ((0, 2),), jnp.float32)
    out_moment = scatter_about(splits[12], (D, D), (0.015 * TOKENS ** 0.5), 14.0, ((0, 2),), jnp.float32)
    up_moment = scatter_about(splits[13], (D, FF), (0.03 * TOKENS ** 0.5), 28.0, ((0, 2),), jnp.float32)
    down_moment = scatter_about(splits[14], (FF, D), (0.06 * TOKENS ** 0.5), 56.0, ((0, 2),), jnp.float32)
    norm_moment = scatter_about(splits[15], (D, 4), (0.1 * TOKENS ** 0.5), 96.0, ((0, 2),), jnp.float32)
    qkv_average = scatter_about(splits[16], (D, 3 * D), D ** -0.5, 0.25, ((0, 2),), jnp.float32)
    out_average = scatter_about(splits[17], (D, D), (max(D // 64, 1)) ** -0.5, 2.0, ((0, 2),), jnp.float32)
    up_average = scatter_about(splits[18], (D, FF), D ** -0.5, 0.25, ((0, 2),), jnp.float32)
    down_average = scatter_about(splits[19], (FF, D), FF ** -0.5, 0.125, ((0, 2),), jnp.float32)
    norm_average = draw_norm_average(jax.random.fold_in(splits[21], 71), 0)
    return {"tokens": tokens, "memory": memory, "cmemory": cmemory, "doc_ids": doc_ids, "cotangent": cotangent, "qkv_weight": qkv_weight, "out_weight": out_weight, "up_weight": up_weight, "down_weight": down_weight, "conv_weight": conv_weight, "norm_params": norm_params, "qkv_moment": qkv_moment, "out_moment": out_moment, "up_moment": up_moment, "down_moment": down_moment, "norm_moment": norm_moment, "qkv_average": qkv_average, "out_average": out_average, "up_average": up_average, "down_average": down_average, "norm_average": norm_average}


MOMENTUM = 0.9
RATE = 0.0025
SMOOTH = 0.8
NEGATIVE = -1e+30

@jax.custom_vjp
def low(v):
    return lax.optimization_barrier(v.astype(jnp.bfloat16)).astype(jnp.float32)

@jax.custom_vjp
def low_back(v):
    return v

def low_keep(v):
    return (low(v), None)

def low_pass(kept, grad):
    return (grad,)

def back_keep(v):
    return (v, None)

def back_low(kept, grad):
    return (low(grad),)
low.defvjp(low_keep, low_pass)
low_back.defvjp(back_keep, back_low)

def matmul(left, right):
    return jnp.dot(left, right, precision=lax.Precision.HIGHEST)

def norm_rows(values, gain, shift):
    center = values - lax.optimization_barrier(jnp.mean(values, axis=-1, keepdims=True))
    spread = lax.optimization_barrier(jnp.mean(center * center, axis=-1, keepdims=True))
    return center * lax.rsqrt(spread + 1e-05) * gain + shift

def forward(weights, segment, recent, older, documents):
    qkv_full, out_full, up_full, down_full, norm_full = weights
    model_width = segment.shape[1]
    history = recent.shape[0] + older.shape[0]
    head_count = HEADS
    head_size = model_width // head_count
    stacked = jnp.concatenate([older, recent, segment], axis=0)
    length = stacked.shape[0]
    normed = low(norm_rows(stacked, norm_full[:, 0], norm_full[:, 1]))
    queries = low(low_back(matmul(normed[history:], qkv_full[:, :model_width])))
    keyvals = low(low_back(matmul(normed, qkv_full[:, model_width:])))
    head_queries = queries.reshape(-1, head_count, head_size)
    head_keys = keyvals[:, :model_width].reshape(length, head_count, head_size)
    head_values = keyvals[:, model_width:].reshape(length, head_count, head_size)
    scores = jnp.einsum('qhd,khd->hqk', head_queries, head_keys, precision=lax.Precision.HIGHEST) * head_size ** (-0.5)
    scores = low_back(scores)
    places = jnp.arange(length)
    allowed = (documents[history:, None] == documents[None, :]) & (places[None, :] <= places[history:, None])
    scores = jnp.where(allowed[None], scores, NEGATIVE)
    maximum = lax.optimization_barrier(jnp.max(scores, axis=2, keepdims=True))
    exponent = jnp.exp(scores - maximum)
    probability = exponent / lax.optimization_barrier(jnp.sum(exponent, axis=2, keepdims=True))
    attended = jnp.einsum('hqk,khd->qhd', low(probability), head_values, precision=lax.Precision.HIGHEST)
    attended = low(low_back(attended)).reshape(-1, model_width)
    branch = low_back(matmul(attended, out_full))
    residual = segment + branch
    lifted = low(norm_rows(residual, norm_full[:, 2], norm_full[:, 3]))
    hidden = low_back(matmul(lifted, up_full))
    active = low(jax.nn.gelu(hidden, approximate=True))
    return residual + matmul(active, down_full)

def renew(grad_total, moment, average, master):
    momentum = MOMENTUM * moment + (1.0 - MOMENTUM) * grad_total
    updated = master - RATE * ((1.0 - MOMENTUM) * grad_total + MOMENTUM * momentum)
    smooth = SMOOTH * average + (1.0 - SMOOTH) * updated
    return (momentum, smooth, updated)

def reference(tokens, memory, cmemory, doc_ids, cotangent, qkv_weight, out_weight, up_weight, down_weight, conv_weight, norm_params, qkv_moment, out_moment, up_moment, down_moment, norm_moment, qkv_average, out_average, up_average, down_average, norm_average):
    masters = (qkv_weight, out_weight, up_weight, down_weight, norm_params)
    copies = tuple((master.astype(jnp.bfloat16).astype(jnp.float32) for master in masters))
    conv_copy = conv_weight.astype(jnp.bfloat16).astype(jnp.float32)

    def one_stream(summed, stream):
        segment, recent, older, documents, incoming = stream

        def run(weights, seg_in):
            return forward(weights, seg_in, recent.astype(jnp.float32), older.astype(jnp.float32), documents)
        result, pullback = jax.vjp(run, copies, segment.astype(jnp.float32))
        weight_grads, segment_grad = pullback(incoming.astype(jnp.float32))
        summed = jax.tree.map(jnp.add, summed, weight_grads)
        evicted = jnp.concatenate([recent, segment], axis=0)[:S].astype(jnp.float32).reshape(S // 3, 3 * D)
        squeezed = matmul(evicted, conv_copy).astype(jnp.bfloat16)
        new_older = jnp.concatenate([older[S // 3:], squeezed], axis=0)
        return (summed, (result.astype(jnp.bfloat16), segment[S - M:], new_older, segment_grad.astype(jnp.bfloat16)))
    zeros_init = tuple((jnp.zeros_like(master) for master in masters))
    grads, (output, new_memory, new_cmemory, token_grad) = lax.scan(one_stream, zeros_init, (tokens, memory, cmemory, doc_ids, cotangent))
    moments = (qkv_moment, out_moment, up_moment, down_moment, norm_moment)
    averages = (qkv_average, out_average, up_average, down_average, norm_average)
    renewed = [renew(grads[index], moments[index], averages[index], masters[index]) for index in range(5)]
    momenta = tuple((entry[0] for entry in renewed))
    smoothed = tuple((entry[1] for entry in renewed))
    updated = tuple((entry[2] for entry in renewed))
    lifted_grads = grads[4][:, 2:4]
    return (output, new_memory, new_cmemory, token_grad, grads[0], grads[1], grads[2], grads[3], grads[4], momenta[0], momenta[1], momenta[2], momenta[3], momenta[4], smoothed[0], smoothed[1], smoothed[2], smoothed[3], smoothed[4], updated[0], updated[1], updated[2], updated[3], updated[4], lifted_grads)
```

```python
import functools

import jax
import jax.numpy as jnp
from jax import lax
from jax.experimental import pallas as pl
from jax.experimental.pallas import tpu as pltpu
from jax.sharding import PartitionSpec as P

HEADS = 8
MOMENTUM = 0.9
RATE = 0.0025
SMOOTH = 0.8
REACH = 448
BF = jnp.bfloat16
F32 = jnp.float32
MESH = pl.DeviceIdType.MESH
GELU_C = 0.7978845608028654
GELU_A = 0.044715


def nn(a, b):
    return lax.dot_general(a, b, (((1,), (0,)), ((), ())), preferred_element_type=F32)


def nt(a, b):
    return lax.dot_general(a, b, (((1,), (1,)), ((), ())), preferred_element_type=F32)


def tn(a, b):
    return lax.dot_general(a, b, (((0,), (0,)), ((), ())), preferred_element_type=F32)


def normalised(x):
    center = x - jnp.mean(x, axis=-1, keepdims=True)
    scale = lax.rsqrt(jnp.mean(center * center, axis=-1, keepdims=True) + 1e-5)
    return center * scale, scale


def norm_back(grad, unit, scale, gain):
    inner = grad * gain
    first = jnp.mean(inner, axis=-1, keepdims=True)
    second = jnp.mean(inner * unit, axis=-1, keepdims=True)
    return (inner - first - unit * second) * scale


def two_heads(block):
    lane = lax.broadcasted_iota(jnp.int32, block.shape, 1)
    zero = jnp.zeros_like(block)
    low = lane < 64
    return jnp.concatenate([jnp.where(low, block, zero), jnp.where(low, zero, block)], axis=0)


def own_halves(block):
    return jnp.concatenate([block[0:64, 0:128], block[64:128, 128:256]], axis=0)


def rows_at(start, count, by=16):
    return pl.ds(pl.multiple_of(start, by), count)


class Sems:
    def __init__(self, ref, size):
        self.ref, self.size, self.used = ref, size, 0

    def take(self):
        self.used += 1
        assert self.used <= self.size
        return self.ref.at[self.used - 1]


class Place:
    def __init__(self, streams, shards):
        self.streams, self.shards = streams, shards
        self.s = lax.axis_index("stream")
        self.y = lax.axis_index("shard")
        self.bits = []
        bit = 1
        while bit < streams:
            self.bits.append(bit)
            bit *= 2

    def bit(self, bit):
        return (self.s // bit) % 2

    def across(self, bit):
        return (self.s + bit * (1 - 2 * self.bit(bit)), self.y)

    def shard_bit(self, bit):
        return (self.y // bit) % 2

    def shard_across(self, bit):
        return (self.s, self.y + bit * (1 - 2 * self.shard_bit(bit)))

    def ahead(self, j):
        return (self.s, (self.y + j) % self.shards)

    def behind(self, j):
        return (self.y + self.shards - j) % self.shards


def remote(src, dst, sems, who):
    copy = pltpu.make_async_remote_copy(
        src_ref=src, dst_ref=dst, send_sem=sems[0], recv_sem=sems[1], device_id=who, device_id_type=MESH
    )
    copy.start()
    return copy


class Gather:
    def __init__(self, place, buf, send, recv, split):
        self.p, self.buf, self.send, self.recv = place, buf, send, recv
        self.rows = buf.shape[0] // place.shards
        self.split = split
        self.count = self.rows // (4 if split else 2)
        core, near = place.bit(1), place.bit(2)
        self.core, self.near = core, near
        self.part = near * 2 + core if split else core
        self.first, self.second, self.third = [], [], []

    def view(self, owner, part):
        return self.buf.at[rows_at(owner * self.rows + part * self.count, self.count), :]

    def sems(self):
        return self.send.take(), self.recv.take()

    def start(self):
        for j in range(1, self.p.shards):
            v = self.view(self.p.y, self.part)
            self.first.append(remote(v, v, self.sems(), self.p.ahead(j)))

    def spread(self):
        for j in range(1, self.p.shards):
            self.first[j - 1].wait_recv()
            v = self.view(self.p.behind(j), self.part)
            if self.split:
                self.second.append(remote(v, v, self.sems(), self.p.across(2)))
            self.third.append(remote(v, v, self.sems(), self.p.across(1)))

    def pass_on(self):
        if self.split:
            for j in range(1, self.p.shards):
                self.second[j - 1].wait_recv()
                v = self.view(self.p.behind(j), (1 - self.near) * 2 + self.core)
                self.third.append(remote(v, v, self.sems(), self.p.across(1)))

    def finish(self):
        for copy in self.third:
            copy.wait_recv()

    def sent(self):
        for copy in self.first + self.second + self.third:
            copy.wait_send()


class Total:
    def __init__(self, place, grad, total, slots, send, recv, order):
        self.p, self.grad, self.total = place, grad, total
        self.send, self.recv = send, recv
        self.slots = list(slots)
        self.order = [("stream", 1)] + list(order)
        rows = grad.shape[0] // place.shards
        self.rows = rows
        self.blocks = [(j * rows, j) for j in range(place.shards)]
        self.count = rows
        self.back = []
        self.live = []
        self.done = []
        self.stage = -1
        self.held = []

    def sems(self):
        return self.send.take(), self.recv.take()

    def n_steps(self):
        return 0

    def begin(self):
        axis, bit = self.order[self.stage]
        slot = self.slots.pop(0)
        self.live, self.held = [], []
        if axis == "stream":
            mine = self.p.bit(bit)
            halve = self.count % 32 == 0
            keep = self.count // 2 if halve else self.count
            for n, start in enumerate(self.starts):
                gone = start + (1 - mine) * keep if halve else start
                kept = start + mine * keep if halve else start
                src = self.grad.at[rows_at(gone, keep), :]
                dst = slot.at[pl.ds(n * keep, keep), :]
                self.live.append(remote(src, dst, self.sems(), self.p.across(bit)))
                self.held.append(kept)
            if halve:
                self.back.append(bit)
            self.count = keep
        else:
            mine = self.p.shard_bit(bit)
            half = len(self.starts) // 2
            low, high = self.starts[:half], self.starts[half:]
            for n in range(half):
                gone = jnp.where(mine == 0, high[n], low[n])
                kept = jnp.where(mine == 0, low[n], high[n])
                src = self.grad.at[rows_at(gone, self.count), :]
                dst = slot.at[pl.ds(n * self.count, self.count), :]
                self.live.append(remote(src, dst, self.sems(), self.p.shard_across(bit)))
                self.held.append(kept)
        self.slot = slot

    def add(self, last):
        for n, copy in enumerate(self.live):
            copy.wait_recv()
            here = rows_at(self.held[n], self.count)
            value = self.grad[here, :].astype(F32) + self.slot[pl.ds(n * self.count, self.count), :].astype(F32)
            if last:
                self.total[rows_at(self.held[n] - self.p.y * self.rows, self.count), :] = value.astype(BF)
            else:
                self.grad[here, :] = value.astype(BF)
        self.done += self.live
        self.starts = self.held

    def share(self):
        bit = self.back.pop()
        v = self.total.at[rows_at(self.own, self.count), :]
        copy = remote(v, v, self.sems(), self.p.across(bit))
        self.own = self.own - self.p.bit(bit) * self.count
        self.count *= 2
        self.live = [copy]

    def steps(self):
        def first():
            self.starts = [b[0] for b in self.blocks]
            self.stage = 0
            self.begin()

        def middle():
            self.add(False)
            self.stage += 1
            self.begin()

        def turn():
            self.add(True)
            self.own = self.held[0] - self.p.y * self.rows
            self.share()

        def later():
            self.live[0].wait_recv()
            self.done += self.live
            self.share()

        def end():
            self.live[0].wait_recv()
            self.done += self.live

        halvings = len(self.order)
        out = [first] + [middle] * (halvings - 1) + [turn]
        count, shares = self.rows, 0
        for axis, bit in self.order:
            if axis == "stream" and count % 32 == 0:
                count //= 2
                shares += 1
        return out + [later] * (shares - 1) + [end]

    def sent(self):
        for copy in self.done:
            copy.wait_send()


def slot_shapes(place_sizes, rows, columns, order):
    streams, shards = place_sizes
    blocks, count, shapes = shards, rows // shards, []
    for axis, bit in [("stream", 1)] + list(order):
        if axis == "stream":
            if count % 32 == 0:
                count //= 2
        else:
            blocks //= 2
        shapes.append((blocks * count, columns))
    return shapes


def orders(streams, shards):
    upper, lower = [], []
    bit = 2
    while bit < streams:
        upper.append(("stream", bit))
        bit *= 2
    bit = shards // 2
    while bit >= 1:
        lower.append(("shard", bit))
        bit //= 2
    return lower + upper, upper[:1] + lower + upper[1:]


GRADS = ("d0", "d1", "u0", "u1", "o", "qa", "qb")
FFN = ("d0", "u0", "d1", "u1")
LATE = ("qb", "qa", "o") + FFN


def layer_kernel(
    sizes, plan, tok, mem, old, docs, cot, wqkv, wo, wu, wd, wc, norms, out, tgrad, newold, norm_total, *rest
):
    totals = rest[:7]
    (
        xs, N, Q, K, V, PT, OT, bias, res, gres, lifted, act, gh, gl, gr, dO, Dv, dK, dV, ct,
        Wq, Wk, Wv, Wo, Wu, Wd, Wc, nblocks, ngrad, nslots, ev,
    ) = rest[7:38]
    rest = rest[38:]
    gbuf, tbuf = rest[:7], rest[7:14]
    rest = rest[14:]
    slots = []
    for n in plan["slot_counts"]:
        slots.append(rest[:n])
        rest = rest[n:]
    send_ref, recv_ref, local_ref = rest
    place = Place(*sizes)
    send, recv, local = Sems(send_ref, plan["sems"]), Sems(recv_ref, plan["sems"]), Sems(local_ref, plan["local"])
    shards = place.shards
    S, D = tok.shape
    M = mem.shape[0]
    H0 = M - REACH
    L = REACH + S
    T0 = REACH
    W = REACH + 128
    FF = Wu.shape[1]
    n_q = S // 128

    barrier = pltpu.get_barrier_semaphore()
    partners = [place.across(bit) for bit in place.bits] + [place.ahead(j) for j in range(1, shards)]
    for who in partners:
        pl.semaphore_signal(barrier, inc=1, device_id=who, device_id_type=MESH)

    def fetch(src, dst):
        copy = pltpu.make_async_copy(src, dst, local.take())
        copy.start()
        return copy

    pools = [dK, dV, gl, gres, res]
    free = [[ref, 0] for ref in pools]

    def room(rows):
        for entry in free:
            if entry[1] + rows <= entry[0].shape[0]:
                entry[1] += rows
                return entry[0].at[pl.ds(entry[1] - rows, rows), :]
        raise ValueError("no room")

    r1 = wqkv.shape[0]
    jobs = {}

    def bring(name, src, target, col):
        piece = min(src.shape[0], 256)
        for n in range(0, src.shape[0], piece):
            stage = room(piece)
            copy = fetch(src.at[pl.ds(n, piece), :], stage)
            jobs.setdefault(name, []).append((copy, stage, target, col, place.y * src.shape[0] + n, piece))

    c512 = pl.ds(0, 512)
    bring("k", wqkv.at[:, pl.ds(512, 512)], Wk, 0)
    bring("v", wqkv.at[:, pl.ds(1024, 512)], Wv, 0)
    bring("q", wqkv.at[:, pl.ds(0, 512)], Wq, 0)
    tok_in = fetch(tok, xs.at[pl.ds(M, S), :])
    mem_in = fetch(mem, xs.at[pl.ds(0, M), :])
    bring("o", wo, Wo, 0)
    for c in range(FF // 512):
        bring("u", wu.at[:, pl.ds(c * 512, 512)], Wu, c * 512)
    bring("d", wd, Wd, 0)
    cot_in = fetch(cot, ct)
    bring("c", wc, Wc, 0)
    old_in = fetch(old.at[pl.ds(S // 3, old.shape[0] - S // 3), :], newold.at[pl.ds(0, old.shape[0] - S // 3), :])

    nblocks[pl.ds(place.y, 1)] = jnp.concatenate(
        [norms[...].astype(BF).astype(F32), jnp.zeros((4, norms.shape[1]), F32)], axis=0
    )[None]

    def cast(name):
        for copy, stage, target, col, start, rows in jobs[name]:
            copy.wait()
            target[rows_at(start, rows), pl.ds(col, 512)] = stage[...].astype(BF)

    cast("k")
    pl.semaphore_wait(barrier, len(partners))
    norm_sent = []
    for j in range(1, shards):
        v = nblocks.at[place.y]
        norm_sent.append(remote(v, v, (send.take(), recv.take()), place.ahead(j)))
    gathers = {}

    def launch(name, buf, split):
        gathers[name] = Gather(place, buf, send, recv, split)
        gathers[name].start()

    split = plan["split"]
    launch("k", Wk, split["k"])
    cast("v")
    launch("v", Wv, split["v"])
    cast("q")
    launch("q", Wq, split["q"])
    cast("o")
    launch("o", Wo, split["o"])
    cast("u")
    launch("u", Wu, split["u"])
    cast("d")
    launch("d", Wd, split["d"])
    cast("c")
    launch("c", Wc, split["c"])

    ids = docs[...].astype(F32)
    column = jnp.transpose(jnp.broadcast_to(ids, (8, ids.shape[1])))
    base = ids.shape[1] - L

    def see(b):
        key = column[base + 128 * b : base + 128 * b + W, 0:1]
        query = ids[:, base + T0 + 128 * b : base + T0 + 128 * b + 128]
        k = lax.broadcasted_iota(jnp.int32, (W, 128), 0)
        q = lax.broadcasted_iota(jnp.int32, (W, 128), 1) + T0
        bias[b] = jnp.where((key == query) & (k <= q), 0.0, -1e30)

    for b in range(n_q):
        see(b)
    gathers["k"].spread()
    for copy in norm_sent:
        copy.wait_recv()
    table = jnp.concatenate([nblocks[j] for j in range(shards)], axis=1)
    g1, b1, g2, b2 = table[0:1], table[1:2], table[2:3], table[3:4]

    tok_in.wait()
    mem_in.wait()

    def ln1(i, _):
        unit, _s = normalised(xs[rows_at(H0 + i * 64, 64), :].astype(F32))
        N[rows_at(i * 64, 64), :] = (unit * g1 + b1).astype(BF)
        return 0

    lax.fori_loop(0, 10, ln1, 0)
    gathers["v"].spread()
    gathers["k"].pass_on()
    lax.fori_loop(10, L // 64, ln1, 0)
    gathers["q"].spread()
    gathers["v"].pass_on()
    gathers["o"].spread()
    gathers["k"].finish()
    for c in range(2):
        cs = slice(c * 256, c * 256 + 256)
        K[:, cs] = nn(N[...], Wk[:, cs]).astype(BF)
    gathers["q"].pass_on()
    gathers["v"].finish()
    for c in range(2):
        cs = slice(c * 256, c * 256 + 256)
        V[:, cs] = nn(N[...], Wv[:, cs]).astype(BF)
    gathers["o"].pass_on()
    gathers["q"].finish()
    for c in range(2):
        cs = slice(c * 256, c * 256 + 256)
        Q[:, cs] = (nn(N[T0:, :], Wq[:, cs]).astype(BF).astype(F32) * 0.125).astype(BF)

    def attend(qb, p):
        q0, l0 = pl.multiple_of(qb * 128, 128), pl.multiple_of(p * 128, 128)
        q2 = two_heads(Q[pl.ds(q0, 128), pl.ds(l0, 128)])
        s = nt(K[pl.ds(q0, W), pl.ds(l0, 128)], q2)
        seen = bias[qb]
        s = s + jnp.concatenate([seen, seen], axis=1)
        e = jnp.exp(s - jnp.max(s, axis=0, keepdims=True))
        probs = (e * (1.0 / jnp.sum(e, axis=0, keepdims=True))).astype(BF)
        PT[p * n_q + qb] = probs
        o = tn(V[pl.ds(q0, W), pl.ds(l0, 128)], probs)
        OT[pl.ds(l0, 128), pl.ds(q0, 128)] = own_halves(o).astype(BF)

    def attend_row(i, _):
        for u in range(2):
            attend(i // 2, (i % 2) * 2 + u)
        return 0

    half = n_q
    lax.fori_loop(0, half, attend_row, 0)
    gathers["u"].spread()
    lax.fori_loop(half, 2 * n_q, attend_row, 0)
    gathers["u"].pass_on()
    gathers["o"].finish()

    for c in range(2):
        cs = slice(c * 256, c * 256 + 256)
        res[:, cs] = xs[M:, cs].astype(F32) + tn(OT[...], Wo[:, cs])

    def ln2(i, _):
        r = rows_at(i * 64, 64)
        unit, _s = normalised(res[r, :])
        lifted[r, :] = (unit * g2 + b2).astype(BF)
        return 0

    lax.fori_loop(0, S // 64, ln2, 0)
    gathers["d"].spread()
    gathers["u"].finish()
    gathers["d"].pass_on()
    gathers["d"].finish()
    cot_in.wait()

    def ffn(i, _):
        cs = rows_at(i * 256, 256, 256)
        h = nn(lifted[...], Wu[:, cs])
        ga = nt(ct[...], Wd[cs, :])
        h2 = h * h
        t = jnp.tanh(GELU_C * h * (1.0 + GELU_A * h2))
        hp = 0.5 + 0.5 * t
        act[:, cs] = (h * hp).astype(BF)
        slope = hp + (0.5 * GELU_C) * h * (1.0 - t * t) * (1.0 + (3 * GELU_A) * h2)
        gh[:, cs] = (ga * slope).astype(BF)
        return 0

    lax.fori_loop(0, FF // 256, ffn, 0)

    sums = {
        name: Total(place, gbuf[i], tbuf[i], slots[i], send, recv, plan["orders"][i]) for i, name in enumerate(GRADS)
    }
    waiting = {name: list(sums[name].steps()) for name in GRADS}
    ends = []

    def go(*names):
        for name in names:
            if waiting[name]:
                waiting[name].pop(0)()
                if not waiting[name]:
                    i = GRADS.index(name)
                    copy = pltpu.make_async_copy(tbuf[i], totals[i], local.take())
                    copy.start()
                    ends.append(copy)

    def grad_down(ref, col):
        def body(i, _):
            r = rows_at(i * 512, 512, 512)
            ref[r, :] = tn(act[:, r], ct[:, col : col + 256]).astype(BF)
            return 0

        lax.fori_loop(0, FF // 512, body, 0)

    grad_down(gbuf[0], 0)
    go("d0")
    grad_down(gbuf[1], 256)
    go("d1")
    for n in range(2):
        for c in range(2):
            gbuf[2 + n][:, c * 512 : c * 512 + 512] = tn(
                lifted[...], gh[:, n * 1024 + c * 512 : n * 1024 + c * 512 + 512]
            ).astype(BF)
        go(*(("u0", "d0") if n == 0 else ("u1", "d1")))
    for c in range(2):
        cs = slice(c * 256, c * 256 + 256)
        gl[:, cs] = nt(gh[...], Wu[cs, :])
    go("u0", "u1")

    zero = jnp.zeros((1, D), F32)

    def ln2_back(i, sums_in):
        r = rows_at(i * 64, 64)
        unit, scale = normalised(res[r, :])
        gy = gl[r, :]
        x = ct[r, :].astype(F32) + norm_back(gy, unit, scale, g2)
        gres[r, :] = x
        gr[r, :] = x.astype(BF)
        return (
            sums_in[0] + jnp.sum(gy * unit, axis=0, keepdims=True),
            sums_in[1] + jnp.sum(gy, axis=0, keepdims=True),
        )

    gain2, shift2 = lax.fori_loop(0, S // 64, ln2_back, (zero, zero))
    gbuf[4][...] = nn(OT[...], gr[...]).astype(BF)
    go("o", "d0")
    for c in range(2):
        cs = slice(c * 256, c * 256 + 256)
        dO[:, cs] = nt(gr[...], Wo[cs, :]).astype(BF)
    for c in range(2):
        cs = slice(c * 256, c * 256 + 256)
        dt = nt(Wo[cs, :], gr[...]).astype(BF).astype(F32) * OT[cs, :].astype(F32)
        for h in range(4):
            Dv[c * 4 + h : c * 4 + h + 1, :] = jnp.sum(dt[h * 64 : h * 64 + 64], axis=0, keepdims=True)
    go("o", "d0", "d1")

    def attend_back(qb, p):
        q0, l0 = pl.multiple_of(qb * 128, 128), pl.multiple_of(p * 128, 128)
        q2 = two_heads(Q[pl.ds(q0, 128), pl.ds(l0, 128)])
        do2 = two_heads(dO[pl.ds(q0, 128), pl.ds(l0, 128)])
        probs = PT[p * n_q + qb]
        dp = nt(V[pl.ds(q0, W), pl.ds(l0, 128)], do2)
        mean = jnp.concatenate([Dv[pl.ds(2 * p, 1), pl.ds(q0, 128)], Dv[pl.ds(2 * p + 1, 1), pl.ds(q0, 128)]], axis=1)
        ds = (probs.astype(F32) * (dp - mean)).astype(BF)
        dV[pl.ds(q0, W), pl.ds(l0, 128)] += nn(probs, do2)
        dK[pl.ds(q0, W), pl.ds(l0, 128)] += nn(ds, q2)
        dq = own_halves(tn(K[pl.ds(q0, W), pl.ds(l0, 128)], ds)) * 0.125
        Q[pl.ds(q0, 128), pl.ds(l0, 128)] = jnp.transpose(dq).astype(BF)

    dK[...] = jnp.zeros_like(dK)
    dV[...] = jnp.zeros_like(dV)
    for quad in range(2):
        ticks = [("d0", "d1", "u0"), ("d0", "d1", "u0"), ("d1", "u0", "u1")] if quad == 0 else [FFN + ("o",)] * 3
        for part in range(3):

            def body(qb, _):
                for u in range(2):
                    attend_back(qb, quad * 2 + u)
                return 0

            lax.fori_loop(part * n_q // 3, (part + 1) * n_q // 3, body, 0)
            go(*ticks[part])
        cs = slice(quad * 256, quad * 256 + 256)
        K[:, cs] = dK[:, cs].astype(BF)
        V[:, cs] = dV[:, cs].astype(BF)
        g = gbuf[5 + quad]
        g[:, 0:256] = tn(N[T0:, :], Q[:, cs]).astype(BF)
        g[:, 256:512] = tn(N[...], K[:, cs]).astype(BF)
        g[:, 512:768] = tn(N[...], V[:, cs]).astype(BF)
        go(*(("qa", "o") + FFN if quad == 0 else ("qb", "qa")))

    for c in range(2):
        cs = slice(c * 256, c * 256 + 256)
        dK[:, cs] = nt(K[...], Wk[cs, :]) + nt(V[...], Wv[cs, :])
        dK[T0:, cs] += nt(Q[...], Wq[cs, :])
    go(*LATE)

    def ln1_back(i, sums_in, tokens):
        unit, scale = normalised(xs[rows_at(H0 + i * 64, 64), :].astype(F32))
        gy = dK[rows_at(i * 64, 64), :]
        if tokens:
            r = rows_at(i * 64 - T0, 64)
            lifted[r, :] = (gres[r, :] + norm_back(gy, unit, scale, g1)).astype(BF)
        return (
            sums_in[0] + jnp.sum(gy * unit, axis=0, keepdims=True),
            sums_in[1] + jnp.sum(gy, axis=0, keepdims=True),
        )

    acc = lax.fori_loop(0, T0 // 64, functools.partial(ln1_back, tokens=False), (zero, zero))
    gain1, shift1 = lax.fori_loop(T0 // 64, L // 64, functools.partial(ln1_back, tokens=True), acc)
    tgrad_out = pltpu.make_async_copy(lifted, tgrad, local.take())
    tgrad_out.start()

    ngrad[0] = jnp.concatenate([gain1, shift1, gain2, shift2, jnp.zeros((4, D), F32)], axis=0)
    hops = [(place.across(bit)) for bit in place.bits]
    bit = 1
    while bit < shards:
        hops.append(place.shard_across(bit))
        bit *= 2
    norm_copies = []

    def norm_send(n):
        norm_copies.append(remote(ngrad.at[n], nslots.at[n], (send.take(), recv.take()), hops[n]))

    def norm_next(n):
        norm_copies[n].wait_recv()
        ngrad[n + 1] = ngrad[n] + nslots[n]
        if n + 1 < len(hops):
            norm_send(n + 1)

    norm_send(0)
    go(*LATE)

    for c in range(2):
        cs = slice(c * 256, c * 256 + 256)
        gr[:, cs] = (res[:, cs] + nn(act[...], Wd[:, cs])).astype(BF)
        norm_next(c)
        go(*LATE)
    out_copy = pltpu.make_async_copy(gr, out, local.take())
    out_copy.start()
    gathers["c"].spread()
    gathers["c"].pass_on()
    for n in range(D // 128):
        ev[n] = xs[pl.ds(0, S), n * 128 : n * 128 + 128].astype(F32)
    squeezed = None
    gathers["c"].finish()
    for t in range(3):
        every = [ev[n, pl.ds(t, S // 3, stride=3), :] for n in range(D // 128)]
        part = jnp.concatenate(every, axis=1).astype(BF)
        term = nn(part, Wc[t * D : (t + 1) * D, :])
        squeezed = term if squeezed is None else squeezed + term
        go(*LATE)
    dO[0 : S // 3, :] = squeezed.astype(BF)
    squeeze_copy = pltpu.make_async_copy(
        dO.at[pl.ds(0, S // 3), :], newold.at[pl.ds(old.shape[0] - S // 3, S // 3), :], local.take()
    )
    squeeze_copy.start()
    for n in range(2, len(hops)):
        norm_next(n)
        go(*LATE)
    for _ in range(20):
        go("d0", "u0", "d1", "u1", "o", "qa", "qb")
    final = ngrad[len(hops)]
    width = norms.shape[1]
    mine = final[:, 0:width]
    for j in range(1, shards):
        mine = jnp.where(place.y == j, final[:, j * width : (j + 1) * width], mine)
    norm_total[...] = mine

    for copy in ends + [tgrad_out, out_copy, squeeze_copy, old_in]:
        copy.wait()
    for name in gathers:
        gathers[name].sent()
    for name in GRADS:
        sums[name].sent()
    for copy in norm_sent + norm_copies:
        copy.wait_send()


def run_layer(sizes, tokens, memory, cmemory, docs, cotangent, wqkv, wo, wu, wd, wc, norms):
    streams, shards = sizes
    S, D = tokens.shape
    M = memory.shape[0]
    L = REACH + S
    W = REACH + 128
    FF = wu.shape[1]
    n_q = S // 128
    main, other = orders(streams, shards)
    shapes = [(FF, D // 2)] * 2 + [(D, FF // 2)] * 2 + [(D, D)] + [(D, 3 * D // 2)] * 2
    plan_orders = [main, main, main, main, main, main, main]
    slot_lists = [slot_shapes(sizes, *shapes[i], plan_orders[i]) for i in range(7)]
    hops = len(orders(streams, shards)[0]) + 1
    sems = 7 * (shards - 1) * 4 + 7 * (2 * shards + 2 * hops) + hops + shards
    plan = {
        "orders": plan_orders,
        "slot_counts": [len(s) for s in slot_lists],
        "sems": sems,
        "local": 32,
        "split": {"k": True, "v": True, "q": True, "o": True, "u": True, "d": True, "c": True},
    }
    f32, bf = (lambda *s: pltpu.VMEM(s, F32)), (lambda *s: pltpu.VMEM(s, BF))
    scratch = [
        bf(M + S, D), bf(L, D), bf(S, D), bf(L, D), bf(L, D), bf((HEADS // 2) * n_q, W, 256), bf(D, S),
        f32(n_q, W, 128), f32(S, D), f32(S, D), bf(S, D), bf(S, FF), bf(S, FF), f32(S, D), bf(S, D), bf(S, D),
        f32(HEADS, S), f32(L, D), f32(L, D), bf(S, D),
        bf(D, D), bf(D, D), bf(D, D), bf(D, D), bf(D, FF), bf(FF, D), bf(3 * D, D),
        f32(shards, 8, norms.shape[1]), f32(hops + 1, 8, D), f32(hops, 8, D), f32(D // 128, S, 128),
    ]
    scratch += [bf(*s) for s in shapes]
    scratch += [bf(s[0] // shards, s[1]) for s in shapes]
    for s in slot_lists:
        scratch += [bf(*x) for x in s]
    scratch += [pltpu.SemaphoreType.DMA((sems,)), pltpu.SemaphoreType.DMA((sems,)), pltpu.SemaphoreType.DMA((32,))]
    anywhere = pl.BlockSpec(memory_space=pl.ANY)
    vmem = pl.BlockSpec(memory_space=pltpu.VMEM)
    out_shape = [
        jax.ShapeDtypeStruct((S, D), BF),
        jax.ShapeDtypeStruct((S, D), BF),
        jax.ShapeDtypeStruct(cmemory.shape, BF),
        jax.ShapeDtypeStruct((8, norms.shape[1]), F32),
    ] + [jax.ShapeDtypeStruct((s[0] // shards, s[1]), BF) for s in shapes]
    return pl.pallas_call(
        functools.partial(layer_kernel, sizes, plan),
        out_shape=out_shape,
        in_specs=[anywhere] * 3 + [vmem] + [anywhere] * 6 + [vmem],
        out_specs=[anywhere] * 3 + [vmem] + [anywhere] * 7,
        scratch_shapes=scratch,
        compiler_params=pltpu.CompilerParams(
            collective_id=0, has_side_effects=True, vmem_limit_bytes=64 * 1024 * 1024
        ),
        name="layer",
    )(tokens, memory, cmemory, docs, cotangent, wqkv, wo, wu, wd, wc, norms)


def renew(grad, moment, average, master):
    momentum = MOMENTUM * moment + (1.0 - MOMENTUM) * grad
    updated = master - RATE * ((1.0 - MOMENTUM) * grad + MOMENTUM * momentum)
    smooth = SMOOTH * average + (1.0 - SMOOTH) * updated
    return momentum, smooth, updated


def update_kernel(steps, *refs):
    totals, masters, moments, averages = refs[0:7], refs[7:11], refs[11:15], refs[15:19]
    norm_grad, norm_old = refs[19], refs[20:23]
    passed = refs[23:27]
    grads, momenta, smooths, updates = refs[27:31], refs[31:35], refs[35:39], refs[39:43]
    norm_out = refs[43:47]
    lifted_out = refs[47]
    kept = refs[48:52]
    sems = refs[52]
    step = pl.program_id(0)
    rows = kept[1].shape[0]
    skip = passed[3].shape[0] - rows
    sources = [passed[0], passed[1], passed[2], passed[3].at[pl.ds(skip, rows), :]]
    targets = [kept[0], kept[2], kept[3], kept[1]]
    copies = [pltpu.make_async_copy(a, b, sems.at[i]) for i, (a, b) in enumerate(zip(sources, targets))]

    @pl.when(step == 0)
    def _():
        for copy in copies:
            copy.start()
        g = norm_grad[0:4, :]
        norm_out[0][...] = g
        lifted_out[...] = g[2:4]
        for ref, value in zip(norm_out[1:], renew(g, norm_old[1][...], norm_old[2][...], norm_old[0][...])):
            ref[...] = value

    d0, d1, u0, u1, o, qa, qb = [t[...].astype(F32) for t in totals]
    pieces = []
    for c in range(0, qa.shape[1], 256):
        pieces += [qa[:, c : c + 256], qb[:, c : c + 256]]
    whole = (
        jnp.concatenate(pieces, axis=1),
        o,
        jnp.concatenate([u0, u1], axis=1),
        jnp.concatenate([d0, d1], axis=1),
    )
    for i in range(4):
        grads[i][...] = whole[i]
        new = renew(whole[i], moments[i][...], averages[i][...], masters[i][...])
        momenta[i][...], smooths[i][...], updates[i][...] = new

    @pl.when(step == steps - 1)
    def _():
        for copy in copies:
            copy.wait()


def run_update(totals, masters, moments, averages, norm_grad, norm_old, output, tgrad, newold, tokens, mem_rows):
    steps = 8
    while masters[1].shape[0] % (steps * 16):
        steps //= 2

    def block(x):
        return pl.BlockSpec((x.shape[0] // steps, x.shape[1]), lambda i: (i, 0))

    def fixed(x):
        return pl.BlockSpec(x.shape, lambda i: (0, 0))

    anywhere = pl.BlockSpec(memory_space=pl.ANY)
    same = [jax.ShapeDtypeStruct(m.shape, F32) for m in masters]
    small = jax.ShapeDtypeStruct(norm_old[0].shape, F32)
    lifted = jax.ShapeDtypeStruct((2, small.shape[1]), F32)
    keep = [
        jax.ShapeDtypeStruct(output.shape, BF),
        jax.ShapeDtypeStruct((mem_rows, tokens.shape[1]), BF),
        jax.ShapeDtypeStruct(tgrad.shape, BF),
        jax.ShapeDtypeStruct(newold.shape, BF),
    ]
    passed = (output, tgrad, newold, tokens)
    return pl.pallas_call(
        functools.partial(update_kernel, steps),
        grid=(steps,),
        out_shape=same * 4 + [small] * 4 + [lifted] + keep,
        in_specs=[block(t) for t in totals]
        + [block(m) for m in masters] * 3
        + [fixed(norm_grad)]
        + [fixed(small)] * 3
        + [anywhere] * 4,
        out_specs=[block(m) for m in masters] * 4 + [fixed(small)] * 4 + [fixed(lifted)] + [anywhere] * 4,
        scratch_shapes=[pltpu.SemaphoreType.DMA((4,))],
        compiler_params=pltpu.CompilerParams(vmem_limit_bytes=48 * 1024 * 1024),
        name="update",
    )(*totals, *masters, *moments, *averages, norm_grad, *norm_old, *passed)


def on_device(
    sizes, tokens, memory, cmemory, doc_ids, cotangent,
    qkv_weight, out_weight, up_weight, down_weight, conv_weight, norm_params,
    qkv_moment, out_moment, up_moment, down_moment, norm_moment,
    qkv_average, out_average, up_average, down_average, norm_average,
):
    results = run_layer(
        sizes, tokens[0], memory[0], cmemory[0], doc_ids, cotangent[0],
        qkv_weight, out_weight, up_weight, down_weight, conv_weight, norm_params.T,
    )
    output, tgrad, newold, norm_grad = results[:4]
    new = run_update(
        results[4:],
        (qkv_weight, out_weight, up_weight, down_weight),
        (qkv_moment, out_moment, up_moment, down_moment),
        (qkv_average, out_average, up_average, down_average),
        norm_grad,
        (norm_params.T, norm_moment.T, norm_average.T),
        output, tgrad, newold, tokens[0], memory.shape[1],
    )
    grads, momenta, smooths, updates = new[0:4], new[4:8], new[8:12], new[12:16]
    norms = [x.T for x in new[16:20]]
    lifted = new[20].T
    out, new_memory, token_grad, new_cmemory = new[21:25]
    return (
        out[None], new_memory[None], new_cmemory[None], token_grad[None],
        *grads, norms[0], *momenta, norms[1], *smooths, norms[2], *updates, norms[3], lifted,
    )


def solution(mesh):
    sizes = (mesh.shape["stream"], mesh.shape["shard"])
    both = ("stream", "shard")
    wide = P(both, None, None)
    rows = P("shard", None)
    return jax.shard_map(
        functools.partial(on_device, sizes),
        mesh=mesh,
        in_specs=(wide, wide, wide, P(both, None), wide) + (rows,) * 16,
        out_specs=(wide,) * 4 + (rows,) * 21,
        check_vma=False,
    )
```

```python
import functools

import jax
import jax.numpy as jnp
from jax import lax
from jax.experimental import pallas as pl
from jax.experimental.pallas import tpu as pltpu
from jax.sharding import PartitionSpec as P

HEADS = 8
MOMENTUM = 0.9
RATE = 0.0025
SMOOTH = 0.8
REACH = 448
BF = jnp.bfloat16
F32 = jnp.float32
MESH = pl.DeviceIdType.MESH
GELU_C = 0.7978845608028654
GELU_A = 0.044715


def nn(a, b):
    return lax.dot_general(a, b, (((1,), (0,)), ((), ())), preferred_element_type=F32)


def nt(a, b):
    return lax.dot_general(a, b, (((1,), (1,)), ((), ())), preferred_element_type=F32)


def tn(a, b):
    return lax.dot_general(a, b, (((0,), (0,)), ((), ())), preferred_element_type=F32)


def normalised(x):
    center = x - jnp.mean(x, axis=-1, keepdims=True)
    scale = lax.rsqrt(jnp.mean(center * center, axis=-1, keepdims=True) + 1e-5)
    return center * scale, scale


def norm_back(grad, unit, scale, gain):
    inner = grad * gain
    first = jnp.mean(inner, axis=-1, keepdims=True)
    second = jnp.mean(inner * unit, axis=-1, keepdims=True)
    return (inner - first - unit * second) * scale


def two_heads(block):
    lane = lax.broadcasted_iota(jnp.int32, block.shape, 1)
    zero = jnp.zeros_like(block)
    low = lane < 64
    return jnp.concatenate([jnp.where(low, block, zero), jnp.where(low, zero, block)], axis=0)


def own_halves(block):
    return jnp.concatenate([block[0:64, 0:128], block[64:128, 128:256]], axis=0)


def rows_at(start, count, by=16):
    return pl.ds(pl.multiple_of(start, by), count)


class Sems:
    def __init__(self, ref, size):
        self.ref, self.size, self.used = ref, size, 0

    def take(self):
        self.used += 1
        assert self.used <= self.size
        return self.ref.at[self.used - 1]


def subsets(bits):
    found = [()]
    for bit in bits:
        found += [f + (bit,) for f in found]
    return found[1:]


class Place:
    def __init__(self, streams, shards):
        self.streams, self.shards = streams, shards
        self.s = lax.axis_index("stream")
        self.y = lax.axis_index("shard")

    def value(self, axis, bit, flipped=False):
        v = ((self.s if axis == "stream" else self.y) // bit) % 2
        return 1 - v if flipped else v

    def flip(self, bits):
        s, y = self.s, self.y
        for axis, bit in bits:
            step = bit * (1 - 2 * self.value(axis, bit))
            if axis == "stream":
                s = s + step
            else:
                y = y + step
        return s, y

    def index(self, bits, flipped=()):
        total = 0
        for axis, bit in bits:
            total = total * 2 + self.value(axis, bit, (axis, bit) in flipped)
        return total


def remote(src, dst, sems, who):
    copy = pltpu.make_async_remote_copy(
        src_ref=src, dst_ref=dst, send_sem=sems[0], recv_sem=sems[1], device_id=who, device_id_type=MESH
    )
    copy.start()
    return copy


CORE, NEAR = ("stream", 1), ("stream", 2)


class Gather:
    def __init__(self, place, buf, take, split):
        self.p, self.buf, self.take = place, buf, take
        self.rows = buf.shape[0] // place.shards
        self.split = split
        self.parts = (NEAR, CORE) if split else (CORE,)
        self.count = self.rows // 2 ** len(self.parts)
        self.deltas = subsets(shard_bits(place.shards))
        self.part = place.index(self.parts)
        self.first, self.second, self.third = [], [], []

    def view(self, owner, part):
        return self.buf.at[rows_at(owner * self.rows + part * self.count, self.count), :]

    def start(self):
        for delta in self.deltas:
            v = self.view(self.p.y, self.part)
            self.first.append(remote(v, v, self.take(), self.p.flip(delta)))

    def spread(self):
        for n, delta in enumerate(self.deltas):
            self.first[n].wait_recv()
            v = self.view(self.p.flip(delta)[1], self.part)
            if self.split:
                self.second.append(remote(v, v, self.take(), self.p.flip((NEAR,))))
            self.third.append(remote(v, v, self.take(), self.p.flip((CORE,))))

    def pass_on(self):
        if self.split:
            for n, delta in enumerate(self.deltas):
                self.second[n].wait_recv()
                v = self.view(self.p.flip(delta)[1], self.p.index(self.parts, (NEAR,)))
                self.third.append(remote(v, v, self.take(), self.p.flip((CORE,))))

    def finish(self):
        for copy in self.third:
            copy.wait_recv()

    def sent(self):
        for copy in self.first + self.second + self.third:
            copy.wait_send()


def shard_bits(shards):
    bits, bit = [], shards // 2
    while bit >= 1:
        bits.append(("shard", bit))
        bit //= 2
    return tuple(bits)


def stream_bits(streams):
    bits, bit = [], 1
    while bit < streams:
        bits.append(("stream", bit))
        bit *= 2
    return tuple(bits)


def plan_total(sizes, rows, order):
    shards = sizes[1]
    count, full, stages, shares = rows // shards, True, [], []
    for group in order:
        across = tuple(b for b in group if b[0] == "shard")
        along = tuple(b for b in group if b[0] == "stream")
        if along and count % (16 * 2 ** len(along)):
            groups = ([(across, ())] if across else []) + [((), (b,)) for b in along]
        else:
            groups = [(across, along)]
        for across, along in groups:
            scatter = count % (16 * 2 ** len(along)) == 0
            if scatter:
                count //= 2 ** len(along)
            full = full and not across
            stages.append((across + along, along if scatter else (), bool(across), shards if full else 1, count))
            if scatter and along:
                shares.insert(0, along)
    return stages, shares


class Total:
    def __init__(self, place, grad, total, slots, take, plan):
        self.p, self.grad, self.total, self.take = place, grad, total, take
        self.slots = slots
        self.stages, self.shares = plan
        self.rows = grad.shape[1]
        self.off, self.count, self.full = 0, self.rows, True
        self.live, self.done = [], []
        self.at = 0

    def begin(self):
        bits, along, across, blocks, piece = self.stages[self.at]
        slot = self.slots[self.at]
        self.live = []
        for n, delta in enumerate(subsets(bits)):
            s, y = who = self.p.flip(delta)
            rows = rows_at(self.off + self.p.index(along, delta) * piece, piece)
            if across:
                src = self.grad.at[pl.ds(y, 1), rows, :]
            elif self.full:
                src = self.grad.at[:, rows, :]
            else:
                src = self.grad.at[pl.ds(self.p.y, 1), rows, :]
            self.live.append(remote(src, slot.at[n], self.take(), who))
        self.off = self.off + self.p.index(along) * piece
        self.count = piece
        self.full = self.full and not across

    def add(self, last):
        slot = self.slots[self.at]
        rows = rows_at(self.off, self.count)
        here = slice(None) if self.full else pl.ds(self.p.y, 1)
        value = self.grad[here, rows, :].astype(F32)
        for n, copy in enumerate(self.live):
            copy.wait_recv()
            value = value + slot[n].astype(F32)
        if last:
            self.total[rows, :] = value[0].astype(BF)
        else:
            self.grad[here, rows, :] = value.astype(BF)
        self.done += self.live
        self.at += 1

    def share(self, bits):
        v = self.total.at[rows_at(self.off, self.count), :]
        self.live = [remote(v, v, self.take(), self.p.flip(delta)) for delta in subsets(bits)]
        self.off = self.off - self.p.index(bits) * self.count
        self.count *= 2 ** len(bits)

    def arrive(self):
        for copy in self.live:
            copy.wait_recv()
        self.done += self.live

    def steps(self):
        def middle():
            self.add(False)
            self.begin()

        def turn():
            self.add(True)
            self.share(self.shares[0])

        def later(bits):
            self.arrive()
            self.share(bits)

        out = [self.begin] + [middle] * (len(self.stages) - 1) + [turn]
        return out + [functools.partial(later, bits) for bits in self.shares[1:]] + [self.arrive]

    def sent(self):
        for copy in self.done:
            copy.wait_send()


class Everywhere:
    def __init__(self, place, table, slots, take, groups):
        self.p, self.table, self.slots, self.take, self.groups = place, table, slots, take, groups
        self.live, self.done, self.at = [], [], 0

    def begin(self):
        group, slot = self.groups[self.at], self.slots[self.at]
        mine = pl.ds(self.p.index(group), 1)
        slot[mine] = self.table[...][None]
        self.live = [remote(slot.at[mine], slot.at[mine], self.take(), self.p.flip(d)) for d in subsets(group)]

    def add(self):
        for copy in self.live:
            copy.wait_recv()
        self.done += self.live
        slot = self.slots[self.at]
        total = slot[0]
        for n in range(1, slot.shape[0]):
            total = total + slot[n]
        self.table[...] = total
        self.at += 1

    def steps(self):
        def middle():
            self.add()
            self.begin()

        return [self.begin] + [middle] * (len(self.groups) - 1) + [self.add]

    def sent(self):
        for copy in self.done:
            copy.wait_send()


GRADS = ("d0", "d1", "u0", "u1", "o", "qa", "qb")
WAYS = {"d0": "yxz", "d1": "yxz", "u0": "yxz", "u1": "yxz", "o": "yxz", "qa": "yxz", "qb": "yxz"}
TICKS = (
    ("d0",),
    ("d1",),
    ("d0", "u0"),
    ("d1", "u1"),
    ("u0",),
    ("u1",),
    (),
    (),
    (),
    ("d0", "o"),
    (),
    ("o",),
    (),
    (),
    ("d0",),
    ("d1",),
    (),
    ("qa",),
    (),
    ("d0", "qa"),
    ("d1", "u0"),
    (),
    (),
    (),
    ("d0", "qb"),
    ("u0", "u1"),
    ("d1", "qb"),
    (),
    ("d0", "o"),
    ("u0",),
    ("n", "d0", "u1", "qa"),
    ("d1", "o"),
    (),
    ("u0",),
    (),
    ("n", "qa", "qb"),
    ("u1",),
    ("d1",),
    ("o",),
    ("n",),
    ("d1",),
    ("qa",),
    ("u0",),
    ("u0",),
    ("qb",),
    ("u1",),
    ("o",),
    ("qa",),
    ("u1",),
    ("qb",),
    ("o",),
    ("u1",),
    ("o",),
    ("qa",),
    ("qb",),
    ("qa",),
    ("qb",),
    ("qb",),
)


def layer_kernel(
    sizes, plan, tok, mem, old, docs, cot, wqkv, wo, wu, wd, wc, norms, out, tgrad, newold, norm_total, *rest
):
    totals = rest[:7]
    (
        xs, N, Q, K, V, PT, OT, bias, res, gres, lifted, act, gh, gl, gr, dO, Dv, dK, dV, ct,
        Wq, Wk, Wv, Wo, Wu, Wd, Wc, nblocks, ngrad, ev,
    ) = rest[7:37]
    rest = rest[37:]
    gbuf, tbuf = rest[:7], rest[7:14]
    rest = rest[14:]
    slots = []
    for stages, _ in plan["totals"]:
        slots.append(rest[: len(stages)])
        rest = rest[len(stages) :]
    nslots, rest = rest[: len(plan["groups"])], rest[len(plan["groups"]) :]
    send_ref, recv_ref, local_ref = rest
    place = Place(*sizes)
    send, recv, local = Sems(send_ref, plan["sems"]), Sems(recv_ref, plan["sems"]), Sems(local_ref, plan["local"])

    def pair():
        return send.take(), recv.take()

    shards = place.shards
    S, D = tok.shape
    M = mem.shape[0]
    H0 = M - REACH
    L = REACH + S
    T0 = REACH
    W = REACH + 128
    FF = Wu.shape[1]
    n_q = S // 128

    barrier = pltpu.get_barrier_semaphore()
    for bits in plan["partners"]:
        pl.semaphore_signal(barrier, inc=1, device_id=place.flip(bits), device_id_type=MESH)

    def fetch(src, dst):
        copy = pltpu.make_async_copy(src, dst, local.take())
        copy.start()
        return copy

    pools = [dK, dV, gl, gres, res]
    free = [[ref, 0] for ref in pools]

    def room(rows):
        for entry in free:
            if entry[1] + rows <= entry[0].shape[0]:
                entry[1] += rows
                return entry[0].at[pl.ds(entry[1] - rows, rows), :]
        raise ValueError("no room")

    r1 = wqkv.shape[0]
    jobs = {}

    def bring(name, src, target, col):
        piece = min(src.shape[0], 256)
        for n in range(0, src.shape[0], piece):
            stage = room(piece)
            copy = fetch(src.at[pl.ds(n, piece), :], stage)
            jobs.setdefault(name, []).append((copy, stage, target, col, place.y * src.shape[0] + n, piece))

    c512 = pl.ds(0, 512)
    bring("k", wqkv.at[:, pl.ds(512, 512)], Wk, 0)
    bring("v", wqkv.at[:, pl.ds(1024, 512)], Wv, 0)
    bring("q", wqkv.at[:, pl.ds(0, 512)], Wq, 0)
    tok_in = fetch(tok, xs.at[pl.ds(M, S), :])
    mem_in = fetch(mem, xs.at[pl.ds(0, M), :])
    bring("o", wo, Wo, 0)
    for c in range(FF // 512):
        bring("u", wu.at[:, pl.ds(c * 512, 512)], Wu, c * 512)
    bring("d", wd, Wd, 0)
    cot_in = fetch(cot, ct)
    bring("c", wc, Wc, 0)
    old_in = fetch(old.at[pl.ds(S // 3, old.shape[0] - S // 3), :], newold.at[pl.ds(0, old.shape[0] - S // 3), :])

    nblocks[pl.ds(place.y, 1)] = jnp.concatenate(
        [norms[...].astype(BF).astype(F32), jnp.zeros((4, norms.shape[1]), F32)], axis=0
    )[None]

    def cast(name):
        for copy, stage, target, col, start, rows in jobs[name]:
            copy.wait()
            target[rows_at(start, rows), pl.ds(col, 512)] = stage[...].astype(BF)

    cast("k")
    pl.semaphore_wait(barrier, len(plan["partners"]))
    own = nblocks.at[pl.ds(place.y, 1)]
    norm_copies = [remote(own, own, pair(), place.flip(delta)) for delta in subsets(shard_bits(shards))]
    gathers = {}

    def launch(name, buf):
        gathers[name] = Gather(place, buf, pair, plan["split"][name])
        gathers[name].start()

    launch("k", Wk)
    cast("v")
    launch("v", Wv)
    cast("q")
    launch("q", Wq)
    cast("o")
    launch("o", Wo)

    ids = docs[...].astype(F32)
    column = jnp.transpose(jnp.broadcast_to(ids, (8, ids.shape[1])))
    base = ids.shape[1] - L

    def see(b):
        key = column[base + 128 * b : base + 128 * b + W, 0:1]
        query = ids[:, base + T0 + 128 * b : base + T0 + 128 * b + 128]
        k = lax.broadcasted_iota(jnp.int32, (W, 128), 0)
        q = lax.broadcasted_iota(jnp.int32, (W, 128), 1) + T0
        bias[b] = jnp.where((key == query) & (k <= q), 0.0, -1e30)

    for b in range(n_q):
        see(b)
    cast("u")
    gathers["k"].spread()
    for copy in norm_copies:
        copy.wait_recv()
    table = jnp.concatenate([nblocks[j] for j in range(shards)], axis=1)
    g1, b1, g2, b2 = table[0:1], table[1:2], table[2:3], table[3:4]

    tok_in.wait()
    mem_in.wait()

    def ln1(i, _):
        unit, _s = normalised(xs[rows_at(H0 + i * 64, 64), :].astype(F32))
        N[rows_at(i * 64, 64), :] = (unit * g1 + b1).astype(BF)
        return 0

    lax.fori_loop(0, 10, ln1, 0)
    gathers["v"].spread()
    gathers["k"].pass_on()
    launch("u", Wu)
    lax.fori_loop(10, L // 64, ln1, 0)
    gathers["q"].spread()
    gathers["v"].pass_on()
    gathers["o"].spread()
    cast("d")
    cast("c")
    gathers["k"].finish()
    for c in range(2):
        cs = slice(c * 256, c * 256 + 256)
        K[:, cs] = nn(N[...], Wk[:, cs]).astype(BF)
    gathers["q"].pass_on()
    gathers["v"].finish()
    for c in range(2):
        cs = slice(c * 256, c * 256 + 256)
        V[:, cs] = nn(N[...], Wv[:, cs]).astype(BF)
    launch("d", Wd)
    launch("c", Wc)
    gathers["o"].pass_on()
    gathers["q"].finish()
    for c in range(2):
        cs = slice(c * 256, c * 256 + 256)
        Q[:, cs] = (nn(N[T0:, :], Wq[:, cs]).astype(BF).astype(F32) * 0.125).astype(BF)

    def attend(qb, p):
        q0, l0 = pl.multiple_of(qb * 128, 128), pl.multiple_of(p * 128, 128)
        q2 = two_heads(Q[pl.ds(q0, 128), pl.ds(l0, 128)])
        s = nt(K[pl.ds(q0, W), pl.ds(l0, 128)], q2)
        seen = bias[qb]
        s = s + jnp.concatenate([seen, seen], axis=1)
        e = jnp.exp(s - jnp.max(s, axis=0, keepdims=True))
        probs = (e * (1.0 / jnp.sum(e, axis=0, keepdims=True))).astype(BF)
        PT[p * n_q + qb] = probs
        o = tn(V[pl.ds(q0, W), pl.ds(l0, 128)], probs)
        OT[pl.ds(l0, 128), pl.ds(q0, 128)] = own_halves(o).astype(BF)

    def attend_row(i, _):
        for u in range(2):
            attend(i // 2, (i % 2) * 2 + u)
        return 0

    half = n_q
    lax.fori_loop(0, half, attend_row, 0)
    gathers["u"].spread()
    lax.fori_loop(half, half + half // 2, attend_row, 0)
    gathers["u"].pass_on()
    gathers["d"].spread()
    lax.fori_loop(half + half // 2, 2 * n_q, attend_row, 0)
    gathers["d"].pass_on()
    gathers["c"].spread()
    gathers["o"].finish()

    for c in range(2):
        cs = slice(c * 256, c * 256 + 256)
        res[:, cs] = xs[M:, cs].astype(F32) + tn(OT[...], Wo[:, cs])

    def ln2(i, _):
        r = rows_at(i * 64, 64)
        unit, _s = normalised(res[r, :])
        lifted[r, :] = (unit * g2 + b2).astype(BF)
        return 0

    lax.fori_loop(0, S // 64, ln2, 0)
    gathers["c"].pass_on()
    gathers["u"].finish()
    gathers["d"].finish()
    cot_in.wait()

    def ffn(i, _):
        cs = rows_at(i * 256, 256, 256)
        h = nn(lifted[...], Wu[:, cs])
        ga = nt(ct[...], Wd[cs, :])
        h2 = h * h
        t = jnp.tanh(GELU_C * h * (1.0 + GELU_A * h2))
        hp = 0.5 + 0.5 * t
        act[:, cs] = (h * hp).astype(BF)
        slope = hp + (0.5 * GELU_C) * h * (1.0 - t * t) * (1.0 + (3 * GELU_A) * h2)
        gh[:, cs] = (ga * slope).astype(BF)
        return 0

    lax.fori_loop(0, FF // 256, ffn, 0)

    sums = {
        name: Total(place, gbuf[i], tbuf[i], slots[i], pair, plan["totals"][i]) for i, name in enumerate(GRADS)
    }
    sums["n"] = Everywhere(place, ngrad, nslots, pair, plan["groups"])
    waiting = {name: sums[name].steps() for name in sums}
    ends = []
    clock = []

    def go(names):
        for name in names:
            if not waiting[name]:
                continue
            waiting[name].pop(0)()
            if name != "n" and not waiting[name]:
                i = GRADS.index(name)
                copy = pltpu.make_async_copy(tbuf[i], totals[i], local.take())
                copy.start()
                ends.append(copy)

    def tick():
        if len(clock) < len(plan["ticks"]):
            go(plan["ticks"][len(clock)])
        clock.append(0)

    def put(ref, start, value):
        rows = value.shape[0]
        if rows > ref.shape[1]:
            n = rows // ref.shape[1]
            ref[pl.ds(start // ref.shape[1], n)] = value.astype(BF).reshape(n, ref.shape[1], value.shape[1])
        else:
            ref[start // ref.shape[1], rows_at(start % ref.shape[1], rows), :] = value.astype(BF)

    def put_all(ref, cols, value):
        ref[:, :, cols] = value.astype(BF).reshape(ref.shape[0], ref.shape[1], value.shape[1])

    def grad_down(ref, col):
        def body(i, _):
            put(ref, i * 512, tn(act[:, rows_at(i * 512, 512, 512)], ct[:, col : col + 256]))
            return 0

        lax.fori_loop(0, FF // 512, body, 0)

    for n in range(2):
        grad_down(gbuf[n], n * 256)
        tick()
    for n in range(2):
        for c in range(2):
            piece = gh[:, n * 1024 + c * 512 : n * 1024 + c * 512 + 512]
            put_all(gbuf[2 + n], slice(c * 512, c * 512 + 512), tn(lifted[...], piece))
        tick()
    for c in range(2):
        cs = slice(c * 256, c * 256 + 256)
        gl[:, cs] = nt(gh[...], Wu[cs, :])
        tick()

    zero = jnp.zeros((1, D), F32)

    def ln2_back(i, sums_in):
        r = rows_at(i * 64, 64)
        unit, scale = normalised(res[r, :])
        gy = gl[r, :]
        x = ct[r, :].astype(F32) + norm_back(gy, unit, scale, g2)
        gres[r, :] = x
        gr[r, :] = x.astype(BF)
        return (
            sums_in[0] + jnp.sum(gy * unit, axis=0, keepdims=True),
            sums_in[1] + jnp.sum(gy, axis=0, keepdims=True),
        )

    second = (zero, zero)
    for n in range(3):
        second = lax.fori_loop(n * S // 192, (n + 1) * S // 192, ln2_back, second)
        tick()
    put_all(gbuf[4], slice(0, D), nn(OT[...], gr[...]))
    tick()
    for c in range(2):
        cs = slice(c * 256, c * 256 + 256)
        dO[:, cs] = nt(gr[...], Wo[cs, :]).astype(BF)
    for c in range(2):
        cs = slice(c * 256, c * 256 + 256)
        dt = nt(Wo[cs, :], gr[...]).astype(BF).astype(F32) * OT[cs, :].astype(F32)
        for h in range(4):
            Dv[c * 4 + h : c * 4 + h + 1, :] = jnp.sum(dt[h * 64 : h * 64 + 64], axis=0, keepdims=True)
    dK[...] = jnp.zeros_like(dK)
    dV[...] = jnp.zeros_like(dV)
    tick()

    def attend_back(qb, p):
        q0, l0 = pl.multiple_of(qb * 128, 128), pl.multiple_of(p * 128, 128)
        q2 = two_heads(Q[pl.ds(q0, 128), pl.ds(l0, 128)])
        do2 = two_heads(dO[pl.ds(q0, 128), pl.ds(l0, 128)])
        probs = PT[p * n_q + qb]
        dp = nt(V[pl.ds(q0, W), pl.ds(l0, 128)], do2)
        mean = jnp.concatenate([Dv[pl.ds(2 * p, 1), pl.ds(q0, 128)], Dv[pl.ds(2 * p + 1, 1), pl.ds(q0, 128)]], axis=1)
        ds = (probs.astype(F32) * (dp - mean)).astype(BF)
        dV[pl.ds(q0, W), pl.ds(l0, 128)] += nn(probs, do2)
        dK[pl.ds(q0, W), pl.ds(l0, 128)] += nn(ds, q2)
        dq = own_halves(tn(K[pl.ds(q0, W), pl.ds(l0, 128)], ds)) * 0.125
        Q[pl.ds(q0, 128), pl.ds(l0, 128)] = jnp.transpose(dq).astype(BF)

    for quad in range(2):
        for qb in range(n_q):
            for u in range(2):
                attend_back(qb, quad * 2 + u)
            tick()
        cs = slice(quad * 256, quad * 256 + 256)
        K[:, cs] = dK[:, cs].astype(BF)
        V[:, cs] = dV[:, cs].astype(BF)
        g = gbuf[5 + quad]
        put_all(g, slice(0, 256), tn(N[T0:, :], Q[:, cs]))
        put_all(g, slice(256, 512), tn(N[...], K[:, cs]))
        put_all(g, slice(512, 768), tn(N[...], V[:, cs]))
        tick()

    for c in range(2):
        cs = slice(c * 256, c * 256 + 256)
        dK[:, cs] = nt(K[...], Wk[cs, :]) + nt(V[...], Wv[cs, :])
        dK[T0:, cs] += nt(Q[...], Wq[cs, :])
        tick()

    def ln1_back(i, sums_in, tokens):
        unit, scale = normalised(xs[rows_at(H0 + i * 64, 64), :].astype(F32))
        gy = dK[rows_at(i * 64, 64), :]
        if tokens:
            r = rows_at(i * 64 - T0, 64)
            lifted[r, :] = (gres[r, :] + norm_back(gy, unit, scale, g1)).astype(BF)
        return (
            sums_in[0] + jnp.sum(gy * unit, axis=0, keepdims=True),
            sums_in[1] + jnp.sum(gy, axis=0, keepdims=True),
        )

    first = lax.fori_loop(0, T0 // 64, functools.partial(ln1_back, tokens=False), (zero, zero))
    tick()
    for n in range(3):
        low, high = (T0 + n * S // 3) // 64, (T0 + (n + 1) * S // 3) // 64
        first = lax.fori_loop(low, high, functools.partial(ln1_back, tokens=True), first)
        if n == 2:
            ngrad[...] = jnp.concatenate([*first, *second, jnp.zeros((4, D), F32)], axis=0)
        tick()
    tgrad_out = pltpu.make_async_copy(lifted, tgrad, local.take())
    tgrad_out.start()

    for c in range(2):
        cs = slice(c * 256, c * 256 + 256)
        gr[:, cs] = (res[:, cs] + nn(act[...], Wd[:, cs])).astype(BF)
        tick()
    out_copy = pltpu.make_async_copy(gr, out, local.take())
    out_copy.start()
    for n in range(D // 128):
        ev[n] = xs[pl.ds(0, S), n * 128 : n * 128 + 128].astype(F32)
    squeezed = None
    gathers["c"].finish()
    for t in range(3):
        every = [ev[n, pl.ds(t, S // 3, stride=3), :] for n in range(D // 128)]
        part = jnp.concatenate(every, axis=1).astype(BF)
        term = nn(part, Wc[t * D : (t + 1) * D, :])
        squeezed = term if squeezed is None else squeezed + term
        tick()
    dO[0 : S // 3, :] = squeezed.astype(BF)
    squeeze_copy = pltpu.make_async_copy(
        dO.at[pl.ds(0, S // 3), :], newold.at[pl.ds(old.shape[0] - S // 3, S // 3), :], local.take()
    )
    squeeze_copy.start()
    while len(clock) < len(plan["ticks"]):
        tick()
    while any(waiting.values()):
        go([name for name in waiting if waiting[name]])
    final = ngrad[...]
    width = norms.shape[1]
    mine = final[:, 0:width]
    for j in range(1, shards):
        mine = jnp.where(place.y == j, final[:, j * width : (j + 1) * width], mine)
    norm_total[...] = mine

    for copy in ends + [tgrad_out, out_copy, squeeze_copy, old_in]:
        copy.wait()
    for part in list(gathers.values()) + list(sums.values()):
        part.sent()
    for copy in norm_copies:
        copy.wait_send()


def run_layer(sizes, tokens, memory, cmemory, docs, cotangent, wqkv, wo, wu, wd, wc, norms):
    streams, shards = sizes
    S, D = tokens.shape
    M = memory.shape[0]
    L = REACH + S
    W = REACH + 128
    FF = wu.shape[1]
    n_q = S // 128
    shapes = [(FF, D // 2)] * 2 + [(D, FF // 2)] * 2 + [(D, D)] + [(D, 3 * D // 2)] * 2
    shapes = [(shards, rows // shards, cols) for rows, cols in shapes]
    across, along = shard_bits(shards), stream_bits(streams)
    far = [along[i : i + 2] for i in range(2, len(along), 2)]
    ways = {
        "yxz": [(CORE,), across, (NEAR,)] + far,
        "xyz": [(CORE,), (NEAR,), across] + far,
        "xzy": [(CORE,), (NEAR,)] + far + [across],
        "yx.z": [(CORE,), across + (NEAR,)] + far,
    }
    totals = [plan_total(sizes, FF if i < 2 else D, ways[WAYS[name]]) for i, name in enumerate(GRADS)]
    groups = [across + (NEAR, CORE)] + far
    used = [subsets(across), subsets((NEAR, CORE))] + [subsets(g) for g in groups]
    for stages, shares in totals:
        used += [subsets(stage[0]) for stage in stages] + [subsets(bits) for bits in shares]
    partners = sorted({tuple(sorted(delta)) for some in used for delta in some})
    sems = 7 * 4 * (shards - 1) + len(subsets(across)) + sum(len(subsets(g)) for g in groups)
    for stages, shares in totals:
        sems += sum(len(subsets(stage[0])) for stage in stages) + sum(len(subsets(bits)) for bits in shares)
    plan = {
        "totals": totals,
        "groups": groups,
        "partners": partners,
        "ticks": TICKS,
        "sems": sems,
        "local": 32,
        "split": {"k": True, "v": True, "q": True, "o": True, "u": True, "d": True, "c": True},
    }
    f32, bf = (lambda *s: pltpu.VMEM(s, F32)), (lambda *s: pltpu.VMEM(s, BF))
    scratch = [
        bf(M + S, D), bf(L, D), bf(S, D), bf(L, D), bf(L, D), bf((HEADS // 2) * n_q, W, 256), bf(D, S),
        f32(n_q, W, 128), f32(S, D), f32(S, D), bf(S, D), bf(S, FF), bf(S, FF), f32(S, D), bf(S, D), bf(S, D),
        f32(HEADS, S), f32(L, D), f32(L, D), bf(S, D),
        bf(D, D), bf(D, D), bf(D, D), bf(D, D), bf(D, FF), bf(FF, D), bf(3 * D, D),
        f32(shards, 8, norms.shape[1]), f32(8, D), f32(D // 128, S, 128),
    ]
    scratch += [bf(*s) for s in shapes]
    scratch += [bf(s[1], s[2]) for s in shapes]
    for (stages, _), s in zip(totals, shapes):
        scratch += [bf(len(subsets(bits)), blocks, piece, s[2]) for bits, _b, _a, blocks, piece in stages]
    scratch += [f32(2 ** len(g), 8, D) for g in groups]
    scratch += [pltpu.SemaphoreType.DMA((sems,)), pltpu.SemaphoreType.DMA((sems,)), pltpu.SemaphoreType.DMA((32,))]
    anywhere = pl.BlockSpec(memory_space=pl.ANY)
    vmem = pl.BlockSpec(memory_space=pltpu.VMEM)
    out_shape = [
        jax.ShapeDtypeStruct((S, D), BF),
        jax.ShapeDtypeStruct((S, D), BF),
        jax.ShapeDtypeStruct(cmemory.shape, BF),
        jax.ShapeDtypeStruct((8, norms.shape[1]), F32),
    ] + [jax.ShapeDtypeStruct((s[1], s[2]), BF) for s in shapes]
    return pl.pallas_call(
        functools.partial(layer_kernel, sizes, plan),
        out_shape=out_shape,
        in_specs=[anywhere] * 3 + [vmem] + [anywhere] * 6 + [vmem],
        out_specs=[anywhere] * 3 + [vmem] + [anywhere] * 7,
        scratch_shapes=scratch,
        compiler_params=pltpu.CompilerParams(
            collective_id=0, has_side_effects=True, vmem_limit_bytes=64 * 1024 * 1024
        ),
        name="layer",
    )(tokens, memory, cmemory, docs, cotangent, wqkv, wo, wu, wd, wc, norms)


def renew(grad, moment, average, master):
    momentum = MOMENTUM * moment + (1.0 - MOMENTUM) * grad
    updated = master - RATE * ((1.0 - MOMENTUM) * grad + MOMENTUM * momentum)
    smooth = SMOOTH * average + (1.0 - SMOOTH) * updated
    return momentum, smooth, updated


def update_kernel(*refs):
    totals, masters, moments, averages = refs[0:7], refs[7:11], refs[11:15], refs[15:19]
    norm_grad, norm_old = refs[19], refs[20:23]
    passed = refs[23:27]
    grads, momenta, smooths, updates = refs[27:31], refs[31:35], refs[35:39], refs[39:43]
    norm_out = refs[43:47]
    lifted_out = refs[47]
    kept = refs[48:52]
    step = pl.program_id(0)
    for source, target in zip(passed, kept):
        target[...] = source[...]

    @pl.when(step == 0)
    def _():
        g = norm_grad[0:4, :]
        norm_out[0][...] = g
        lifted_out[...] = g[2:4]
        for ref, value in zip(norm_out[1:], renew(g, norm_old[1][...], norm_old[2][...], norm_old[0][...])):
            ref[...] = value

    d0, d1, u0, u1, o, qa, qb = [t[...].astype(F32) for t in totals]
    pieces = []
    for c in range(0, qa.shape[1], 256):
        pieces += [qa[:, c : c + 256], qb[:, c : c + 256]]
    whole = (
        jnp.concatenate(pieces, axis=1),
        o,
        jnp.concatenate([u0, u1], axis=1),
        jnp.concatenate([d0, d1], axis=1),
    )
    for i in range(4):
        grads[i][...] = whole[i]
        new = renew(whole[i], moments[i][...], averages[i][...], masters[i][...])
        momenta[i][...], smooths[i][...], updates[i][...] = new


def run_update(totals, masters, moments, averages, norm_grad, norm_old, output, tgrad, newold, tokens, mem_rows):
    steps = 8
    while masters[1].shape[0] % (steps * 16):
        steps //= 2

    def block(x):
        return pl.BlockSpec((x.shape[0] // steps, x.shape[1]), lambda i: (i, 0))

    def fixed(x):
        return pl.BlockSpec(x.shape, lambda i: (0, 0))

    skip = (tokens.shape[0] - mem_rows) // (mem_rows // steps)
    recent = pl.BlockSpec((mem_rows // steps, tokens.shape[1]), lambda i: (i + skip, 0))
    same = [jax.ShapeDtypeStruct(m.shape, F32) for m in masters]
    small = jax.ShapeDtypeStruct(norm_old[0].shape, F32)
    lifted = jax.ShapeDtypeStruct((2, small.shape[1]), F32)
    keep = [
        jax.ShapeDtypeStruct(output.shape, BF),
        jax.ShapeDtypeStruct(tgrad.shape, BF),
        jax.ShapeDtypeStruct(newold.shape, BF),
        jax.ShapeDtypeStruct((mem_rows, tokens.shape[1]), BF),
    ]
    passed = (output, tgrad, newold, tokens)
    return pl.pallas_call(
        update_kernel,
        grid=(steps,),
        out_shape=same * 4 + [small] * 4 + [lifted] + keep,
        in_specs=[block(t) for t in totals]
        + [block(m) for m in masters] * 3
        + [fixed(norm_grad)]
        + [fixed(small)] * 3
        + [block(x) for x in passed[:3]]
        + [recent],
        out_specs=[block(m) for m in masters] * 4 + [fixed(small)] * 4 + [fixed(lifted)] + [block(x) for x in keep],
        compiler_params=pltpu.CompilerParams(vmem_limit_bytes=64 * 1024 * 1024),
        name="update",
    )(*totals, *masters, *moments, *averages, norm_grad, *norm_old, *passed)


def on_device(
    sizes, tokens, memory, cmemory, doc_ids, cotangent,
    qkv_weight, out_weight, up_weight, down_weight, conv_weight, norm_params,
    qkv_moment, out_moment, up_moment, down_moment, norm_moment,
    qkv_average, out_average, up_average, down_average, norm_average,
):
    results = run_layer(
        sizes, tokens[0], memory[0], cmemory[0], doc_ids, cotangent[0],
        qkv_weight, out_weight, up_weight, down_weight, conv_weight, norm_params.T,
    )
    output, tgrad, newold, norm_grad = results[:4]
    new = run_update(
        results[4:],
        (qkv_weight, out_weight, up_weight, down_weight),
        (qkv_moment, out_moment, up_moment, down_moment),
        (qkv_average, out_average, up_average, down_average),
        norm_grad,
        (norm_params.T, norm_moment.T, norm_average.T),
        output, tgrad, newold, tokens[0], memory.shape[1],
    )
    grads, momenta, smooths, updates = new[0:4], new[4:8], new[8:12], new[12:16]
    norms = [x.T for x in new[16:20]]
    lifted = new[20].T
    out, token_grad, new_cmemory, new_memory = new[21:25]
    return (
        out[None], new_memory[None], new_cmemory[None], token_grad[None],
        *grads, norms[0], *momenta, norms[1], *smooths, norms[2], *updates, norms[3], lifted,
    )


def solution(mesh):
    sizes = (mesh.shape["stream"], mesh.shape["shard"])
    both = ("stream", "shard")
    wide = P(both, None, None)
    rows = P("shard", None)
    return jax.shard_map(
        functools.partial(on_device, sizes),
        mesh=mesh,
        in_specs=(wide, wide, wide, P(both, None), wide) + (rows,) * 16,
        out_specs=(wide,) * 4 + (rows,) * 21,
        check_vma=False,
    )
```

```python
import functools

import jax
import jax.numpy as jnp
from jax import lax
from jax.experimental import pallas as pl
from jax.experimental.pallas import tpu as pltpu
from jax.sharding import PartitionSpec as P

HEADS = 8
MOMENTUM = 0.9
RATE = 0.0025
SMOOTH = 0.8
REACH = 448
BF = jnp.bfloat16
F32 = jnp.float32
MESH = pl.DeviceIdType.MESH
GELU_C = 0.7978845608028654
GELU_A = 0.044715


def nn(a, b):
    return lax.dot_general(a, b, (((1,), (0,)), ((), ())), preferred_element_type=F32)


def nt(a, b):
    return lax.dot_general(a, b, (((1,), (1,)), ((), ())), preferred_element_type=F32)


def tn(a, b):
    return lax.dot_general(a, b, (((0,), (0,)), ((), ())), preferred_element_type=F32)


def normalised(x):
    center = x - jnp.mean(x, axis=-1, keepdims=True)
    scale = lax.rsqrt(jnp.mean(center * center, axis=-1, keepdims=True) + 1e-5)
    return center * scale, scale


def norm_back(grad, unit, scale, gain):
    inner = grad * gain
    first = jnp.mean(inner, axis=-1, keepdims=True)
    second = jnp.mean(inner * unit, axis=-1, keepdims=True)
    return (inner - first - unit * second) * scale


def two_heads(block):
    lane = lax.broadcasted_iota(jnp.int32, block.shape, 1)
    zero = jnp.zeros_like(block)
    low = lane < 64
    return jnp.concatenate([jnp.where(low, block, zero), jnp.where(low, zero, block)], axis=0)


def own_halves(block):
    return jnp.concatenate([block[0:64, 0:128], block[64:128, 128:256]], axis=0)


def rows_at(start, count, by=16):
    return pl.ds(pl.multiple_of(start, by), count)


class Sems:
    def __init__(self, ref, size):
        self.ref, self.size, self.used = ref, size, 0

    def take(self):
        self.used += 1
        assert self.used <= self.size
        return self.ref.at[self.used - 1]


def subsets(bits):
    found = [()]
    for bit in bits:
        found += [f + (bit,) for f in found]
    return found[1:]


class Place:
    def __init__(self, streams, shards):
        self.streams, self.shards = streams, shards
        self.s = lax.axis_index("stream")
        self.y = lax.axis_index("shard")

    def value(self, axis, bit, flipped=False):
        v = ((self.s if axis == "stream" else self.y) // bit) % 2
        return 1 - v if flipped else v

    def flip(self, bits):
        s, y = self.s, self.y
        for axis, bit in bits:
            step = bit * (1 - 2 * self.value(axis, bit))
            if axis == "stream":
                s = s + step
            else:
                y = y + step
        return s, y

    def index(self, bits, flipped=()):
        total = 0
        for axis, bit in bits:
            total = total * 2 + self.value(axis, bit, (axis, bit) in flipped)
        return total


def remote(src, dst, sems, who):
    copy = pltpu.make_async_remote_copy(
        src_ref=src, dst_ref=dst, send_sem=sems[0], recv_sem=sems[1], device_id=who, device_id_type=MESH
    )
    copy.start()
    return copy


CORE, NEAR = ("stream", 1), ("stream", 2)


class Gather:
    def __init__(self, place, buf, take, split):
        self.p, self.buf, self.take = place, buf, take
        self.rows = buf.shape[0] // place.shards
        self.split = split
        self.parts = (NEAR, CORE) if split else (CORE,)
        self.count = self.rows // 2 ** len(self.parts)
        self.deltas = subsets(shard_bits(place.shards))
        self.part = place.index(self.parts)
        self.first, self.second, self.third = [], [], []

    def view(self, owner, part):
        return self.buf.at[rows_at(owner * self.rows + part * self.count, self.count), :]

    def start(self):
        for delta in self.deltas:
            v = self.view(self.p.y, self.part)
            self.first.append(remote(v, v, self.take(), self.p.flip(delta)))

    def spread(self):
        for n, delta in enumerate(self.deltas):
            self.first[n].wait_recv()
            v = self.view(self.p.flip(delta)[1], self.part)
            if self.split:
                self.second.append(remote(v, v, self.take(), self.p.flip((NEAR,))))
            self.third.append(remote(v, v, self.take(), self.p.flip((CORE,))))

    def pass_on(self):
        if self.split:
            for n, delta in enumerate(self.deltas):
                self.second[n].wait_recv()
                v = self.view(self.p.flip(delta)[1], self.p.index(self.parts, (NEAR,)))
                self.third.append(remote(v, v, self.take(), self.p.flip((CORE,))))

    def finish(self):
        for copy in self.third:
            copy.wait_recv()

    def sent(self):
        for copy in self.first + self.second + self.third:
            copy.wait_send()


def shard_bits(shards):
    bits, bit = [], shards // 2
    while bit >= 1:
        bits.append(("shard", bit))
        bit //= 2
    return tuple(bits)


def stream_bits(streams):
    bits, bit = [], 1
    while bit < streams:
        bits.append(("stream", bit))
        bit *= 2
    return tuple(bits)


def plan_total(sizes, rows, order):
    shards = sizes[1]
    count, full, stages, shares = rows // shards, True, [], []
    for group in order:
        across = tuple(b for b in group if b[0] == "shard")
        along = tuple(b for b in group if b[0] == "stream")
        if along and count % (16 * 2 ** len(along)):
            groups = ([(across, ())] if across else []) + [((), (b,)) for b in along]
        else:
            groups = [(across, along)]
        for across, along in groups:
            scatter = count % (16 * 2 ** len(along)) == 0
            if scatter:
                count //= 2 ** len(along)
            full = full and not across
            stages.append((across + along, along if scatter else (), bool(across), shards if full else 1, count))
            if scatter and along:
                shares.insert(0, along)
    return stages, shares


class Total:
    def __init__(self, place, grad, total, slots, take, plan):
        self.p, self.grad, self.total, self.take = place, grad, total, take
        self.slots = slots
        self.stages, self.shares = plan
        self.rows = grad.shape[1]
        self.off, self.count, self.full = 0, self.rows, True
        self.live, self.done = [], []
        self.at = 0

    def begin(self):
        bits, along, across, blocks, piece = self.stages[self.at]
        slot = self.slots[self.at]
        self.live = []
        for n, delta in enumerate(subsets(bits)):
            s, y = who = self.p.flip(delta)
            rows = rows_at(self.off + self.p.index(along, delta) * piece, piece)
            if across:
                src = self.grad.at[pl.ds(y, 1), rows, :]
            elif self.full:
                src = self.grad.at[:, rows, :]
            else:
                src = self.grad.at[pl.ds(self.p.y, 1), rows, :]
            self.live.append(remote(src, slot.at[n], self.take(), who))
        self.off = self.off + self.p.index(along) * piece
        self.count = piece
        self.full = self.full and not across

    def add(self, last):
        slot = self.slots[self.at]
        rows = rows_at(self.off, self.count)
        here = slice(None) if self.full else pl.ds(self.p.y, 1)
        value = self.grad[here, rows, :].astype(F32)
        for n, copy in enumerate(self.live):
            copy.wait_recv()
            value = value + slot[n].astype(F32)
        if last:
            self.total[rows, :] = value[0].astype(BF)
        else:
            self.grad[here, rows, :] = value.astype(BF)
        self.done += self.live
        self.at += 1

    def share(self, bits):
        v = self.total.at[rows_at(self.off, self.count), :]
        self.live = [remote(v, v, self.take(), self.p.flip(delta)) for delta in subsets(bits)]
        self.off = self.off - self.p.index(bits) * self.count
        self.count *= 2 ** len(bits)

    def arrive(self):
        for copy in self.live:
            copy.wait_recv()
        self.done += self.live

    def steps(self):
        def middle():
            self.add(False)
            self.begin()

        def turn():
            self.add(True)
            self.share(self.shares[0])

        def later(bits):
            self.arrive()
            self.share(bits)

        out = [self.begin] + [middle] * (len(self.stages) - 1) + [turn]
        return out + [functools.partial(later, bits) for bits in self.shares[1:]] + [self.arrive]

    def sent(self):
        for copy in self.done:
            copy.wait_send()


class Everywhere:
    def __init__(self, place, table, slots, take, groups):
        self.p, self.table, self.slots, self.take, self.groups = place, table, slots, take, groups
        self.live, self.done, self.at = [], [], 0

    def begin(self):
        group, slot = self.groups[self.at], self.slots[self.at]
        mine = pl.ds(self.p.index(group), 1)
        slot[mine] = self.table[...][None]
        self.live = [remote(slot.at[mine], slot.at[mine], self.take(), self.p.flip(d)) for d in subsets(group)]

    def add(self):
        for copy in self.live:
            copy.wait_recv()
        self.done += self.live
        slot = self.slots[self.at]
        total = slot[0]
        for n in range(1, slot.shape[0]):
            total = total + slot[n]
        self.table[...] = total
        self.at += 1

    def steps(self):
        def middle():
            self.add()
            self.begin()

        return [self.begin] + [middle] * (len(self.groups) - 1) + [self.add]

    def sent(self):
        for copy in self.done:
            copy.wait_send()


GRADS = ("d0", "d1", "u0", "u1", "o", "qa", "qb")
WAYS = {"d0": "yxz", "d1": "yxz", "u0": "yxz", "u1": "yxz", "o": "yxz", "qa": "yxz", "qb": "yxz"}
RING = 4
TICKS = (
    ("d0",),
    ("d1",),
    ("d0", "u0"),
    ("d1", "u1"),
    ("u0",),
    ("u1",),
    (),
    (),
    (),
    ("d0", "o"),
    (),
    ("o",),
    (),
    (),
    ("d0",),
    ("d1",),
    (),
    ("qa",),
    (),
    ("d0", "qa"),
    ("d1", "u0"),
    (),
    (),
    (),
    ("d0", "qb"),
    ("u0", "u1"),
    ("d1", "qb"),
    (),
    ("d0", "o"),
    ("u0",),
    ("n", "d0", "u1", "qa"),
    ("d1", "o"),
    (),
    ("u0",),
    (),
    ("n", "qa", "qb"),
    ("u1",),
    ("d1",),
    ("o",),
    ("n",),
    ("d1",),
    ("qa",),
    ("u0",),
    ("u0",),
    ("qb",),
    ("u1",),
    ("o",),
    ("qa",),
    ("u1",),
    ("qb",),
    ("o",),
    ("u1",),
    ("o",),
    ("qa",),
    ("qb",),
    ("qa",),
    ("qb",),
    ("qb",),
)


def layer_kernel(
    sizes, plan, tok, mem, old, docs, cot, wqkv, wo, wu, wd, wc, norms, *rest
):
    moments, averages, rest = rest[:4], rest[4:8], rest[8:]
    xs, ct, lifted, newold, norm_total, kept, dK, dV, seen_at, gl, gres, res, *rest = rest
    tbuf, rest = rest[:7], rest[7:]
    (N, Q, K, V, PT, OT, act, gh, Dv, Wq, Wk, Wv, Wo, Wu, Wd, Wc, nblocks, ngrad, *rest) = rest
    gbuf, rest = rest[:7], rest[7:]
    gr, dO = gh.at[:, pl.ds(0, Wo.shape[1])], gh.at[:, pl.ds(Wo.shape[1], Wo.shape[1])]
    slots = []
    for stages, _ in plan["totals"]:
        slots.append(rest[: len(stages)])
        rest = rest[len(stages) :]
    nslots, rest = rest[: len(plan["groups"])], rest[len(plan["groups"]) :]
    send_ref, recv_ref, local_ref = rest
    place = Place(*sizes)
    send, recv, local = Sems(send_ref, plan["sems"]), Sems(recv_ref, plan["sems"]), Sems(local_ref, plan["local"])

    def pair():
        return send.take(), recv.take()

    shards = place.shards
    S, D = tok.shape
    M = mem.shape[0]
    H0 = M - REACH
    L = REACH + S
    T0 = REACH
    W = REACH + 128
    FF = Wu.shape[1]
    n_q = S // 128

    barrier = pltpu.get_barrier_semaphore()
    for bits in plan["partners"]:
        pl.semaphore_signal(barrier, inc=1, device_id=place.flip(bits), device_id_type=MESH)

    def fetch(src, dst):
        copy = pltpu.make_async_copy(src, dst, local.take())
        copy.start()
        return copy

    jobs = {}

    def bring(name, pieces, target, unit, ref):
        for n, (src, row, col) in enumerate(pieces):
            stage = ref.at[pl.ds((unit + n) * r1, r1), :]
            jobs.setdefault(name, []).append((fetch(src, stage), stage, target, row, col))

    r1 = wqkv.shape[0]
    pieces = unit_list(wqkv, wo, wu, wd)
    bring("k", [(pieces[1][0], 0, 0)], Wk, 1, kept)
    bring("v", [(pieces[2][0], 0, 0)], Wv, 2, kept)
    bring("q", pieces[0:1], Wq, 0, kept)
    tok_in = fetch(tok, xs.at[pl.ds(M, S), :])
    mem_in = fetch(mem, xs.at[pl.ds(0, M), :])
    bring("o", pieces[3:4], Wo, 3, kept)
    bring("u", pieces[4 : 4 + FF // D], Wu, 4, kept)
    bring("d", pieces[4 + FF // D :], Wd, 0, dK)
    stage = dV.at[pl.ds(0, wc.shape[0]), :]
    jobs["c"] = [(fetch(wc, stage), stage, Wc, 0, 0)]
    cot_in = fetch(cot, ct)
    old_in = fetch(old.at[pl.ds(S // 3, old.shape[0] - S // 3), :], newold.at[pl.ds(0, old.shape[0] - S // 3), :])

    nblocks[pl.ds(place.y, 1)] = jnp.concatenate(
        [norms[...].astype(BF).astype(F32), jnp.zeros((4, norms.shape[1]), F32)], axis=0
    )[None]

    def cast(name):
        for copy, stage, target, row, col in jobs[name]:
            copy.wait()
            here = rows_at(place.y * (target.shape[0] // shards) + row, stage.shape[0])
            target[here, pl.ds(col, 512)] = stage[...].astype(BF)

    cast("k")
    pl.semaphore_wait(barrier, len(plan["partners"]))
    own = nblocks.at[pl.ds(place.y, 1)]
    norm_copies = [remote(own, own, pair(), place.flip(delta)) for delta in subsets(shard_bits(shards))]
    gathers = {}

    def launch(name, buf):
        gathers[name] = Gather(place, buf, pair, plan["split"][name])
        gathers[name].start()

    launch("k", Wk)
    cast("v")
    launch("v", Wv)
    cast("q")
    launch("q", Wq)
    cast("o")
    launch("o", Wo)
    cast("u")
    launch("u", Wu)
    cast("d")
    launch("d", Wd)
    cast("c")
    launch("c", Wc)

    ids = docs[...].astype(F32)
    column = jnp.transpose(jnp.broadcast_to(ids, (8, ids.shape[1])))
    base = ids.shape[1] - L

    def see(b):
        key = column[base + 128 * b : base + 128 * b + W, 0:1]
        query = ids[:, base + T0 + 128 * b : base + T0 + 128 * b + 128]
        k = lax.broadcasted_iota(jnp.int32, (W, 128), 0)
        q = lax.broadcasted_iota(jnp.int32, (W, 128), 1) + T0
        seen_at[pl.ds(b // 4 * W, W), pl.ds(b % 4 * 128, 128)] = jnp.where((key == query) & (k <= q), 0.0, -1e30)

    for b in range(n_q):
        see(b)
    gathers["k"].spread()
    for copy in norm_copies:
        copy.wait_recv()
    table = jnp.concatenate([nblocks[j] for j in range(shards)], axis=1)
    g1, b1, g2, b2 = table[0:1], table[1:2], table[2:3], table[3:4]

    tok_in.wait()
    mem_in.wait()

    def ln1(i, _):
        unit, _s = normalised(xs[rows_at(H0 + i * 64, 64), :].astype(F32))
        N[rows_at(i * 64, 64), :] = (unit * g1 + b1).astype(BF)
        return 0

    lax.fori_loop(0, 6, ln1, 0)
    gathers["v"].spread()
    lax.fori_loop(6, 12, ln1, 0)
    gathers["k"].pass_on()
    gathers["q"].spread()
    lax.fori_loop(12, L // 64, ln1, 0)
    gathers["v"].pass_on()
    gathers["o"].spread()
    gathers["k"].finish()
    for c in range(2):
        cs = slice(c * 256, c * 256 + 256)
        K[:, cs] = nn(N[...], Wk[:, cs]).astype(BF)
    gathers["q"].pass_on()
    gathers["v"].finish()
    for c in range(2):
        cs = slice(c * 256, c * 256 + 256)
        V[:, cs] = nn(N[...], Wv[:, cs]).astype(BF)
    gathers["o"].pass_on()
    gathers["q"].finish()
    for c in range(2):
        cs = slice(c * 256, c * 256 + 256)
        Q[:, cs] = (nn(N[T0:, :], Wq[:, cs]).astype(BF).astype(F32) * 0.125).astype(BF)

    def attend(qb, p):
        q0, l0 = pl.multiple_of(qb * 128, 128), pl.multiple_of(p * 128, 128)
        q2 = two_heads(Q[pl.ds(q0, 128), pl.ds(l0, 128)])
        s = nt(K[pl.ds(q0, W), pl.ds(l0, 128)], q2)
        seen = seen_at[rows_at(qb // 4 * W, W), rows_at(qb % 4 * 128, 128, 128)]
        s = s + jnp.concatenate([seen, seen], axis=1)
        e = jnp.exp(s - jnp.max(s, axis=0, keepdims=True))
        probs = (e * (1.0 / jnp.sum(e, axis=0, keepdims=True))).astype(BF)
        PT[p * n_q + qb] = probs
        o = tn(V[pl.ds(q0, W), pl.ds(l0, 128)], probs)
        OT[pl.ds(l0, 128), pl.ds(q0, 128)] = own_halves(o).astype(BF)

    def attend_row(i, _):
        for u in range(2):
            attend(i // 2, (i % 2) * 2 + u)
        return 0

    lax.fori_loop(0, 3, attend_row, 0)
    gathers["u"].spread()
    lax.fori_loop(3, 7, attend_row, 0)
    gathers["d"].spread()
    lax.fori_loop(7, 10, attend_row, 0)
    gathers["u"].pass_on()
    lax.fori_loop(10, 2 * n_q, attend_row, 0)
    gathers["c"].spread()
    gathers["o"].finish()

    for c in range(2):
        cs = slice(c * 256, c * 256 + 256)
        res[:, cs] = xs[M:, cs].astype(F32) + tn(OT[...], Wo[:, cs])

    gathers["d"].pass_on()

    def ln2(i, _):
        r = rows_at(i * 64, 64)
        unit, _s = normalised(res[r, :])
        lifted[r, :] = (unit * g2 + b2).astype(BF)
        return 0

    lax.fori_loop(0, S // 64, ln2, 0)
    gathers["u"].finish()
    gathers["d"].finish()
    cot_in.wait()

    def ffn(i, _):
        cs = rows_at(i * 256, 256, 256)
        h = nn(lifted[...], Wu[:, cs])
        ga = nt(ct[...], Wd[cs, :])
        h2 = h * h
        t = jnp.tanh(GELU_C * h * (1.0 + GELU_A * h2))
        hp = 0.5 + 0.5 * t
        act[:, cs] = (h * hp).astype(BF)
        slope = hp + (0.5 * GELU_C) * h * (1.0 - t * t) * (1.0 + (3 * GELU_A) * h2)
        gh[:, cs] = (ga * slope).astype(BF)
        return 0

    lax.fori_loop(0, FF // 256, ffn, 0)

    gathers["c"].pass_on()

    homes = unit_homes(plan["work"], r1, 2 * len(pieces))
    old_units = [p[0] for p in unit_list(*moments)] + [p[0] for p in unit_list(*averages)]
    work = (dK, dV, seen_at, gl, gres, res)
    refill = []

    def bring_old(index):
        for src, (where, row) in zip(old_units, homes):
            if where == index:
                refill.append(fetch(src, work[index].at[pl.ds(row, r1), :]))

    bring_old(2)

    sums = {
        name: Total(place, gbuf[i], tbuf[i], slots[i], pair, plan["totals"][i]) for i, name in enumerate(GRADS)
    }
    sums["n"] = Everywhere(place, ngrad, nslots, pair, plan["groups"])
    waiting = {name: sums[name].steps() for name in sums}
    clock = []

    def go(names):
        for name in names:
            if not waiting[name]:
                continue
            waiting[name].pop(0)()

    def tick():
        if len(clock) < len(plan["ticks"]):
            go(plan["ticks"][len(clock)])
        clock.append(0)

    def put(ref, start, value):
        rows = value.shape[0]
        if rows > ref.shape[1]:
            n = rows // ref.shape[1]
            ref[pl.ds(start // ref.shape[1], n)] = value.astype(BF).reshape(n, ref.shape[1], value.shape[1])
        else:
            ref[start // ref.shape[1], rows_at(start % ref.shape[1], rows), :] = value.astype(BF)

    def put_all(ref, cols, value):
        ref[:, :, cols] = value.astype(BF).reshape(ref.shape[0], ref.shape[1], value.shape[1])

    def grad_down(ref, col):
        def body(i, _):
            put(ref, i * 512, tn(act[:, rows_at(i * 512, 512, 512)], ct[:, col : col + 256]))
            return 0

        lax.fori_loop(0, FF // 512, body, 0)

    for n in range(2):
        grad_down(gbuf[n], n * 256)
        tick()
    for n in range(2):
        for c in range(2):
            piece = gh[:, n * 1024 + c * 512 : n * 1024 + c * 512 + 512]
            put_all(gbuf[2 + n], slice(c * 512, c * 512 + 512), tn(lifted[...], piece))
        tick()
    for c in range(2):
        cs = slice(c * 256, c * 256 + 256)
        gl[:, cs] = nt(gh[...], Wu[cs, :])
        tick()

    zero = jnp.zeros((1, D), F32)

    def ln2_back(i, sums_in):
        r = rows_at(i * 64, 64)
        unit, scale = normalised(res[r, :])
        gy = gl[r, :]
        x = ct[r, :].astype(F32) + norm_back(gy, unit, scale, g2)
        gres[r, :] = x
        gr[r, :] = x.astype(BF)
        return (
            sums_in[0] + jnp.sum(gy * unit, axis=0, keepdims=True),
            sums_in[1] + jnp.sum(gy, axis=0, keepdims=True),
        )

    second = (zero, zero)
    for n in range(3):
        second = lax.fori_loop(n * S // 192, (n + 1) * S // 192, ln2_back, second)
        tick()
    bring_old(3)
    put_all(gbuf[4], slice(0, D), nn(OT[...], gr[...]))
    tick()
    for c in range(2):
        cs = slice(c * 256, c * 256 + 256)
        dO[:, cs] = nt(gr[...], Wo[cs, :]).astype(BF)
    for c in range(2):
        cs = slice(c * 256, c * 256 + 256)
        dt = nt(Wo[cs, :], gr[...]).astype(BF).astype(F32) * OT[cs, :].astype(F32)
        for h in range(4):
            Dv[c * 4 + h : c * 4 + h + 1, :] = jnp.sum(dt[h * 64 : h * 64 + 64], axis=0, keepdims=True)
    dK[...] = jnp.zeros_like(dK)
    dV[...] = jnp.zeros_like(dV)
    tick()

    def attend_back(qb, p):
        q0, l0 = pl.multiple_of(qb * 128, 128), pl.multiple_of(p * 128, 128)
        q2 = two_heads(Q[pl.ds(q0, 128), pl.ds(l0, 128)])
        do2 = two_heads(dO[pl.ds(q0, 128), pl.ds(l0, 128)])
        probs = PT[p * n_q + qb]
        dp = nt(V[pl.ds(q0, W), pl.ds(l0, 128)], do2)
        mean = jnp.concatenate([Dv[pl.ds(2 * p, 1), pl.ds(q0, 128)], Dv[pl.ds(2 * p + 1, 1), pl.ds(q0, 128)]], axis=1)
        ds = (probs.astype(F32) * (dp - mean)).astype(BF)
        dV[pl.ds(q0, W), pl.ds(l0, 128)] += nn(probs, do2)
        dK[pl.ds(q0, W), pl.ds(l0, 128)] += nn(ds, q2)
        dq = own_halves(tn(K[pl.ds(q0, W), pl.ds(l0, 128)], ds)) * 0.125
        Q[pl.ds(q0, 128), pl.ds(l0, 128)] = jnp.transpose(dq).astype(BF)

    for quad in range(2):
        for qb in range(n_q):
            for u in range(2):
                attend_back(qb, quad * 2 + u)
            tick()
        cs = slice(quad * 256, quad * 256 + 256)
        K[:, cs] = dK[0:L, cs].astype(BF)
        V[:, cs] = dV[0:L, cs].astype(BF)
        g = gbuf[5 + quad]
        put_all(g, slice(0, 256), tn(N[T0:, :], Q[:, cs]))
        put_all(g, slice(256, 512), tn(N[...], K[:, cs]))
        put_all(g, slice(512, 768), tn(N[...], V[:, cs]))
        tick()

    bring_old(1)
    for c in range(2):
        cs = slice(c * 256, c * 256 + 256)
        dK[0:L, cs] = nt(K[...], Wk[cs, :]) + nt(V[...], Wv[cs, :])
        dK[T0:L, cs] += nt(Q[...], Wq[cs, :])
        tick()

    def ln1_back(i, sums_in, tokens):
        unit, scale = normalised(xs[rows_at(H0 + i * 64, 64), :].astype(F32))
        gy = dK[rows_at(i * 64, 64), :]
        if tokens:
            r = rows_at(i * 64 - T0, 64)
            lifted[r, :] = (gres[r, :] + norm_back(gy, unit, scale, g1)).astype(BF)
        return (
            sums_in[0] + jnp.sum(gy * unit, axis=0, keepdims=True),
            sums_in[1] + jnp.sum(gy, axis=0, keepdims=True),
        )

    first = lax.fori_loop(0, T0 // 64, functools.partial(ln1_back, tokens=False), (zero, zero))
    tick()
    for n in range(3):
        low, high = (T0 + n * S // 3) // 64, (T0 + (n + 1) * S // 3) // 64
        first = lax.fori_loop(low, high, functools.partial(ln1_back, tokens=True), first)
        if n == 2:
            ngrad[...] = jnp.concatenate([*first, *second, jnp.zeros((4, D), F32)], axis=0)
        tick()
    bring_old(0)
    bring_old(4)

    for c in range(2):
        cs = slice(c * 256, c * 256 + 256)
        ct[:, cs] = (res[:, cs] + nn(act[...], Wd[:, cs])).astype(BF)
        tick()
    bring_old(5)
    gathers["c"].finish()
    squeezed = None
    for t in range(3):
        row = lax.broadcasted_iota(jnp.int32, (S // 3, S), 0) * 3 + t
        pick = jnp.where(lax.broadcasted_iota(jnp.int32, (S // 3, S), 1) == row, 1.0, 0.0).astype(BF)
        term = nn(nn(pick, xs[pl.ds(0, S), :]).astype(BF), Wc[t * D : (t + 1) * D, :])
        squeezed = term if squeezed is None else squeezed + term
        tick()
    newold[pl.ds(old.shape[0] - S // 3, S // 3), :] = squeezed.astype(BF)
    while len(clock) < len(plan["ticks"]):
        tick()
    while any(waiting.values()):
        go([name for name in waiting if waiting[name]])
    final = ngrad[...]
    width = norms.shape[1]
    mine = final[:, 0:width]
    for j in range(1, shards):
        mine = jnp.where(place.y == j, final[:, j * width : (j + 1) * width], mine)
    norm_total[...] = mine

    for copy in refill + [old_in]:
        copy.wait()
    for part in list(gathers.values()) + list(sums.values()):
        part.sent()
    for copy in norm_copies:
        copy.wait_send()


def unit_list(wqkv, wo, wu, wd):
    r, w = wo.shape
    units = [(wqkv.at[:, pl.ds(c * w, w)], 0, 0) for c in range(3)] + [(wo, 0, 0)]
    units += [(wu.at[:, pl.ds(c * w, w)], 0, c * w) for c in range(wu.shape[1] // w)]
    return units + [(wd.at[pl.ds(n, r), :], n, 0) for n in range(0, wd.shape[0], r)]


def unit_homes(work, r, count):
    homes = [(i, row) for i, rows in enumerate(work) for row in range(0, rows - r + 1, r)]
    assert len(homes) >= count
    return homes[:count]


def work_rows(S):
    big = -(-(REACH + S) // 256) * 256
    return (big, big, big, S, S, S)


def run_layer(sizes, tokens, memory, cmemory, docs, cotangent, wqkv, wo, wu, wd, wc, norms, moments, averages):
    streams, shards = sizes
    S, D = tokens.shape
    M = memory.shape[0]
    L = REACH + S
    W = REACH + 128
    FF = wu.shape[1]
    n_q = S // 128
    shapes = [(FF, D // 2)] * 2 + [(D, FF // 2)] * 2 + [(D, D)] + [(D, 3 * D // 2)] * 2
    shapes = [(shards, rows // shards, cols) for rows, cols in shapes]
    across, along = shard_bits(shards), stream_bits(streams)
    far = [along[i : i + 2] for i in range(2, len(along), 2)]
    ways = {
        "yxz": [(CORE,), across, (NEAR,)] + far,
        "xyz": [(CORE,), (NEAR,), across] + far,
        "xzy": [(CORE,), (NEAR,)] + far + [across],
        "yx.z": [(CORE,), across + (NEAR,)] + far,
    }
    totals = [plan_total(sizes, FF if i < 2 else D, ways[WAYS[name]]) for i, name in enumerate(GRADS)]
    groups = [across + (NEAR, CORE)] + far
    used = [subsets(across), subsets((NEAR, CORE))] + [subsets(g) for g in groups]
    for stages, shares in totals:
        used += [subsets(stage[0]) for stage in stages] + [subsets(bits) for bits in shares]
    partners = sorted({tuple(sorted(delta)) for some in used for delta in some})
    sems = 7 * 4 * (shards - 1) + len(subsets(across)) + sum(len(subsets(g)) for g in groups)
    for stages, shares in totals:
        sems += sum(len(subsets(stage[0])) for stage in stages) + sum(len(subsets(bits)) for bits in shares)
    plan = {
        "totals": totals,
        "groups": groups,
        "partners": partners,
        "ticks": TICKS,
        "sems": sems,
        "local": 64,
        "work": work_rows(S),
        "split": {"k": True, "v": True, "q": True, "o": True, "u": True, "d": True, "c": True},
    }
    f32, bf = (lambda *s: pltpu.VMEM(s, F32)), (lambda *s: pltpu.VMEM(s, BF))
    scratch = [
        bf(L, D), bf(S, D), bf(L, D), bf(L, D), bf((HEADS // 2) * n_q, W, 256), bf(D, S), bf(S, FF), bf(S, FF),
        f32(HEADS, S), bf(D, D), bf(D, D), bf(D, D), bf(D, D), bf(D, FF), bf(FF, D), bf(3 * D, D),
        f32(shards, 8, norms.shape[1]), f32(8, D),
    ]
    scratch += [bf(*s) for s in shapes]
    for (stages, _), s in zip(totals, shapes):
        scratch += [bf(len(subsets(bits)), blocks, piece, s[2]) for bits, _b, _a, blocks, piece in stages]
    scratch += [f32(2 ** len(g), 8, D) for g in groups]
    scratch += [pltpu.SemaphoreType.DMA((sems,)), pltpu.SemaphoreType.DMA((sems,)), pltpu.SemaphoreType.DMA((64,))]
    anywhere = pl.BlockSpec(memory_space=pl.ANY)
    vmem = pl.BlockSpec(memory_space=pltpu.VMEM)
    units = 3 + 1 + FF // D
    out_shape = [bf(M + S, D), bf(S, D), bf(S, D), bf(*cmemory.shape), f32(8, norms.shape[1]), f32(units * wo.shape[0], D)]
    out_shape += [f32(rows, D) for rows in plan["work"]]
    out_shape += [bf(s[1], s[2]) for s in shapes]
    big = [pltpu.with_memory_space_constraint(x, pltpu.HBM) for x in (tokens, memory, cmemory)]
    more = [pltpu.with_memory_space_constraint(x, pltpu.HBM) for x in (cotangent, wqkv, wo, wu, wd, wc)]
    later = [pltpu.with_memory_space_constraint(x, pltpu.HBM) for x in (*moments, *averages)]
    return pl.pallas_call(
        functools.partial(layer_kernel, sizes, plan),
        out_shape=out_shape,
        in_specs=[anywhere] * 3 + [vmem] + [anywhere] * 6 + [vmem] + [anywhere] * 8,
        out_specs=[vmem] * len(out_shape),
        scratch_shapes=scratch,
        compiler_params=pltpu.CompilerParams(
            collective_id=0, has_side_effects=True, vmem_limit_bytes=82 * 512 * 1024
        ),
        name="layer",
    )(*big, docs, *more, norms, *later)


def renew(grad, moment, average, master):
    momentum = MOMENTUM * moment + (1.0 - MOMENTUM) * grad
    updated = master - RATE * ((1.0 - MOMENTUM) * grad + MOMENTUM * momentum)
    smooth = SMOOTH * average + (1.0 - SMOOTH) * updated
    return momentum, smooth, updated


def update_kernel(
    wd, xs, output, tgrad, newold, norm_grad, kept, dK, dV, seen_at, gl, gres, res, d0, d1, u0, u1, o, qa, qb, w_norm, v_norm, a_norm,
    *rest
):
    work = (dK, dV, seen_at, gl, gres, res)
    results, rest = [rest[n * 4 : n * 4 + 4] for n in range(4)], rest[16:]
    norm_out, lifted_out, rest = rest[:4], rest[4], rest[5:]
    out_to, memory_to, cmemory_to, tgrad_to, stage, late, sems = rest
    sem = iter(range(sems.shape[0]))
    copies = []

    def store(src, dst):
        copies.append(pltpu.make_async_copy(src, dst, sems.at[next(sem)]))
        copies[-1].start()

    late_in = pltpu.make_async_copy(wd, late, sems.at[next(sem)])
    late_in.start()
    g = norm_grad[0:4, :]
    norm_out[0][...] = g
    lifted_out[...] = g[2:4]
    for ref, value in zip(norm_out[1:], renew(g, v_norm[...], a_norm[...], w_norm[...])):
        ref[...] = value

    r, D = o.shape
    places = list(zip(*[[p[0] for p in unit_list(*arrays)] for arrays in results]))
    homes = unit_homes([ref.shape[0] for ref in work], r, 2 * len(places))
    half = D // 2

    def total(n):
        if n < 3:
            return jnp.concatenate([t[:, n * half : n * half + half] for t in (qa, qb)], axis=1)
        if n == 3:
            return o[...]
        n -= 4
        if n < 2 * u0.shape[1] // D:
            per = u0.shape[1] // D
            return (u0, u1)[n // per][:, n % per * D : n % per * D + D]
        n -= 2 * u0.shape[1] // D
        return jnp.concatenate([t[n * r : n * r + r, :] for t in (d0, d1)], axis=1)

    def old(n):
        where, row = homes[n]
        return work[where][pl.ds(row, r), :]

    here = kept.shape[0] // r
    for n in range(len(places)):
        if n == here:
            late_in.wait()
        master = kept[pl.ds(n * r, r), :] if n < here else late[pl.ds((n - here) * r, r), :]
        grad = total(n).astype(F32)
        new = (grad,) + renew(grad, old(n), old(len(places) + n), master)
        for m, value in enumerate(new):
            if n >= RING:
                copies[(n - RING) * 4 + m].wait()
            slot = stage.at[n % RING * 4 + m]
            slot[...] = value
            store(slot, places[n][m])
    store(output, out_to)
    store(xs.at[pl.ds(xs.shape[0] - memory_to.shape[0], memory_to.shape[0]), :], memory_to)
    store(newold, cmemory_to)
    store(tgrad, tgrad_to)
    for copy in copies[max(0, len(places) - RING) * 4 :]:
        copy.wait()


def run_update(from_layer, masters, norm_old, memory):
    r, w = masters[1].shape
    units = sum(m.size for m in masters) // (r * w)
    anywhere = pl.BlockSpec(memory_space=pl.ANY)
    vmem = pl.BlockSpec(memory_space=pltpu.VMEM)
    same = [jax.ShapeDtypeStruct(m.shape, F32) for m in masters]
    small = jax.ShapeDtypeStruct(norm_old[0].shape, F32)
    lifted = jax.ShapeDtypeStruct((2, small.shape[1]), F32)
    bf = lambda x: jax.ShapeDtypeStruct(x.shape, BF)
    keep = [bf(from_layer[1]), bf(memory), bf(from_layer[3]), bf(from_layer[2])]
    held = [pltpu.with_memory_space_constraint(x, pltpu.VMEM) for x in from_layer]
    return pl.pallas_call(
        update_kernel,
        out_shape=same * 4 + [small] * 4 + [lifted] + keep,
        in_specs=[anywhere] + [vmem] * (len(held) + 3),
        out_specs=[anywhere] * 16 + [vmem] * 5 + [anywhere] * 4,
        scratch_shapes=[
            pltpu.VMEM((RING * 4, r, w), F32),
            pltpu.VMEM(masters[3].shape, F32),
            pltpu.SemaphoreType.DMA((units * 4 + 5,)),
        ],
        compiler_params=pltpu.CompilerParams(vmem_limit_bytes=16 * 1024 * 1024),
        name="update",
    )(pltpu.with_memory_space_constraint(masters[3], pltpu.HBM), *held, *norm_old)


def on_device(
    sizes, tokens, memory, cmemory, doc_ids, cotangent,
    qkv_weight, out_weight, up_weight, down_weight, conv_weight, norm_params,
    qkv_moment, out_moment, up_moment, down_moment, norm_moment,
    qkv_average, out_average, up_average, down_average, norm_average,
):
    masters = (qkv_weight, out_weight, up_weight, down_weight)
    from_layer = run_layer(
        sizes, tokens[0], memory[0], cmemory[0], doc_ids, cotangent[0], *masters, conv_weight, norm_params.T,
        (qkv_moment, out_moment, up_moment, down_moment), (qkv_average, out_average, up_average, down_average),
    )
    new = run_update(from_layer, masters, (norm_params.T, norm_moment.T, norm_average.T), memory[0])
    grads, momenta, smooths, updates = new[0:4], new[4:8], new[8:12], new[12:16]
    norms = [x.T for x in new[16:20]]
    lifted = new[20].T
    out, new_memory, new_cmemory, token_grad = new[21:25]
    return (
        out[None], new_memory[None], new_cmemory[None], token_grad[None],
        *grads, norms[0], *momenta, norms[1], *smooths, norms[2], *updates, norms[3], lifted,
    )


def solution(mesh):
    sizes = (mesh.shape["stream"], mesh.shape["shard"])
    both = ("stream", "shard")
    wide = P(both, None, None)
    rows = P("shard", None)
    return jax.shard_map(
        functools.partial(on_device, sizes),
        mesh=mesh,
        in_specs=(wide, wide, wide, P(both, None), wide) + (rows,) * 16,
        out_specs=(wide,) * 4 + (rows,) * 21,
        check_vma=False,
    )
```

```python
import functools

import jax
import jax.numpy as jnp
from jax import lax
from jax.experimental import pallas as pl
from jax.experimental.pallas import tpu as pltpu
from jax.sharding import PartitionSpec as P

HEADS = 8
MOMENTUM = 0.9
RATE = 0.0025
SMOOTH = 0.8
REACH = 448
BF = jnp.bfloat16
F32 = jnp.float32
MESH = pl.DeviceIdType.MESH
GELU_C = 0.7978845608028654
GELU_A = 0.044715


def nn(a, b):
    return lax.dot_general(a, b, (((1,), (0,)), ((), ())), preferred_element_type=F32)


def nt(a, b):
    return lax.dot_general(a, b, (((1,), (1,)), ((), ())), preferred_element_type=F32)


def tn(a, b):
    return lax.dot_general(a, b, (((0,), (0,)), ((), ())), preferred_element_type=F32)


def normalised(x):
    center = x - jnp.mean(x, axis=-1, keepdims=True)
    scale = lax.rsqrt(jnp.mean(center * center, axis=-1, keepdims=True) + 1e-5)
    return center * scale, scale


def norm_back(grad, unit, scale, gain):
    inner = grad * gain
    first = jnp.mean(inner, axis=-1, keepdims=True)
    second = jnp.mean(inner * unit, axis=-1, keepdims=True)
    return (inner - first - unit * second) * scale


def two_heads(block):
    lane = lax.broadcasted_iota(jnp.int32, block.shape, 1)
    zero = jnp.zeros_like(block)
    low = lane < 64
    return jnp.concatenate([jnp.where(low, block, zero), jnp.where(low, zero, block)], axis=0)


def own_halves(block):
    return jnp.concatenate([block[0:64, 0:128], block[64:128, 128:256]], axis=0)


def rows_at(start, count, by=16):
    return pl.ds(pl.multiple_of(start, by), count)


class Sems:
    def __init__(self, ref, size):
        self.ref, self.size, self.used = ref, size, 0

    def take(self):
        self.used += 1
        assert self.used <= self.size
        return self.ref.at[self.used - 1]


def subsets(bits):
    found = [()]
    for bit in bits:
        found += [f + (bit,) for f in found]
    return found[1:]


class Place:
    def __init__(self, streams, shards):
        self.streams, self.shards = streams, shards
        self.s = lax.axis_index("stream")
        self.y = lax.axis_index("shard")

    def value(self, axis, bit, flipped=False):
        v = ((self.s if axis == "stream" else self.y) // bit) % 2
        return 1 - v if flipped else v

    def flip(self, bits):
        s, y = self.s, self.y
        for axis, bit in bits:
            step = bit * (1 - 2 * self.value(axis, bit))
            if axis == "stream":
                s = s + step
            else:
                y = y + step
        return s, y

    def index(self, bits, flipped=()):
        total = 0
        for axis, bit in bits:
            total = total * 2 + self.value(axis, bit, (axis, bit) in flipped)
        return total


def remote(src, dst, sems, who):
    copy = pltpu.make_async_remote_copy(
        src_ref=src, dst_ref=dst, send_sem=sems[0], recv_sem=sems[1], device_id=who, device_id_type=MESH
    )
    copy.start()
    return copy


CORE, NEAR = ("stream", 1), ("stream", 2)


class Gather:
    def __init__(self, place, buf, take, split, piece=(0, 1), cols=None):
        self.p, self.buf, self.take = place, buf, take
        self.block = buf.shape[0] // place.shards
        self.rows = self.block // piece[1]
        self.first_row = piece[0] * self.rows
        self.cols = cols or pl.ds(0, buf.shape[1])
        self.split = split
        self.parts = (NEAR, CORE) if split else (CORE,)
        self.count = self.rows // 2 ** len(self.parts)
        self.deltas = subsets(shard_bits(place.shards))
        self.part = place.index(self.parts)
        self.first, self.second, self.third = [], [], []

    def view(self, owner, part):
        start = owner * self.block + self.first_row + part * self.count
        return self.buf.at[rows_at(start, self.count), self.cols]

    def start(self):
        for delta in self.deltas:
            v = self.view(self.p.y, self.part)
            self.first.append(remote(v, v, self.take(), self.p.flip(delta)))

    def spread(self):
        for n, delta in enumerate(self.deltas):
            self.first[n].wait_recv()
            v = self.view(self.p.flip(delta)[1], self.part)
            if self.split:
                self.second.append(remote(v, v, self.take(), self.p.flip((NEAR,))))
            self.third.append(remote(v, v, self.take(), self.p.flip((CORE,))))

    def pass_on(self):
        if self.split:
            for n, delta in enumerate(self.deltas):
                self.second[n].wait_recv()
                v = self.view(self.p.flip(delta)[1], self.p.index(self.parts, (NEAR,)))
                self.third.append(remote(v, v, self.take(), self.p.flip((CORE,))))

    def finish(self):
        for copy in self.third:
            copy.wait_recv()

    def sent(self):
        for copy in self.first + self.second + self.third:
            copy.wait_send()


def shard_bits(shards):
    bits, bit = [], shards // 2
    while bit >= 1:
        bits.append(("shard", bit))
        bit //= 2
    return tuple(bits)


def stream_bits(streams):
    bits, bit = [], 1
    while bit < streams:
        bits.append(("stream", bit))
        bit *= 2
    return tuple(bits)


def plan_total(sizes, rows, order, merge=False):
    shards = sizes[1]
    count, full, stages, shares = rows // shards, True, [], []
    for group in order:
        across = tuple(b for b in group if b[0] == "shard")
        along = tuple(b for b in group if b[0] == "stream")
        if along and count % (16 * 2 ** len(along)):
            groups = ([(across, ())] if across else []) + [((), (b,)) for b in along]
        else:
            groups = [(across, along)]
        for across, along in groups:
            scatter = count % (16 * 2 ** len(along)) == 0
            if scatter:
                count //= 2 ** len(along)
            full = full and not across
            stages.append((across + along, along if scatter else (), bool(across), shards if full else 1, count))
            if scatter and along:
                shares.insert(0, along)
    if merge and len(shares) > 2:
        shares = [tuple(b for group in shares[-2::-1] for b in group), shares[-1]]
    return stages, shares


class Total:
    def __init__(self, place, grad, total, slots, take, plan):
        self.p, self.grad, self.total, self.take = place, grad, total, take
        self.slots = slots
        self.stages, self.shares = plan
        self.rows = grad.shape[1]
        self.off, self.count, self.full = 0, self.rows, True
        self.live, self.done = [], []
        self.at = 0

    def begin(self):
        bits, along, across, blocks, piece = self.stages[self.at]
        slot = self.slots[self.at]
        self.live = []
        for n, delta in enumerate(subsets(bits)):
            s, y = who = self.p.flip(delta)
            rows = rows_at(self.off + self.p.index(along, delta) * piece, piece)
            if across:
                src = self.grad.at[pl.ds(y, 1), rows, :]
            elif self.full:
                src = self.grad.at[:, rows, :]
            else:
                src = self.grad.at[pl.ds(self.p.y, 1), rows, :]
            self.live.append(remote(src, slot.at[n], self.take(), who))
        self.off = self.off + self.p.index(along) * piece
        self.count = piece
        self.full = self.full and not across

    def add(self, last):
        slot = self.slots[self.at]
        rows = rows_at(self.off, self.count)
        here = slice(None) if self.full else pl.ds(self.p.y, 1)
        value = self.grad[here, rows, :].astype(F32)
        for n, copy in enumerate(self.live):
            copy.wait_recv()
            value = value + slot[n].astype(F32)
        if last:
            self.total[rows, :] = value[0].astype(BF)
        else:
            self.grad[here, rows, :] = value.astype(BF)
        self.done += self.live
        self.at += 1

    def share(self, bits):
        v = self.total.at[rows_at(self.off, self.count), :]
        self.live = [remote(v, v, self.take(), self.p.flip(delta)) for delta in subsets(bits)]
        self.off = self.off - self.p.index(bits) * self.count
        self.count *= 2 ** len(bits)

    def arrive(self):
        for copy in self.live:
            copy.wait_recv()
        self.done += self.live

    def steps(self):
        def middle():
            self.add(False)
            self.begin()

        def turn():
            self.add(True)
            self.share(self.shares[0])

        def later(bits):
            self.arrive()
            self.share(bits)

        out = [self.begin] + [middle] * (len(self.stages) - 1) + [turn]
        return out + [functools.partial(later, bits) for bits in self.shares[1:]] + [self.arrive]

    def sent(self):
        for copy in self.done:
            copy.wait_send()


class Everywhere:
    def __init__(self, place, table, slots, take, groups):
        self.p, self.table, self.slots, self.take, self.groups = place, table, slots, take, groups
        self.live, self.done, self.at = [], [], 0

    def begin(self):
        group, slot = self.groups[self.at], self.slots[self.at]
        mine = pl.ds(self.p.index(group), 1)
        slot[mine] = self.table[...][None]
        self.live = [remote(slot.at[mine], slot.at[mine], self.take(), self.p.flip(d)) for d in subsets(group)]

    def add(self):
        for copy in self.live:
            copy.wait_recv()
        self.done += self.live
        slot = self.slots[self.at]
        total = slot[0]
        for n in range(1, slot.shape[0]):
            total = total + slot[n]
        self.table[...] = total
        self.at += 1

    def steps(self):
        def middle():
            self.add()
            self.begin()

        return [self.begin] + [middle] * (len(self.groups) - 1) + [self.add]

    def sent(self):
        for copy in self.done:
            copy.wait_send()


GRADS = ("d0", "d1", "u0", "u1", "o", "qa", "qb")
WAYS = {"d0": "yx.z", "d1": "yx.z", "u0": "yx.z", "u1": "yx.z", "o": "x.y.z", "qa": "y.x.z+", "qb": "x.y.z"}
RING = 4
TICKS = (
    ("d0",),
    ("d1", "d0"),
    ("d1", "u0"),
    ("u1",),
    ("u0", "u1"),
    (),
    (),
    (),
    (),
    ("o",),
    ("d0", "o"),
    (),
    (),
    (),
    (),
    (),
    (),
    ("qa", "d1"),
    ("d0",),
    ("qa",),
    (),
    (),
    ("u0",),
    (),
    ("qb",),
    ("d1",),
    ("qb",),
    (),
    (),
    ("d0", "u1"),
    (),
    ("n",),
    (),
    ("u0", "o"),
    ("qa",),
    ("n",),
    ("d1",),
    ("qb",),
    ("o",),
    ("u1",),
    ("n",),
    ("d0",),
    ("d0",),
    ("u0",),
    ("qb",),
    ("qa",),
    ("o",),
    ("d1",),
    ("u1",),
    ("d1",),
    ("u0",),
    ("qb",),
    ("u0",),
    ("qa",),
    ("u1",),
    ("o",),
    ("u1",),
    ("qb",),
    ("o",),
    ("o",),
    ("qa",),
    ("qb",),
    ("qa",),
    ("qb",),
)


def layer_kernel(
    sizes, plan, tok, mem, old, docs, cot, wqkv, wo, wu, wd, wc, norms, *rest
):
    moments, averages, rest = rest[:4], rest[4:8], rest[8:]
    xs, ct, lifted, newold, norm_total, kept, dK, dV, seen_at, gl, gres, res, *rest = rest
    tbuf, rest = rest[:7], rest[7:]
    (N, Q, K, V, PT, OT, act, gh, Dv, Wq, Wk, Wv, Wo, Wu, Wd, Wc, nblocks, ngrad, *rest) = rest
    gbuf, rest = rest[:7], rest[7:]
    gr, dO = gh.at[:, pl.ds(0, Wo.shape[1])], gh.at[:, pl.ds(Wo.shape[1], Wo.shape[1])]
    slots = []
    for stages, _ in plan["totals"]:
        slots.append(rest[: len(stages)])
        rest = rest[len(stages) :]
    nslots, rest = rest[: len(plan["groups"])], rest[len(plan["groups"]) :]
    send_ref, recv_ref, local_ref = rest
    place = Place(*sizes)
    send, recv, local = Sems(send_ref, plan["sems"]), Sems(recv_ref, plan["sems"]), Sems(local_ref, plan["local"])

    def pair():
        return send.take(), recv.take()

    shards = place.shards
    S, D = tok.shape
    M = mem.shape[0]
    H0 = M - REACH
    L = REACH + S
    T0 = REACH
    W = REACH + 128
    FF = Wu.shape[1]
    n_q = S // 128

    barrier = pltpu.get_barrier_semaphore()
    for bits in plan["partners"]:
        pl.semaphore_signal(barrier, inc=1, device_id=place.flip(bits), device_id_type=MESH)

    def fetch(src, dst):
        copy = pltpu.make_async_copy(src, dst, local.take())
        copy.start()
        return copy

    jobs = {}

    def bring(name, pieces, target, unit, ref):
        for n, (src, row, col) in enumerate(pieces):
            stage = ref.at[pl.ds((unit + n) * r1, r1), :]
            jobs.setdefault(name, []).append((fetch(src, stage), stage, target, row, col))

    r1 = wqkv.shape[0]
    pieces = unit_list(wqkv, wo, wu, wd)
    bring("k", [(pieces[1][0], 0, 0)], Wk, 1, kept)
    bring("v", [(pieces[2][0], 0, 0)], Wv, 2, kept)
    bring("q", pieces[0:1], Wq, 0, kept)
    tok_in = fetch(tok, xs.at[pl.ds(M, S), :])
    mem_in = fetch(mem, xs.at[pl.ds(0, M), :])
    bring("o", pieces[3:4], Wo, 3, kept)
    bring("u", pieces[4 : 4 + FF // D], Wu, 0, dV)
    bring("d", pieces[4 + FF // D :], Wd, 0, dK)
    stage = seen_at.at[pl.ds(0, wc.shape[0]), :]
    jobs["c"] = [(fetch(wc, stage), stage, Wc, 0, 0)]
    cot_in = fetch(cot, ct)
    old_in = fetch(old.at[pl.ds(S // 3, old.shape[0] - S // 3), :], newold.at[pl.ds(0, old.shape[0] - S // 3), :])

    nblocks[pl.ds(place.y, 1)] = jnp.concatenate(
        [norms[...].astype(BF).astype(F32), jnp.zeros((4, norms.shape[1]), F32)], axis=0
    )[None]

    def cast(name):
        for copy, stage, target, row, col in jobs[name]:
            copy.wait()
            here = rows_at(place.y * (target.shape[0] // shards) + row, stage.shape[0])
            target[here, pl.ds(col, 512)] = stage[...].astype(BF)

    cast("k")
    pl.semaphore_wait(barrier, len(plan["partners"]))
    own = nblocks.at[pl.ds(place.y, 1)]
    norm_copies = [remote(own, own, pair(), place.flip(delta)) for delta in subsets(shard_bits(shards))]
    gathers = {}

    def launch(name, buf, **piece):
        gathers[name] = Gather(place, buf, pair, plan["split"], **piece)
        gathers[name].start()

    launch("k", Wk)
    cast("v")
    launch("v", Wv)
    cast("q")
    launch("q", Wq)
    cast("o")
    launch("o", Wo)
    cast("u")
    for n in range(2):
        launch("u" + str(n), Wu, cols=pl.ds(n * FF // 2, FF // 2))
    cast("d")
    for n in range(2):
        launch("d" + str(n), Wd, piece=(n, 2))
    cast("c")
    launch("c", Wc)

    ids = docs[...].astype(F32)
    column = jnp.transpose(jnp.broadcast_to(ids, (8, ids.shape[1])))
    base = ids.shape[1] - L

    def see(b):
        key = column[base + 128 * b : base + 128 * b + W, 0:1]
        query = ids[:, base + T0 + 128 * b : base + T0 + 128 * b + 128]
        k = lax.broadcasted_iota(jnp.int32, (W, 128), 0)
        q = lax.broadcasted_iota(jnp.int32, (W, 128), 1) + T0
        seen_at[pl.ds(b // 4 * W, W), pl.ds(b % 4 * 128, 128)] = jnp.where((key == query) & (k <= q), 0.0, -1e30)

    for b in range(n_q):
        see(b)
    gathers["k"].spread()
    for copy in norm_copies:
        copy.wait_recv()
    table = jnp.concatenate([nblocks[j] for j in range(shards)], axis=1)
    g1, b1, g2, b2 = table[0:1], table[1:2], table[2:3], table[3:4]

    tok_in.wait()
    mem_in.wait()

    def ln1(n):
        r = slice(n * L // 4, (n + 1) * L // 4)
        unit, _s = normalised(xs[H0 + r.start : H0 + r.stop, :].astype(F32))
        N[r, :] = (unit * g1 + b1).astype(BF)

    ln1(0)
    ln1(1)
    gathers["v"].spread()
    ln1(2)
    ln1(3)
    gathers["k"].pass_on()
    gathers["q"].spread()
    gathers["v"].pass_on()
    gathers["k"].finish()
    for c in range(2):
        cs = slice(c * 256, c * 256 + 256)
        for r in (slice(0, L // 2), slice(L // 2, L)):
            K[r, cs] = nn(N[r, :], Wk[:, cs]).astype(BF)
    gathers["o"].spread()
    gathers["q"].pass_on()
    gathers["v"].finish()
    for c in range(2):
        cs = slice(c * 256, c * 256 + 256)
        for r in (slice(0, L // 2), slice(L // 2, L)):
            V[r, cs] = nn(N[r, :], Wv[:, cs]).astype(BF)
    gathers["o"].pass_on()
    gathers["q"].finish()
    for c in range(2):
        cs = slice(c * 256, c * 256 + 256)
        Q[:, cs] = (nn(N[T0:, :], Wq[:, cs]).astype(BF).astype(F32) * 0.125).astype(BF)

    def scores(i, u, slot):
        qb, p = i // 2, (i % 2) * 2 + u
        q0, l0 = rows_at(qb * 128, 128, 128), rows_at(p * 128, 128, 128)
        s = nt(K[rows_at(qb * 128, W, 128), l0], two_heads(Q[q0, l0]))
        seen = seen_at[rows_at(qb // 4 * W, W), rows_at(qb % 4 * 128, 128, 128)]
        raw[slot][0:W, u * 256 : u * 256 + 256] = s + jnp.concatenate([seen, seen], axis=1)

    def attend(i, u, slot):
        qb, p = i // 2, (i % 2) * 2 + u
        q0, l0 = rows_at(qb * 128, 128, 128), rows_at(p * 128, 128, 128)
        cs = slice(u * 256, u * 256 + 256)
        pieces = [slice(c, c + 64) for c in range(0, W, 64)]
        top, total = None, None
        for r in pieces:
            part = jnp.max(raw[slot][r, cs].reshape(8, 8, 256), axis=0)
            top = part if top is None else jnp.maximum(top, part)
        top = jnp.max(top, axis=0, keepdims=True)
        for r in pieces:
            e = jnp.exp(raw[slot][r, cs] - top)
            raw[slot][r, cs] = e
            part = jnp.sum(e.reshape(8, 8, 256), axis=0)
            total = part if total is None else total + part
        scale = 1.0 / jnp.sum(total, axis=0, keepdims=True)
        for r in pieces:
            PT[p * n_q + qb, r, :] = (raw[slot][r, cs] * scale).astype(BF)
        OT[l0, q0] = own_halves(tn(V[rows_at(qb * 128, W, 128), l0], PT[p * n_q + qb])).astype(BF)

    def attend_two(j, _):
        for slot in range(2):
            for u in range(2):
                scores(jnp.minimum(2 * j + slot + 1, 2 * n_q - 1), u, 1 - slot)
            for u in range(2):
                attend(2 * j + slot, u, slot)
        return 0

    raw = (gl, gres)
    for u in range(2):
        scores(0, u, 0)
    gathers["u0"].spread()
    lax.fori_loop(0, 2, attend_two, 0)
    gathers["u1"].spread()
    lax.fori_loop(2, 4, attend_two, 0)
    gathers["d0"].spread()
    gathers["u0"].pass_on()
    lax.fori_loop(4, n_q, attend_two, 0)
    gathers["d1"].spread()
    gathers["u1"].pass_on()
    gathers["o"].finish()

    for c in range(2):
        cs = slice(c * 256, c * 256 + 256)
        res[:, cs] = xs[M:, cs].astype(F32) + tn(OT[...], Wo[:, cs])

    for n in range(3):
        r = slice(n * S // 3, (n + 1) * S // 3)
        unit, _s = normalised(res[r, :])
        lifted[r, :] = (unit * g2 + b2).astype(BF)
    gathers["d0"].pass_on()
    cot_in.wait()
    gathers["u0"].finish()
    gathers["u1"].finish()

    tiles = FF // 256

    def tile_at(i):
        return rows_at((i + place.y * (tiles // shards)) % tiles * 256, 256, 256)

    def ffn_in(i, slot):
        here = slice(slot * 256, slot * 256 + 256)
        dK[0:S, here] = nn(lifted[...], Wu[:, tile_at(i)])
        dV[0:S, here] = nt(ct[...], Wd[tile_at(i), :])

    def ffn_out(i, slot):
        here = slice(slot * 256, slot * 256 + 256)
        for n in range(0, S, 128):
            r = slice(n, n + 128)
            h, ga = dK[r, here], dV[r, here]
            h2 = h * h
            hp = 0.5 + 0.5 * jnp.tanh(h * (GELU_C + (GELU_C * GELU_A) * h2))
            a = h * hp
            slope = hp + (a - a * hp) * (2.0 * GELU_C + (6.0 * GELU_C * GELU_A) * h2)
            act[r, tile_at(i)] = a.astype(BF)
            gh[r, tile_at(i)] = (ga * slope).astype(BF)

    ffn_in(0, 0)
    for i in range(tiles):
        if i + 1 == tiles // shards:
            gathers["d1"].pass_on()
            gathers["d0"].finish()
            gathers["d1"].finish()
        if i + 1 < tiles:
            ffn_in(i + 1, (i + 1) % 2)
        ffn_out(i, i % 2)
    gathers["c"].spread()

    homes = unit_homes(plan["work"], r1, 2 * len(pieces))
    old_units = [p[0] for p in unit_list(*moments)] + [p[0] for p in unit_list(*averages)]
    work = (dK, dV, seen_at, gl, gres, res)
    refill = []

    def bring_old(index):
        for src, (where, row) in zip(old_units, homes):
            if where == index:
                refill.append(fetch(src, work[index].at[pl.ds(row, r1), :]))

    sums = {
        name: Total(place, gbuf[i], tbuf[i], slots[i], pair, plan["totals"][i]) for i, name in enumerate(GRADS)
    }
    sums["n"] = Everywhere(place, ngrad, nslots, pair, plan["groups"])
    waiting = {name: sums[name].steps() for name in sums}
    clock = []

    def go(names):
        for name in names:
            if not waiting[name]:
                continue
            waiting[name].pop(0)()

    def tick():
        if len(clock) < len(plan["ticks"]):
            go(plan["ticks"][len(clock)])
        clock.append(0)

    def put(ref, start, value):
        rows = value.shape[0]
        if rows > ref.shape[1]:
            n = rows // ref.shape[1]
            ref[pl.ds(start // ref.shape[1], n)] = value.astype(BF).reshape(n, ref.shape[1], value.shape[1])
        else:
            ref[start // ref.shape[1], rows_at(start % ref.shape[1], rows), :] = value.astype(BF)

    def put_all(ref, cols, value):
        ref[:, :, cols] = value.astype(BF).reshape(ref.shape[0], ref.shape[1], value.shape[1])

    def grad_down(ref, col):
        def body(i, _):
            put(ref, i * 512, tn(act[:, rows_at(i * 512, 512, 512)], ct[:, col : col + 256]))
            return 0

        lax.fori_loop(0, FF // 512, body, 0)

    for n in range(2):
        grad_down(gbuf[n], n * 256)
        tick()
    for n in range(2):
        for c in range(2):
            piece = gh[:, n * 1024 + c * 512 : n * 1024 + c * 512 + 512]
            put_all(gbuf[2 + n], slice(c * 512, c * 512 + 512), tn(lifted[...], piece))
        tick()
    for c in range(2):
        cs = slice(c * 256, c * 256 + 256)
        gl[:, cs] = nt(gh[...], Wu[cs, :])
        tick()

    def by_eight(x):
        return jnp.sum(x.reshape(x.shape[0] // 8, 8, D), axis=0)

    second = [jnp.zeros((8, D), F32)] * 2
    for n in range(3):
        r = slice(n * S // 3, (n + 1) * S // 3)
        unit, scale = normalised(res[r, :])
        gy = gl[r, :]
        x = ct[r, :].astype(F32) + norm_back(gy, unit, scale, g2)
        gres[r, :] = x
        gr[r, :] = x.astype(BF)
        second = [second[0] + by_eight(gy * unit), second[1] + by_eight(gy)]
        tick()
    put_all(gbuf[4], slice(0, D), nn(OT[...], gr[...]))
    tick()
    for c in range(2):
        cs = slice(c * 256, c * 256 + 256)
        dO[:, cs] = nt(gr[...], Wo[cs, :]).astype(BF)
    for c in range(2):
        cs = slice(c * 256, c * 256 + 256)
        dt = nt(Wo[cs, :], gr[...]).astype(BF).astype(F32) * OT[cs, :].astype(F32)
        for h in range(4):
            Dv[c * 2 + h // 2, h % 2 : h % 2 + 1, :] = jnp.sum(dt[h * 64 : h * 64 + 64], axis=0, keepdims=True)
    dK[...] = jnp.zeros_like(dK)
    dV[...] = jnp.zeros_like(dV)
    tick()

    def back_in(i, u, slot):
        qb, p = i % n_q, i // n_q * 2 + u
        q0, l0 = slice(qb * 128, qb * 128 + 128), slice(p * 128, p * 128 + 128)
        raw[slot][0:W, u * 256 : u * 256 + 256] = nt(V[qb * 128 : qb * 128 + W, l0], two_heads(dO[q0, l0]))

    def back_out(i, u, slot):
        qb, p = i % n_q, i // n_q * 2 + u
        q0, l0, keys = slice(qb * 128, qb * 128 + 128), slice(p * 128, p * 128 + 128), slice(qb * 128, qb * 128 + W)
        mean = jnp.concatenate([Dv[p, 0:1, q0], Dv[p, 1:2, q0]], axis=1)
        probs = PT[p * n_q + qb]
        ds = (probs.astype(F32) * (raw[slot][0:W, u * 256 : u * 256 + 256] - mean)).astype(BF)
        dV[keys, l0] += nn(probs, two_heads(dO[q0, l0]))
        dK[keys, l0] += nn(ds, two_heads(Q[q0, l0]))
        dq = own_halves(tn(K[keys, l0], ds)) * 0.125
        Q[q0, l0] = jnp.transpose(dq).astype(BF)

    raw = (gl, seen_at)
    for u in range(2):
        back_in(0, u, 0)
    for i in range(2 * n_q):
        if i + 1 < 2 * n_q:
            for u in range(2):
                back_in(i + 1, u, (i + 1) % 2)
        for u in range(2):
            back_out(i, u, i % 2)
        tick()
        if i % n_q == n_q - 1:
            quad = i // n_q
            cs = slice(quad * 256, quad * 256 + 256)
            K[:, cs] = dK[0:L, cs].astype(BF)
            V[:, cs] = dV[0:L, cs].astype(BF)
            g = gbuf[5 + quad]
            put_all(g, slice(0, 256), tn(N[T0:, :], Q[:, cs]))
            put_all(g, slice(256, 512), tn(N[...], K[:, cs]))
            put_all(g, slice(512, 768), tn(N[...], V[:, cs]))
            tick()

    for index in range(1, 4):
        bring_old(index)
    for c in range(2):
        cs = slice(c * 256, c * 256 + 256)
        for r in (slice(0, L // 2), slice(L // 2, L)):
            dK[r, cs] = nt(K[r, :], Wk[cs, :])
            dK[r, cs] += nt(V[r, :], Wv[cs, :])
        dK[T0:L, cs] += nt(Q[...], Wq[cs, :])
        tick()

    first = [jnp.zeros((8, D), F32)] * 2
    for low, high in [(0, T0 // 2), (T0 // 2, T0)] + [(T0 + n * S // 3, T0 + (n + 1) * S // 3) for n in range(3)]:
        unit, scale = normalised(xs[H0 + low : H0 + high, :].astype(F32))
        gy = dK[low:high, :]
        if low >= T0:
            r = slice(low - T0, high - T0)
            lifted[r, :] = (gres[r, :] + norm_back(gy, unit, scale, g1)).astype(BF)
        first = [first[0] + by_eight(gy * unit), first[1] + by_eight(gy)]
        if high == L:
            rows = [jnp.sum(x, axis=0, keepdims=True) for x in first + second]
            ngrad[...] = jnp.concatenate(rows + [jnp.zeros((4, D), F32)], axis=0)
        tick()
    bring_old(0)
    bring_old(4)

    for c in range(2):
        cs = slice(c * 256, c * 256 + 256)
        ct[:, cs] = (res[:, cs] + nn(act[...], Wd[:, cs])).astype(BF)
        tick()
    bring_old(5)
    gathers["c"].pass_on()
    gathers["c"].finish()
    squeezed = None
    for t in range(3):
        row = lax.broadcasted_iota(jnp.int32, (S // 3, S), 0) * 3 + t
        pick = jnp.where(lax.broadcasted_iota(jnp.int32, (S // 3, S), 1) == row, 1.0, 0.0).astype(BF)
        term = nn(nn(pick, xs[pl.ds(0, S), :]).astype(BF), Wc[t * D : (t + 1) * D, :])
        squeezed = term if squeezed is None else squeezed + term
        tick()
    newold[pl.ds(old.shape[0] - S // 3, S // 3), :] = squeezed.astype(BF)
    while len(clock) < len(plan["ticks"]):
        tick()
    while any(waiting.values()):
        go([name for name in waiting if waiting[name]])
    final = ngrad[...]
    width = norms.shape[1]
    mine = final[:, 0:width]
    for j in range(1, shards):
        mine = jnp.where(place.y == j, final[:, j * width : (j + 1) * width], mine)
    norm_total[...] = mine

    for copy in refill + [old_in]:
        copy.wait()
    for part in list(gathers.values()) + list(sums.values()):
        part.sent()
    for copy in norm_copies:
        copy.wait_send()


def wide_units(wu, wd, r, w):
    units = [(wu.at[:, pl.ds(c * w, w)], 0, c * w) for c in range(wu.shape[1] // w)]
    return units + [(wd.at[pl.ds(n, r), :], n, 0) for n in range(0, wd.shape[0], r)]


def unit_list(wqkv, wo, wu, wd):
    r, w = wo.shape
    return [(wqkv.at[:, pl.ds(c * w, w)], 0, 0) for c in range(3)] + [(wo, 0, 0)] + wide_units(wu, wd, r, w)


def unit_homes(work, r, count):
    homes = [(i, row) for i, rows in enumerate(work) for row in range(0, rows - r + 1, r)]
    assert len(homes) >= count
    return homes[:count]


def work_rows(S):
    big = -(-(REACH + S) // 256) * 256
    return (big, big, big, S, S, S)


def run_layer(sizes, tokens, memory, cmemory, docs, cotangent, wqkv, wo, wu, wd, wc, norms, moments, averages):
    streams, shards = sizes
    S, D = tokens.shape
    M = memory.shape[0]
    L = REACH + S
    W = REACH + 128
    FF = wu.shape[1]
    n_q = S // 128
    shapes = [(FF, D // 2)] * 2 + [(D, FF // 2)] * 2 + [(D, D)] + [(D, 3 * D // 2)] * 2
    shapes = [(shards, rows // shards, cols) for rows, cols in shapes]
    across, along = shard_bits(shards), stream_bits(streams)
    far = [along[i : i + 2] for i in range(2, len(along), 2)]
    axes = {"c": [(CORE,)], "y": [across], "x": [(NEAR,)], "yx": [across + (NEAR,)], "z": far}
    totals = []
    for i, name in enumerate(GRADS):
        way = WAYS[name].rstrip("+")
        order = [group for axis in ["c"] + way.split(".") for group in axes[axis]]
        totals.append(plan_total(sizes, FF if i < 2 else D, order, WAYS[name].endswith("+")))
    groups = [across + (NEAR, CORE)] + far
    used = [subsets(across), subsets((NEAR, CORE))] + [subsets(g) for g in groups]
    for stages, shares in totals:
        used += [subsets(stage[0]) for stage in stages] + [subsets(bits) for bits in shares]
    partners = sorted({tuple(sorted(delta)) for some in used for delta in some})
    sems = 9 * 4 * (shards - 1) + len(subsets(across)) + sum(len(subsets(g)) for g in groups)
    for stages, shares in totals:
        sems += sum(len(subsets(stage[0])) for stage in stages) + sum(len(subsets(bits)) for bits in shares)
    plan = {
        "totals": totals,
        "groups": groups,
        "partners": partners,
        "ticks": TICKS,
        "sems": sems,
        "local": 64,
        "work": work_rows(S),
        "split": True,
    }
    f32, bf = (lambda *s: pltpu.VMEM(s, F32)), (lambda *s: pltpu.VMEM(s, BF))
    scratch = [
        bf(L, D), bf(S, D), bf(L, D), bf(L, D), bf((HEADS // 2) * n_q, W, 256), bf(D, S), bf(S, FF), bf(S, FF),
        f32(HEADS // 2, 2, S), bf(D, D), bf(D, D), bf(D, D), bf(D, D), bf(D, FF), bf(FF, D), bf(3 * D, D),
        f32(shards, 8, norms.shape[1]), f32(8, D),
    ]
    scratch += [bf(*s) for s in shapes]
    for (stages, _), s in zip(totals, shapes):
        scratch += [bf(len(subsets(bits)), blocks, piece, s[2]) for bits, _b, _a, blocks, piece in stages]
    scratch += [f32(2 ** len(g), 8, D) for g in groups]
    scratch += [pltpu.SemaphoreType.DMA((sems,)), pltpu.SemaphoreType.DMA((sems,)), pltpu.SemaphoreType.DMA((64,))]
    anywhere = pl.BlockSpec(memory_space=pl.ANY)
    vmem = pl.BlockSpec(memory_space=pltpu.VMEM)
    units = 3 + 1
    out_shape = [bf(M + S, D), bf(S, D), bf(S, D), bf(*cmemory.shape), f32(8, norms.shape[1]), f32(units * wo.shape[0], D)]
    out_shape += [f32(rows, D) for rows in plan["work"]]
    out_shape += [bf(s[1], s[2]) for s in shapes]
    room = 253 * 256 * 1024 - sum(x.inner_aval.size * x.inner_aval.dtype.itemsize for x in out_shape)
    big = [pltpu.with_memory_space_constraint(x, pltpu.HBM) for x in (tokens, memory, cmemory)]
    more = [pltpu.with_memory_space_constraint(x, pltpu.HBM) for x in (cotangent, wqkv, wo, wu, wd, wc)]
    later = [pltpu.with_memory_space_constraint(x, pltpu.HBM) for x in (*moments, *averages)]
    return pl.pallas_call(
        functools.partial(layer_kernel, sizes, plan),
        out_shape=out_shape,
        in_specs=[anywhere] * 3 + [vmem] + [anywhere] * 6 + [vmem] + [anywhere] * 8,
        out_specs=[vmem] * len(out_shape),
        scratch_shapes=scratch,
        compiler_params=pltpu.CompilerParams(
            collective_id=0, has_side_effects=True, vmem_limit_bytes=room
        ),
        name="layer",
    )(*big, docs, *more, norms, *later)


def renew(grad, moment, average, master):
    momentum = MOMENTUM * moment + (1.0 - MOMENTUM) * grad
    updated = master - RATE * ((1.0 - MOMENTUM) * grad + MOMENTUM * momentum)
    smooth = SMOOTH * average + (1.0 - SMOOTH) * updated
    return momentum, smooth, updated


def update_kernel(
    wu, wd, xs, output, tgrad, newold, norm_grad, kept, dK, dV, seen_at, gl, gres, res, d0, d1, u0, u1, o, qa, qb, w_norm, v_norm, a_norm,
    *rest
):
    work = (dK, dV, seen_at, gl, gres, res)
    results, rest = [rest[n * 4 : n * 4 + 4] for n in range(4)], rest[16:]
    norm_out, lifted_out, rest = rest[:4], rest[4], rest[5:]
    out_to, memory_to, cmemory_to, tgrad_to, stage, late, sems = rest
    sem = iter(range(sems.shape[0]))
    copies = []

    def store(src, dst):
        copies.append(pltpu.make_async_copy(src, dst, sems.at[next(sem)]))
        copies[-1].start()

    r, D = o.shape
    late_in = []
    for n, (src, _r, _c) in enumerate(wide_units(wu, wd, r, D)):
        late_in.append(pltpu.make_async_copy(src, late.at[pl.ds(n * r, r), :], sems.at[next(sem)]))
        late_in[-1].start()
    g = norm_grad[0:4, :]
    norm_out[0][...] = g
    lifted_out[...] = g[2:4]
    for ref, value in zip(norm_out[1:], renew(g, v_norm[...], a_norm[...], w_norm[...])):
        ref[...] = value

    places = list(zip(*[[p[0] for p in unit_list(*arrays)] for arrays in results]))
    homes = unit_homes([ref.shape[0] for ref in work], r, 2 * len(places))
    half = D // 2

    def total(n):
        if n < 3:
            return jnp.concatenate([t[:, n * half : n * half + half] for t in (qa, qb)], axis=1)
        if n == 3:
            return o[...]
        n -= 4
        if n < 2 * u0.shape[1] // D:
            per = u0.shape[1] // D
            return (u0, u1)[n // per][:, n % per * D : n % per * D + D]
        n -= 2 * u0.shape[1] // D
        return jnp.concatenate([t[n * r : n * r + r, :] for t in (d0, d1)], axis=1)

    def old(n):
        where, row = homes[n]
        return work[where][pl.ds(row, r), :]

    here = kept.shape[0] // r
    for n in range(len(places)):
        if n >= here:
            late_in[n - here].wait()
        master = kept[pl.ds(n * r, r), :] if n < here else late[pl.ds((n - here) * r, r), :]
        grad = total(n).astype(F32)
        new = (grad,) + renew(grad, old(n), old(len(places) + n), master)
        for m, value in enumerate(new):
            if n >= RING:
                copies[(n - RING) * 4 + m].wait()
            slot = stage.at[n % RING * 4 + m]
            slot[...] = value
            store(slot, places[n][m])
    store(output, out_to)
    store(xs.at[pl.ds(xs.shape[0] - memory_to.shape[0], memory_to.shape[0]), :], memory_to)
    store(newold, cmemory_to)
    store(tgrad, tgrad_to)
    for copy in copies[max(0, len(places) - RING) * 4 :]:
        copy.wait()


def run_update(from_layer, masters, norm_old, memory):
    r, w = masters[1].shape
    units = sum(m.size for m in masters) // (r * w)
    anywhere = pl.BlockSpec(memory_space=pl.ANY)
    vmem = pl.BlockSpec(memory_space=pltpu.VMEM)
    same = [jax.ShapeDtypeStruct(m.shape, F32) for m in masters]
    small = jax.ShapeDtypeStruct(norm_old[0].shape, F32)
    lifted = jax.ShapeDtypeStruct((2, small.shape[1]), F32)
    bf = lambda x: jax.ShapeDtypeStruct(x.shape, BF)
    keep = [bf(from_layer[1]), bf(memory), bf(from_layer[3]), bf(from_layer[2])]
    held = [pltpu.with_memory_space_constraint(x, pltpu.VMEM) for x in from_layer]
    return pl.pallas_call(
        update_kernel,
        out_shape=same * 4 + [small] * 4 + [lifted] + keep,
        in_specs=[anywhere] * 2 + [vmem] * (len(held) + 3),
        out_specs=[anywhere] * 16 + [vmem] * 5 + [anywhere] * 4,
        scratch_shapes=[
            pltpu.VMEM((RING * 4, r, w), F32),
            pltpu.VMEM(((units - 4) * r, w), F32),
            pltpu.SemaphoreType.DMA((units * 5,)),
        ],
        compiler_params=pltpu.CompilerParams(vmem_limit_bytes=18 * 1024 * 1024),
        name="update",
    )(*[pltpu.with_memory_space_constraint(x, pltpu.HBM) for x in masters[2:]], *held, *[pltpu.with_memory_space_constraint(x, pltpu.HBM) for x in norm_old])


def on_device(
    sizes, tokens, memory, cmemory, doc_ids, cotangent,
    qkv_weight, out_weight, up_weight, down_weight, conv_weight, norm_params,
    qkv_moment, out_moment, up_moment, down_moment, norm_moment,
    qkv_average, out_average, up_average, down_average, norm_average,
):
    masters = (qkv_weight, out_weight, up_weight, down_weight)
    from_layer = run_layer(
        sizes, tokens[0], memory[0], cmemory[0], doc_ids, cotangent[0], *masters, conv_weight, norm_params.T,
        (qkv_moment, out_moment, up_moment, down_moment), (qkv_average, out_average, up_average, down_average),
    )
    new = run_update(from_layer, masters, (norm_params.T, norm_moment.T, norm_average.T), memory[0])
    grads, momenta, smooths, updates = new[0:4], new[4:8], new[8:12], new[12:16]
    norms = [x.T for x in new[16:20]]
    lifted = new[20].T
    out, new_memory, new_cmemory, token_grad = new[21:25]
    return (
        out[None], new_memory[None], new_cmemory[None], token_grad[None],
        *grads, norms[0], *momenta, norms[1], *smooths, norms[2], *updates, norms[3], lifted,
    )


def solution(mesh):
    sizes = (mesh.shape["stream"], mesh.shape["shard"])
    both = ("stream", "shard")
    wide = P(both, None, None)
    rows = P("shard", None)
    return jax.shard_map(
        functools.partial(on_device, sizes),
        mesh=mesh,
        in_specs=(wide, wide, wide, P(both, None), wide) + (rows,) * 16,
        out_specs=(wide,) * 4 + (rows,) * 21,
        check_vma=False,
    )
```

```python
import functools

import jax
import jax.numpy as jnp
from jax import lax
from jax.experimental import pallas as pl
from jax.experimental.pallas import tpu as pltpu
from jax.sharding import PartitionSpec as P

HEADS = 8
MOMENTUM = 0.9
RATE = 0.0025
SMOOTH = 0.8
REACH = 448
BF = jnp.bfloat16
F32 = jnp.float32
MESH = pl.DeviceIdType.MESH
GELU_C = 0.7978845608028654
GELU_A = 0.044715


def nn(a, b):
    return lax.dot_general(a, b, (((1,), (0,)), ((), ())), preferred_element_type=F32)


def nt(a, b):
    return lax.dot_general(a, b, (((1,), (1,)), ((), ())), preferred_element_type=F32)


def tn(a, b):
    return lax.dot_general(a, b, (((0,), (0,)), ((), ())), preferred_element_type=F32)


def normalised(x):
    center = x - jnp.mean(x, axis=-1, keepdims=True)
    scale = lax.rsqrt(jnp.mean(center * center, axis=-1, keepdims=True) + 1e-5)
    return center * scale, scale


def norm_back(grad, unit, scale, gain):
    inner = grad * gain
    first = jnp.mean(inner, axis=-1, keepdims=True)
    second = jnp.mean(inner * unit, axis=-1, keepdims=True)
    return (inner - first - unit * second) * scale


def two_heads(block):
    lane = lax.broadcasted_iota(jnp.int32, block.shape, 1)
    zero = jnp.zeros_like(block)
    low = lane < 64
    return jnp.concatenate([jnp.where(low, block, zero), jnp.where(low, zero, block)], axis=0)


def own_halves(block):
    return jnp.concatenate([block[0:64, 0:128], block[64:128, 128:256]], axis=0)


def rows_at(start, count, by=16):
    return pl.ds(pl.multiple_of(start, by), count)


class Sems:
    def __init__(self, ref, size):
        self.ref, self.size, self.used = ref, size, 0

    def take(self):
        self.used += 1
        assert self.used <= self.size
        return self.ref.at[self.used - 1]


def subsets(bits):
    found = [()]
    for bit in bits:
        found += [f + (bit,) for f in found]
    return found[1:]


class Place:
    def __init__(self, streams, shards):
        self.streams, self.shards = streams, shards
        self.s = lax.axis_index("stream")
        self.y = lax.axis_index("shard")

    def value(self, axis, bit, flipped=False):
        v = ((self.s if axis == "stream" else self.y) // bit) % 2
        return 1 - v if flipped else v

    def flip(self, bits):
        s, y = self.s, self.y
        for axis, bit in bits:
            step = bit * (1 - 2 * self.value(axis, bit))
            if axis == "stream":
                s = s + step
            else:
                y = y + step
        return s, y

    def index(self, bits, flipped=()):
        total = 0
        for axis, bit in bits:
            total = total * 2 + self.value(axis, bit, (axis, bit) in flipped)
        return total


def remote(src, dst, sems, who):
    copy = pltpu.make_async_remote_copy(
        src_ref=src, dst_ref=dst, send_sem=sems[0], recv_sem=sems[1], device_id=who, device_id_type=MESH
    )
    copy.start()
    return copy


CORE, NEAR = ("stream", 1), ("stream", 2)


class Gather:
    def __init__(self, place, buf, take, split, piece=(0, 1), cols=None):
        self.p, self.buf, self.take = place, buf, take
        self.block = buf.shape[0] // place.shards
        self.rows = self.block // piece[1]
        self.first_row = piece[0] * self.rows
        self.cols = cols or pl.ds(0, buf.shape[1])
        self.split = split
        self.parts = (NEAR, CORE) if split else (CORE,)
        self.count = self.rows // 2 ** len(self.parts)
        self.deltas = subsets(shard_bits(place.shards))
        self.part = place.index(self.parts)
        self.first, self.second, self.third = [], [], []

    def view(self, owner, part):
        start = owner * self.block + self.first_row + part * self.count
        return self.buf.at[rows_at(start, self.count), self.cols]

    def start(self):
        for delta in self.deltas:
            v = self.view(self.p.y, self.part)
            self.first.append(remote(v, v, self.take(), self.p.flip(delta)))

    def spread(self):
        for n, delta in enumerate(self.deltas):
            self.first[n].wait_recv()
            v = self.view(self.p.flip(delta)[1], self.part)
            if self.split:
                self.second.append(remote(v, v, self.take(), self.p.flip((NEAR,))))
            self.third.append(remote(v, v, self.take(), self.p.flip((CORE,))))

    def pass_on(self):
        if self.split:
            for n, delta in enumerate(self.deltas):
                self.second[n].wait_recv()
                v = self.view(self.p.flip(delta)[1], self.p.index(self.parts, (NEAR,)))
                self.third.append(remote(v, v, self.take(), self.p.flip((CORE,))))

    def finish(self):
        for copy in self.third:
            copy.wait_recv()

    def sent(self):
        for copy in self.first + self.second + self.third:
            copy.wait_send()


def shard_bits(shards):
    bits, bit = [], shards // 2
    while bit >= 1:
        bits.append(("shard", bit))
        bit //= 2
    return tuple(bits)


def stream_bits(streams):
    bits, bit = [], 1
    while bit < streams:
        bits.append(("stream", bit))
        bit *= 2
    return tuple(bits)


def plan_total(sizes, rows, order, merge=False):
    shards = sizes[1]
    count, full, stages, shares = rows // shards, True, [], []
    for group in order:
        across = tuple(b for b in group if b[0] == "shard")
        along = tuple(b for b in group if b[0] == "stream")
        if along and count % (16 * 2 ** len(along)):
            groups = ([(across, ())] if across else []) + [((), (b,)) for b in along]
        else:
            groups = [(across, along)]
        for across, along in groups:
            scatter = count % (16 * 2 ** len(along)) == 0
            if scatter:
                count //= 2 ** len(along)
            full = full and not across
            stages.append((across + along, along if scatter else (), bool(across), shards if full else 1, count))
            if scatter and along:
                shares.insert(0, along)
    if merge and len(shares) > 2:
        shares = [tuple(b for group in shares[-2::-1] for b in group), shares[-1]]
    return stages, shares


class Total:
    def __init__(self, place, grad, total, slots, take, plan):
        self.p, self.grad, self.total, self.take = place, grad, total, take
        self.slots = slots
        self.stages, self.shares = plan
        self.rows = grad.shape[1]
        self.off, self.count, self.full = 0, self.rows, True
        self.live, self.done = [], []
        self.at = 0

    def begin(self):
        bits, along, across, blocks, piece = self.stages[self.at]
        slot = self.slots[self.at]
        self.live = []
        for n, delta in enumerate(subsets(bits)):
            s, y = who = self.p.flip(delta)
            rows = rows_at(self.off + self.p.index(along, delta) * piece, piece)
            if across:
                src = self.grad.at[pl.ds(y, 1), rows, :]
            elif self.full:
                src = self.grad.at[:, rows, :]
            else:
                src = self.grad.at[pl.ds(self.p.y, 1), rows, :]
            self.live.append(remote(src, slot.at[n], self.take(), who))
        self.off = self.off + self.p.index(along) * piece
        self.count = piece
        self.full = self.full and not across

    def add(self, last):
        slot = self.slots[self.at]
        rows = rows_at(self.off, self.count)
        here = slice(None) if self.full else pl.ds(self.p.y, 1)
        value = self.grad[here, rows, :].astype(F32)
        for n, copy in enumerate(self.live):
            copy.wait_recv()
            value = value + slot[n].astype(F32)
        if last:
            self.total[rows, :] = value[0].astype(BF)
        else:
            self.grad[here, rows, :] = value.astype(BF)
        self.done += self.live
        self.at += 1

    def share(self, bits):
        v = self.total.at[rows_at(self.off, self.count), :]
        self.live = [remote(v, v, self.take(), self.p.flip(delta)) for delta in subsets(bits)]
        self.off = self.off - self.p.index(bits) * self.count
        self.count *= 2 ** len(bits)

    def arrive(self):
        for copy in self.live:
            copy.wait_recv()
        self.done += self.live

    def steps(self):
        def middle():
            self.add(False)
            self.begin()

        def turn():
            self.add(True)
            self.share(self.shares[0])

        def later(bits):
            self.arrive()
            self.share(bits)

        out = [self.begin] + [middle] * (len(self.stages) - 1) + [turn]
        return out + [functools.partial(later, bits) for bits in self.shares[1:]] + [self.arrive]

    def sent(self):
        for copy in self.done:
            copy.wait_send()


class Everywhere:
    def __init__(self, place, table, slots, take, groups):
        self.p, self.table, self.slots, self.take, self.groups = place, table, slots, take, groups
        self.live, self.done, self.at = [], [], 0

    def begin(self):
        group, slot = self.groups[self.at], self.slots[self.at]
        mine = pl.ds(self.p.index(group), 1)
        slot[mine] = self.table[...][None]
        self.live = [remote(slot.at[mine], slot.at[mine], self.take(), self.p.flip(d)) for d in subsets(group)]

    def add(self):
        for copy in self.live:
            copy.wait_recv()
        self.done += self.live
        slot = self.slots[self.at]
        total = slot[0]
        for n in range(1, slot.shape[0]):
            total = total + slot[n]
        self.table[...] = total
        self.at += 1

    def steps(self):
        def middle():
            self.add()
            self.begin()

        return [self.begin] + [middle] * (len(self.groups) - 1) + [self.add]

    def sent(self):
        for copy in self.done:
            copy.wait_send()


GRADS = ("d0", "d1", "u0", "u1", "o", "qa", "qb")
WAYS = {"d0": "yx.z", "d1": "z.y.x", "u0": "x.z.y", "u1": "y.x.z", "o": "yx.z", "qa": "yx.z", "qb": "yx.z+"}
RING = 4
TICKS = (
    ("d0",),
    ("d1",),
    ("u0", "d0", "d1"),
    ("u0", "u1"),
    (),
    ("u1",),
    (),
    (),
    (),
    ("o",),
    (),
    ("o", "d0"),
    (),
    (),
    (),
    (),
    (),
    ("u0", "qa", "u1"),
    (),
    ("qa", "d1"),
    ("o",),
    (),
    ("d0",),
    ("u1",),
    ("qb",),
    (),
    ("qb",),
    (),
    (),
    ("u0", "qa", "d1"),
    (),
    ("n", "o"),
    (),
    (),
    (),
    ("n", "d0"),
    (),
    ("qb",),
    ("u0",),
    ("d1",),
    ("u1",),
    ("n",),
    ("qa",),
    ("d0",),
    ("o",),
    ("d1",),
    ("d0",),
    ("qb",),
    ("o",),
    ("u0",),
    ("o",),
    ("u1",),
    ("qa",),
    ("u0",),
    ("u0",),
    ("u1",),
    ("u1",),
    ("qa",),
    ("d1",),
    ("qa",),
    ("d1",),
    ("qb",),
    ("qb",),
)


def layer_kernel(
    sizes, plan, tok, mem, old, docs, cot, wqkv, wo, wu, wd, wc, norms, *rest
):
    moments, averages, rest = rest[:4], rest[4:8], rest[8:]
    xs, ct, lifted, newold, norm_total, kept, dK, dV, seen_at, gl, gres, res, *rest = rest
    tbuf, rest = rest[:7], rest[7:]
    (N, Q, K, V, PT, OT, act, gh, Dv, Wq, Wk, Wv, Wo, Wu, Wd, Wc, nblocks, ngrad, *rest) = rest
    gbuf, rest = rest[:7], rest[7:]
    gr, dO = gh.at[:, pl.ds(0, Wo.shape[1])], gh.at[:, pl.ds(Wo.shape[1], Wo.shape[1])]
    slots = []
    for stages, _ in plan["totals"]:
        slots.append(rest[: len(stages)])
        rest = rest[len(stages) :]
    nslots, rest = rest[: len(plan["groups"])], rest[len(plan["groups"]) :]
    send_ref, recv_ref, local_ref = rest
    place = Place(*sizes)
    send, recv, local = Sems(send_ref, plan["sems"]), Sems(recv_ref, plan["sems"]), Sems(local_ref, plan["local"])

    def pair():
        return send.take(), recv.take()

    shards = place.shards
    S, D = tok.shape
    M = mem.shape[0]
    H0 = M - REACH
    L = REACH + S
    T0 = REACH
    W = REACH + 128
    FF = Wu.shape[1]
    n_q = S // 128

    barrier = pltpu.get_barrier_semaphore()
    for bits in plan["partners"]:
        pl.semaphore_signal(barrier, inc=1, device_id=place.flip(bits), device_id_type=MESH)

    def fetch(src, dst):
        copy = pltpu.make_async_copy(src, dst, local.take())
        copy.start()
        return copy

    jobs = {}

    def bring(name, pieces, target, unit, ref):
        for n, (src, row, col) in enumerate(pieces):
            stage = ref.at[pl.ds((unit + n) * r1, r1), :]
            jobs.setdefault(name, []).append((fetch(src, stage), stage, target, row, col))

    r1 = wqkv.shape[0]
    pieces = unit_list(wqkv, wo, wu, wd)
    bring("k", [(pieces[1][0], 0, 0)], Wk, 1, kept)
    bring("v", [(pieces[2][0], 0, 0)], Wv, 2, kept)
    bring("q", pieces[0:1], Wq, 0, kept)
    tok_in = fetch(tok, xs.at[pl.ds(M, S), :])
    mem_in = fetch(mem, xs.at[pl.ds(0, M), :])
    bring("o", pieces[3:4], Wo, 3, kept)
    bring("u", pieces[4 : 4 + FF // D], Wu, 0, dV)
    bring("d", pieces[4 + FF // D :], Wd, 0, dK)
    stage = gl.at[pl.ds(0, wc.shape[0]), :]
    jobs["c"] = [(fetch(wc, stage), stage, Wc, 0, 0)]
    cot_in = fetch(cot, ct)
    old_in = fetch(old.at[pl.ds(S // 3, old.shape[0] - S // 3), :], newold.at[pl.ds(0, old.shape[0] - S // 3), :])

    nblocks[pl.ds(place.y, 1)] = jnp.concatenate(
        [norms[...].astype(BF).astype(F32), jnp.zeros((4, norms.shape[1]), F32)], axis=0
    )[None]

    def cast(name):
        for copy, stage, target, row, col in jobs[name]:
            copy.wait()
            here = rows_at(place.y * (target.shape[0] // shards) + row, stage.shape[0])
            target[here, pl.ds(col, 512)] = stage[...].astype(BF)

    cast("k")
    pl.semaphore_wait(barrier, len(plan["partners"]))
    own = nblocks.at[pl.ds(place.y, 1)]
    norm_copies = [remote(own, own, pair(), place.flip(delta)) for delta in subsets(shard_bits(shards))]
    gathers = {}

    def launch(name, buf, **piece):
        gathers[name] = Gather(place, buf, pair, plan["split"], **piece)
        gathers[name].start()

    launch("k", Wk)
    cast("v")
    launch("v", Wv)
    cast("q")
    launch("q", Wq)
    cast("o")
    launch("o", Wo)

    ids = docs[...].astype(F32)
    column = jnp.transpose(jnp.broadcast_to(ids, (8, ids.shape[1])))
    base = ids.shape[1] - L

    def see(b):
        key = column[base + 128 * b : base + 128 * b + W, 0:1]
        query = ids[:, base + T0 + 128 * b : base + T0 + 128 * b + 128]
        k = lax.broadcasted_iota(jnp.int32, (W, 128), 0)
        q = lax.broadcasted_iota(jnp.int32, (W, 128), 1) + T0
        seen_at[pl.ds(b // 4 * W, W), pl.ds(b % 4 * 128, 128)] = jnp.where((key == query) & (k <= q), 0.0, -1e30)

    for b in range(n_q):
        see(b)
    cast("u")
    for n in range(2):
        launch("u" + str(n), Wu, cols=pl.ds(n * FF // 2, FF // 2))
    for copy in norm_copies:
        copy.wait_recv()
    table = jnp.concatenate([nblocks[j] for j in range(shards)], axis=1)
    g1, b1, g2, b2 = table[0:1], table[1:2], table[2:3], table[3:4]

    tok_in.wait()
    mem_in.wait()

    def ln1(n):
        r = slice(n * L // 4, (n + 1) * L // 4)
        unit, _s = normalised(xs[H0 + r.start : H0 + r.stop, :].astype(F32))
        N[r, :] = (unit * g1 + b1).astype(BF)

    ln1(0)
    ln1(1)
    gathers["k"].spread()
    cast("d")
    for n in range(2):
        launch("d" + str(n), Wd, piece=(n, 2))
    gathers["v"].spread()
    ln1(2)
    ln1(3)
    gathers["q"].spread()
    cast("c")
    launch("c", Wc)
    gathers["k"].pass_on()
    gathers["o"].spread()
    gathers["v"].pass_on()
    gathers["k"].finish()
    for c in range(2):
        cs = slice(c * 256, c * 256 + 256)
        for r in (slice(0, L // 2), slice(L // 2, L)):
            K[r, cs] = nn(N[r, :], Wk[:, cs]).astype(BF)
    gathers["q"].pass_on()
    gathers["v"].finish()
    for c in range(2):
        cs = slice(c * 256, c * 256 + 256)
        for r in (slice(0, L // 2), slice(L // 2, L)):
            V[r, cs] = nn(N[r, :], Wv[:, cs]).astype(BF)
    gathers["o"].pass_on()
    gathers["q"].finish()
    for c in range(2):
        cs = slice(c * 256, c * 256 + 256)
        Q[:, cs] = (nn(N[T0:, :], Wq[:, cs]).astype(BF).astype(F32) * 0.125).astype(BF)

    def scores(i, u, slot):
        qb, p = i // 2, (i % 2) * 2 + u
        q0, l0 = rows_at(qb * 128, 128, 128), rows_at(p * 128, 128, 128)
        s = nt(K[rows_at(qb * 128, W, 128), l0], two_heads(Q[q0, l0]))
        seen = seen_at[rows_at(qb // 4 * W, W), rows_at(qb % 4 * 128, 128, 128)]
        raw[slot][0:W, u * 256 : u * 256 + 256] = s + jnp.concatenate([seen, seen], axis=1)

    def attend(i, u, slot):
        qb, p = i // 2, (i % 2) * 2 + u
        q0, l0 = rows_at(qb * 128, 128, 128), rows_at(p * 128, 128, 128)
        cs = slice(u * 256, u * 256 + 256)
        pieces = [slice(c, c + 64) for c in range(0, W, 64)]
        top, total = None, None
        for r in pieces:
            part = jnp.max(raw[slot][r, cs].reshape(8, 8, 256), axis=0)
            top = part if top is None else jnp.maximum(top, part)
        top = jnp.max(top, axis=0, keepdims=True)
        for r in pieces:
            e = jnp.exp(raw[slot][r, cs] - top)
            raw[slot][r, cs] = e
            part = jnp.sum(e.reshape(8, 8, 256), axis=0)
            total = part if total is None else total + part
        scale = 1.0 / jnp.sum(total, axis=0, keepdims=True)
        for r in pieces:
            PT[p * n_q + qb, r, :] = (raw[slot][r, cs] * scale).astype(BF)
        OT[l0, q0] = own_halves(tn(V[rows_at(qb * 128, W, 128), l0], PT[p * n_q + qb])).astype(BF)

    def attend_two(j, _):
        for slot in range(2):
            for u in range(2):
                scores(jnp.minimum(2 * j + slot + 1, 2 * n_q - 1), u, 1 - slot)
            for u in range(2):
                attend(2 * j + slot, u, slot)
        return 0

    raw = (gl, gres)
    for u in range(2):
        scores(0, u, 0)
    gathers["u0"].spread()
    lax.fori_loop(0, 2, attend_two, 0)
    gathers["u1"].spread()
    lax.fori_loop(2, 4, attend_two, 0)
    gathers["d0"].spread()
    gathers["u0"].pass_on()
    lax.fori_loop(4, n_q, attend_two, 0)
    gathers["d1"].spread()
    gathers["u1"].pass_on()
    gathers["o"].finish()

    for c in range(2):
        cs = slice(c * 256, c * 256 + 256)
        res[:, cs] = xs[M:, cs].astype(F32) + tn(OT[...], Wo[:, cs])

    for n in range(3):
        r = slice(n * S // 3, (n + 1) * S // 3)
        unit, _s = normalised(res[r, :])
        lifted[r, :] = (unit * g2 + b2).astype(BF)
    gathers["d0"].pass_on()
    cot_in.wait()
    gathers["u0"].finish()
    gathers["u1"].finish()

    tiles = FF // 256

    def tile_at(i):
        return rows_at((i + place.y * (tiles // shards)) % tiles * 256, 256, 256)

    def ffn_in(i, slot):
        here = slice(slot * 256, slot * 256 + 256)
        dK[0:S, here] = nn(lifted[...], Wu[:, tile_at(i)])
        dV[0:S, here] = nt(ct[...], Wd[tile_at(i), :])

    def ffn_out(i, slot):
        here = slice(slot * 256, slot * 256 + 256)
        for n in range(0, S, 128):
            r = slice(n, n + 128)
            h, ga = dK[r, here], dV[r, here]
            h2 = h * h
            hp = 0.5 + 0.5 * jnp.tanh(h * (GELU_C + (GELU_C * GELU_A) * h2))
            a = h * hp
            slope = hp + (a - a * hp) * (2.0 * GELU_C + (6.0 * GELU_C * GELU_A) * h2)
            act[r, tile_at(i)] = a.astype(BF)
            gh[r, tile_at(i)] = (ga * slope).astype(BF)

    def put(ref, start, value):
        rows = value.shape[0]
        if rows > ref.shape[1]:
            n = rows // ref.shape[1]
            ref[pl.ds(start // ref.shape[1], n)] = value.astype(BF).reshape(n, ref.shape[1], value.shape[1])
        else:
            ref[start // ref.shape[1], rows_at(start % ref.shape[1], rows), :] = value.astype(BF)

    def put_all(ref, cols, value):
        ref[:, :, cols] = value.astype(BF).reshape(ref.shape[0], ref.shape[1], value.shape[1])

    def grad_down(ref, col, low, high):
        def body(i, _):
            first = (2 * i + place.y * (tiles // shards)) % tiles
            put(ref, first * 256, tn(act[:, rows_at(first * 256, 512, 256)], ct[:, col : col + 256]))
            return 0

        lax.fori_loop(low // 2, high // 2, body, 0)

    own_tiles = tiles // shards
    early = own_tiles if own_tiles % 2 == 0 else 0
    ffn_in(0, 0)
    for i in range(tiles):
        if i + 1 == own_tiles:
            ffn_out(i, i % 2)
            for n in range(2):
                grad_down(gbuf[n], n * D // 2, 0, early)
            gathers["d1"].pass_on()
            gathers["d0"].finish()
            gathers["d1"].finish()
            ffn_in(i + 1, (i + 1) % 2)
            continue
        if i + 1 < tiles:
            ffn_in(i + 1, (i + 1) % 2)
        ffn_out(i, i % 2)
    gathers["c"].spread()

    homes = unit_homes(plan["work"], r1, 2 * len(pieces))
    old_units = [p[0] for p in unit_list(*moments)] + [p[0] for p in unit_list(*averages)]
    work = (dK, dV, seen_at, gl, gres, res)
    refill = []

    def bring_old(index):
        for src, (where, row) in zip(old_units, homes):
            if where == index:
                refill.append(fetch(src, work[index].at[pl.ds(row, r1), :]))

    sums = {
        name: Total(place, gbuf[i], tbuf[i], slots[i], pair, plan["totals"][i]) for i, name in enumerate(GRADS)
    }
    sums["n"] = Everywhere(place, ngrad, nslots, pair, plan["groups"])
    waiting = {name: sums[name].steps() for name in sums}
    clock = []

    def go(names):
        for name in names:
            if not waiting[name]:
                continue
            waiting[name].pop(0)()

    def tick():
        if len(clock) < len(plan["ticks"]):
            go(plan["ticks"][len(clock)])
        clock.append(0)

    for n in range(2):
        grad_down(gbuf[n], n * D // 2, early, tiles)
        tick()
    for n in range(2):
        for c in range(2):
            piece = gh[:, n * 1024 + c * 512 : n * 1024 + c * 512 + 512]
            put_all(gbuf[2 + n], slice(c * 512, c * 512 + 512), tn(lifted[...], piece))
        tick()
    for c in range(2):
        cs = slice(c * 256, c * 256 + 256)
        gl[:, cs] = nt(gh[...], Wu[cs, :])
        tick()

    def by_eight(x):
        return jnp.sum(x.reshape(x.shape[0] // 8, 8, D), axis=0)

    second = [jnp.zeros((8, D), F32)] * 2
    for n in range(3):
        r = slice(n * S // 3, (n + 1) * S // 3)
        unit, scale = normalised(res[r, :])
        gy = gl[r, :]
        x = ct[r, :].astype(F32) + norm_back(gy, unit, scale, g2)
        gres[r, :] = x
        gr[r, :] = x.astype(BF)
        second = [second[0] + by_eight(gy * unit), second[1] + by_eight(gy)]
        tick()
    put_all(gbuf[4], slice(0, D), nn(OT[...], gr[...]))
    tick()
    for c in range(2):
        cs = slice(c * 256, c * 256 + 256)
        dO[:, cs] = nt(gr[...], Wo[cs, :]).astype(BF)
    for c in range(2):
        cs = slice(c * 256, c * 256 + 256)
        dt = nt(Wo[cs, :], gr[...]).astype(BF).astype(F32) * OT[cs, :].astype(F32)
        for h in range(4):
            Dv[c * 2 + h // 2, h % 2 : h % 2 + 1, :] = jnp.sum(dt[h * 64 : h * 64 + 64], axis=0, keepdims=True)
    dK[...] = jnp.zeros_like(dK)
    dV[...] = jnp.zeros_like(dV)
    tick()

    def back_in(i, u, slot):
        qb, p = i % n_q, i // n_q * 2 + u
        q0, l0 = slice(qb * 128, qb * 128 + 128), slice(p * 128, p * 128 + 128)
        raw[slot][0:W, u * 256 : u * 256 + 256] = nt(V[qb * 128 : qb * 128 + W, l0], two_heads(dO[q0, l0]))

    def back_out(i, u, slot):
        qb, p = i % n_q, i // n_q * 2 + u
        q0, l0, keys = slice(qb * 128, qb * 128 + 128), slice(p * 128, p * 128 + 128), slice(qb * 128, qb * 128 + W)
        mean = jnp.concatenate([Dv[p, 0:1, q0], Dv[p, 1:2, q0]], axis=1)
        probs = PT[p * n_q + qb]
        ds = (probs.astype(F32) * (raw[slot][0:W, u * 256 : u * 256 + 256] - mean)).astype(BF)
        dV[keys, l0] += nn(probs, two_heads(dO[q0, l0]))
        dK[keys, l0] += nn(ds, two_heads(Q[q0, l0]))
        dq = own_halves(tn(K[keys, l0], ds)) * 0.125
        Q[q0, l0] = jnp.transpose(dq).astype(BF)

    raw = (gl, seen_at)
    for u in range(2):
        back_in(0, u, 0)
    for i in range(2 * n_q):
        if i + 1 < 2 * n_q:
            for u in range(2):
                back_in(i + 1, u, (i + 1) % 2)
        for u in range(2):
            back_out(i, u, i % 2)
        tick()
        if i % n_q == n_q - 1:
            quad = i // n_q
            cs = slice(quad * 256, quad * 256 + 256)
            K[:, cs] = dK[0:L, cs].astype(BF)
            V[:, cs] = dV[0:L, cs].astype(BF)
            g = gbuf[5 + quad]
            put_all(g, slice(0, 256), tn(N[T0:, :], Q[:, cs]))
            put_all(g, slice(256, 512), tn(N[...], K[:, cs]))
            put_all(g, slice(512, 768), tn(N[...], V[:, cs]))
            tick()

    for index in range(1, 4):
        bring_old(index)
    for c in range(2):
        cs = slice(c * 256, c * 256 + 256)
        for r in (slice(0, L // 2), slice(L // 2, L)):
            dK[r, cs] = nt(K[r, :], Wk[cs, :])
            dK[r, cs] += nt(V[r, :], Wv[cs, :])
        dK[T0:L, cs] += nt(Q[...], Wq[cs, :])
        tick()

    first = [jnp.zeros((8, D), F32)] * 2
    for low, high in [(0, T0 // 2), (T0 // 2, T0)] + [(T0 + n * S // 3, T0 + (n + 1) * S // 3) for n in range(3)]:
        unit, scale = normalised(xs[H0 + low : H0 + high, :].astype(F32))
        gy = dK[low:high, :]
        if low >= T0:
            r = slice(low - T0, high - T0)
            lifted[r, :] = (gres[r, :] + norm_back(gy, unit, scale, g1)).astype(BF)
        first = [first[0] + by_eight(gy * unit), first[1] + by_eight(gy)]
        if high == L:
            rows = [jnp.sum(x, axis=0, keepdims=True) for x in first + second]
            ngrad[...] = jnp.concatenate(rows + [jnp.zeros((4, D), F32)], axis=0)
        tick()
    bring_old(0)
    bring_old(4)

    for c in range(2):
        cs = slice(c * 256, c * 256 + 256)
        ct[:, cs] = (res[:, cs] + nn(act[...], Wd[:, cs])).astype(BF)
        tick()
    bring_old(5)
    gathers["c"].pass_on()
    gathers["c"].finish()
    squeezed = None
    for t in range(3):
        row = lax.broadcasted_iota(jnp.int32, (S // 3, S), 0) * 3 + t
        pick = jnp.where(lax.broadcasted_iota(jnp.int32, (S // 3, S), 1) == row, 1.0, 0.0).astype(BF)
        term = nn(nn(pick, xs[pl.ds(0, S), :]).astype(BF), Wc[t * D : (t + 1) * D, :])
        squeezed = term if squeezed is None else squeezed + term
        tick()
    newold[pl.ds(old.shape[0] - S // 3, S // 3), :] = squeezed.astype(BF)
    while len(clock) < len(plan["ticks"]):
        tick()
    while any(waiting.values()):
        go([name for name in waiting if waiting[name]])
    final = ngrad[...]
    width = norms.shape[1]
    mine = final[:, 0:width]
    for j in range(1, shards):
        mine = jnp.where(place.y == j, final[:, j * width : (j + 1) * width], mine)
    norm_total[...] = mine

    for copy in refill + [old_in]:
        copy.wait()
    for part in list(gathers.values()) + list(sums.values()):
        part.sent()
    for copy in norm_copies:
        copy.wait_send()


def wide_units(wu, wd, r, w):
    units = [(wu.at[:, pl.ds(c * w, w)], 0, c * w) for c in range(wu.shape[1] // w)]
    return units + [(wd.at[pl.ds(n, r), :], n, 0) for n in range(0, wd.shape[0], r)]


def unit_list(wqkv, wo, wu, wd):
    r, w = wo.shape
    return [(wqkv.at[:, pl.ds(c * w, w)], 0, 0) for c in range(3)] + [(wo, 0, 0)] + wide_units(wu, wd, r, w)


def unit_homes(work, r, count):
    homes = [(i, row) for i, rows in enumerate(work) for row in range(0, rows - r + 1, r)]
    assert len(homes) >= count
    return homes[:count]


def work_rows(S):
    big = -(-(REACH + S) // 256) * 256
    return (big, big, big, S, S, S)


def run_layer(sizes, tokens, memory, cmemory, docs, cotangent, wqkv, wo, wu, wd, wc, norms, moments, averages):
    streams, shards = sizes
    S, D = tokens.shape
    M = memory.shape[0]
    L = REACH + S
    W = REACH + 128
    FF = wu.shape[1]
    n_q = S // 128
    shapes = [(FF, D // 2)] * 2 + [(D, FF // 2)] * 2 + [(D, D)] + [(D, 3 * D // 2)] * 2
    shapes = [(shards, rows // shards, cols) for rows, cols in shapes]
    across, along = shard_bits(shards), stream_bits(streams)
    far = [along[i : i + 2] for i in range(2, len(along), 2)]
    axes = {"c": [(CORE,)], "y": [across], "x": [(NEAR,)], "yx": [across + (NEAR,)], "z": far}
    totals = []
    for i, name in enumerate(GRADS):
        way = WAYS[name].rstrip("+")
        order = [group for axis in ["c"] + way.split(".") for group in axes[axis]]
        totals.append(plan_total(sizes, FF if i < 2 else D, order, WAYS[name].endswith("+")))
    groups = [across + (NEAR, CORE)] + far
    used = [subsets(across), subsets((NEAR, CORE))] + [subsets(g) for g in groups]
    for stages, shares in totals:
        used += [subsets(stage[0]) for stage in stages] + [subsets(bits) for bits in shares]
    partners = sorted({tuple(sorted(delta)) for some in used for delta in some})
    sems = 9 * 4 * (shards - 1) + len(subsets(across)) + sum(len(subsets(g)) for g in groups)
    for stages, shares in totals:
        sems += sum(len(subsets(stage[0])) for stage in stages) + sum(len(subsets(bits)) for bits in shares)
    plan = {
        "totals": totals,
        "groups": groups,
        "partners": partners,
        "ticks": TICKS,
        "sems": sems,
        "local": 64,
        "work": work_rows(S),
        "split": True,
    }
    f32, bf = (lambda *s: pltpu.VMEM(s, F32)), (lambda *s: pltpu.VMEM(s, BF))
    scratch = [
        bf(L, D), bf(S, D), bf(L, D), bf(L, D), bf((HEADS // 2) * n_q, W, 256), bf(D, S), bf(S, FF), bf(S, FF),
        f32(HEADS // 2, 2, S), bf(D, D), bf(D, D), bf(D, D), bf(D, D), bf(D, FF), bf(FF, D), bf(3 * D, D),
        f32(shards, 8, norms.shape[1]), f32(8, D),
    ]
    scratch += [bf(*s) for s in shapes]
    for (stages, _), s in zip(totals, shapes):
        scratch += [bf(len(subsets(bits)), blocks, piece, s[2]) for bits, _b, _a, blocks, piece in stages]
    scratch += [f32(2 ** len(g), 8, D) for g in groups]
    scratch += [pltpu.SemaphoreType.DMA((sems,)), pltpu.SemaphoreType.DMA((sems,)), pltpu.SemaphoreType.DMA((64,))]
    anywhere = pl.BlockSpec(memory_space=pl.ANY)
    vmem = pl.BlockSpec(memory_space=pltpu.VMEM)
    units = 3 + 1
    out_shape = [bf(M + S, D), bf(S, D), bf(S, D), bf(*cmemory.shape), f32(8, norms.shape[1]), f32(units * wo.shape[0], D)]
    out_shape += [f32(rows, D) for rows in plan["work"]]
    out_shape += [bf(s[1], s[2]) for s in shapes]
    room = 253 * 256 * 1024 - sum(x.inner_aval.size * x.inner_aval.dtype.itemsize for x in out_shape)
    big = [pltpu.with_memory_space_constraint(x, pltpu.HBM) for x in (tokens, memory, cmemory)]
    more = [pltpu.with_memory_space_constraint(x, pltpu.HBM) for x in (cotangent, wqkv, wo, wu, wd, wc)]
    later = [pltpu.with_memory_space_constraint(x, pltpu.HBM) for x in (*moments, *averages)]
    return pl.pallas_call(
        functools.partial(layer_kernel, sizes, plan),
        out_shape=out_shape,
        in_specs=[anywhere] * 3 + [vmem] + [anywhere] * 6 + [vmem] + [anywhere] * 8,
        out_specs=[vmem] * len(out_shape),
        scratch_shapes=scratch,
        compiler_params=pltpu.CompilerParams(
            collective_id=0, has_side_effects=True, vmem_limit_bytes=room
        ),
        name="layer",
    )(*big, docs, *more, norms, *later)


def renew(grad, moment, average, master):
    momentum = MOMENTUM * moment + (1.0 - MOMENTUM) * grad
    updated = master - RATE * ((1.0 - MOMENTUM) * grad + MOMENTUM * momentum)
    smooth = SMOOTH * average + (1.0 - SMOOTH) * updated
    return momentum, smooth, updated


def update_kernel(
    wu, wd, xs, output, tgrad, newold, norm_grad, kept, dK, dV, seen_at, gl, gres, res, d0, d1, u0, u1, o, qa, qb, w_norm, v_norm, a_norm,
    *rest
):
    work = (dK, dV, seen_at, gl, gres, res)
    results, rest = [rest[n * 4 : n * 4 + 4] for n in range(4)], rest[16:]
    norm_out, lifted_out, rest = rest[:4], rest[4], rest[5:]
    out_to, memory_to, cmemory_to, tgrad_to, stage, late, sems = rest
    sem = iter(range(sems.shape[0]))
    copies = []

    def store(src, dst):
        copies.append(pltpu.make_async_copy(src, dst, sems.at[next(sem)]))
        copies[-1].start()

    r, D = o.shape
    late_in = []
    for n, (src, _r, _c) in enumerate(wide_units(wu, wd, r, D)):
        late_in.append(pltpu.make_async_copy(src, late.at[pl.ds(n * r, r), :], sems.at[next(sem)]))
        late_in[-1].start()
    g = norm_grad[0:4, :]
    norm_out[0][...] = g
    lifted_out[...] = g[2:4]
    for ref, value in zip(norm_out[1:], renew(g, v_norm[...], a_norm[...], w_norm[...])):
        ref[...] = value

    places = list(zip(*[[p[0] for p in unit_list(*arrays)] for arrays in results]))
    homes = unit_homes([ref.shape[0] for ref in work], r, 2 * len(places))
    half = D // 2

    def total(n):
        if n < 3:
            return jnp.concatenate([t[:, n * half : n * half + half] for t in (qa, qb)], axis=1)
        if n == 3:
            return o[...]
        n -= 4
        if n < 2 * u0.shape[1] // D:
            per = u0.shape[1] // D
            return (u0, u1)[n // per][:, n % per * D : n % per * D + D]
        n -= 2 * u0.shape[1] // D
        return jnp.concatenate([t[n * r : n * r + r, :] for t in (d0, d1)], axis=1)

    def old(n):
        where, row = homes[n]
        return work[where][pl.ds(row, r), :]

    here = kept.shape[0] // r
    for n in range(len(places)):
        if n >= here:
            late_in[n - here].wait()
        master = kept[pl.ds(n * r, r), :] if n < here else late[pl.ds((n - here) * r, r), :]
        grad = total(n).astype(F32)
        new = (grad,) + renew(grad, old(n), old(len(places) + n), master)
        for m, value in enumerate(new):
            if n >= RING:
                copies[(n - RING) * 4 + m].wait()
            slot = stage.at[n % RING * 4 + m]
            slot[...] = value
            store(slot, places[n][m])
    store(output, out_to)
    store(xs.at[pl.ds(xs.shape[0] - memory_to.shape[0], memory_to.shape[0]), :], memory_to)
    store(newold, cmemory_to)
    store(tgrad, tgrad_to)
    for copy in copies[max(0, len(places) - RING) * 4 :]:
        copy.wait()


def run_update(from_layer, masters, norm_old, memory):
    r, w = masters[1].shape
    units = sum(m.size for m in masters) // (r * w)
    anywhere = pl.BlockSpec(memory_space=pl.ANY)
    vmem = pl.BlockSpec(memory_space=pltpu.VMEM)
    same = [jax.ShapeDtypeStruct(m.shape, F32) for m in masters]
    small = jax.ShapeDtypeStruct(norm_old[0].shape, F32)
    lifted = jax.ShapeDtypeStruct((2, small.shape[1]), F32)
    bf = lambda x: jax.ShapeDtypeStruct(x.shape, BF)
    keep = [bf(from_layer[1]), bf(memory), bf(from_layer[3]), bf(from_layer[2])]
    held = [pltpu.with_memory_space_constraint(x, pltpu.VMEM) for x in from_layer]
    return pl.pallas_call(
        update_kernel,
        out_shape=same * 4 + [small] * 4 + [lifted] + keep,
        in_specs=[anywhere] * 2 + [vmem] * (len(held) + 3),
        out_specs=[anywhere] * 16 + [vmem] * 5 + [anywhere] * 4,
        scratch_shapes=[
            pltpu.VMEM((RING * 4, r, w), F32),
            pltpu.VMEM(((units - 4) * r, w), F32),
            pltpu.SemaphoreType.DMA((units * 5,)),
        ],
        compiler_params=pltpu.CompilerParams(vmem_limit_bytes=18 * 1024 * 1024),
        name="update",
    )(*[pltpu.with_memory_space_constraint(x, pltpu.HBM) for x in masters[2:]], *held, *[pltpu.with_memory_space_constraint(x, pltpu.HBM) for x in norm_old])


def on_device(
    sizes, tokens, memory, cmemory, doc_ids, cotangent,
    qkv_weight, out_weight, up_weight, down_weight, conv_weight, norm_params,
    qkv_moment, out_moment, up_moment, down_moment, norm_moment,
    qkv_average, out_average, up_average, down_average, norm_average,
):
    masters = (qkv_weight, out_weight, up_weight, down_weight)
    from_layer = run_layer(
        sizes, tokens[0], memory[0], cmemory[0], doc_ids, cotangent[0], *masters, conv_weight, norm_params.T,
        (qkv_moment, out_moment, up_moment, down_moment), (qkv_average, out_average, up_average, down_average),
    )
    new = run_update(from_layer, masters, (norm_params.T, norm_moment.T, norm_average.T), memory[0])
    grads, momenta, smooths, updates = new[0:4], new[4:8], new[8:12], new[12:16]
    norms = [x.T for x in new[16:20]]
    lifted = new[20].T
    out, new_memory, new_cmemory, token_grad = new[21:25]
    return (
        out[None], new_memory[None], new_cmemory[None], token_grad[None],
        *grads, norms[0], *momenta, norms[1], *smooths, norms[2], *updates, norms[3], lifted,
    )


def solution(mesh):
    sizes = (mesh.shape["stream"], mesh.shape["shard"])
    both = ("stream", "shard")
    wide = P(both, None, None)
    rows = P("shard", None)
    return jax.shard_map(
        functools.partial(on_device, sizes),
        mesh=mesh,
        in_specs=(wide, wide, wide, P(both, None), wide) + (rows,) * 16,
        out_specs=(wide,) * 4 + (rows,) * 21,
        check_vma=False,
    )
```

```python
import functools

import jax
import jax.numpy as jnp
from jax import lax
from jax.experimental import pallas as pl
from jax.experimental.pallas import tpu as pltpu
from jax.sharding import PartitionSpec as P

HEADS = 8
MOMENTUM = 0.9
RATE = 0.0025
SMOOTH = 0.8
REACH = 448
BF = jnp.bfloat16
F32 = jnp.float32
MESH = pl.DeviceIdType.MESH
GELU_C = 0.7978845608028654
GELU_A = 0.044715


def nn(a, b):
    return lax.dot_general(a, b, (((1,), (0,)), ((), ())), preferred_element_type=F32)


def nt(a, b):
    return lax.dot_general(a, b, (((1,), (1,)), ((), ())), preferred_element_type=F32)


def tn(a, b):
    return lax.dot_general(a, b, (((0,), (0,)), ((), ())), preferred_element_type=F32)


def normalised(x):
    center = x - jnp.mean(x, axis=-1, keepdims=True)
    scale = lax.rsqrt(jnp.mean(center * center, axis=-1, keepdims=True) + 1e-5)
    return center * scale, scale


def norm_back(grad, unit, scale, gain):
    inner = grad * gain
    first = jnp.mean(inner, axis=-1, keepdims=True)
    second = jnp.mean(inner * unit, axis=-1, keepdims=True)
    return (inner - first - unit * second) * scale


def two_heads(block):
    lane = lax.broadcasted_iota(jnp.int32, block.shape, 1)
    zero = jnp.zeros_like(block)
    low = lane < 64
    return jnp.concatenate([jnp.where(low, block, zero), jnp.where(low, zero, block)], axis=0)


def own_halves(block):
    return jnp.concatenate([block[0:64, 0:128], block[64:128, 128:256]], axis=0)


def rows_at(start, count, by=16):
    return pl.ds(pl.multiple_of(start, by), count)


class Sems:
    def __init__(self, ref, size):
        self.ref, self.size, self.used = ref, size, 0

    def take(self):
        self.used += 1
        assert self.used <= self.size
        return self.ref.at[self.used - 1]


def subsets(bits):
    found = [()]
    for bit in bits:
        found += [f + (bit,) for f in found]
    return found[1:]


class Place:
    def __init__(self, streams, shards):
        self.streams, self.shards = streams, shards
        self.s = lax.axis_index("stream")
        self.y = lax.axis_index("shard")

    def value(self, axis, bit, flipped=False):
        v = ((self.s if axis == "stream" else self.y) // bit) % 2
        return 1 - v if flipped else v

    def flip(self, bits):
        s, y = self.s, self.y
        for axis, bit in bits:
            step = bit * (1 - 2 * self.value(axis, bit))
            if axis == "stream":
                s = s + step
            else:
                y = y + step
        return s, y

    def index(self, bits, flipped=()):
        total = 0
        for axis, bit in bits:
            total = total * 2 + self.value(axis, bit, (axis, bit) in flipped)
        return total


def remote(src, dst, sems, who):
    copy = pltpu.make_async_remote_copy(
        src_ref=src, dst_ref=dst, send_sem=sems[0], recv_sem=sems[1], device_id=who, device_id_type=MESH
    )
    copy.start()
    return copy


CORE, NEAR = ("stream", 1), ("stream", 2)


class Gather:
    def __init__(self, place, buf, take, split, piece=(0, 1), cols=None):
        self.p, self.buf, self.take = place, buf, take
        self.block = buf.shape[0] // place.shards
        self.rows = self.block // piece[1]
        self.first_row = piece[0] * self.rows
        self.cols = cols or pl.ds(0, buf.shape[1])
        self.split = split
        self.parts = (NEAR, CORE) if split else (CORE,)
        self.count = self.rows // 2 ** len(self.parts)
        self.deltas = subsets(shard_bits(place.shards))
        self.part = place.index(self.parts)
        self.first, self.second, self.third = [], [], []

    def view(self, owner, part):
        start = owner * self.block + self.first_row + part * self.count
        return self.buf.at[rows_at(start, self.count), self.cols]

    def start(self):
        for delta in self.deltas:
            v = self.view(self.p.y, self.part)
            self.first.append(remote(v, v, self.take(), self.p.flip(delta)))

    def spread(self):
        for n, delta in enumerate(self.deltas):
            self.first[n].wait_recv()
            v = self.view(self.p.flip(delta)[1], self.part)
            if self.split:
                self.second.append(remote(v, v, self.take(), self.p.flip((NEAR,))))
            self.third.append(remote(v, v, self.take(), self.p.flip((CORE,))))

    def pass_on(self):
        if self.split:
            for n, delta in enumerate(self.deltas):
                self.second[n].wait_recv()
                v = self.view(self.p.flip(delta)[1], self.p.index(self.parts, (NEAR,)))
                self.third.append(remote(v, v, self.take(), self.p.flip((CORE,))))

    def finish(self):
        for copy in self.third:
            copy.wait_recv()

    def sent(self):
        for copy in self.first + self.second + self.third:
            copy.wait_send()


def shard_bits(shards):
    bits, bit = [], shards // 2
    while bit >= 1:
        bits.append(("shard", bit))
        bit //= 2
    return tuple(bits)


def stream_bits(streams):
    bits, bit = [], 1
    while bit < streams:
        bits.append(("stream", bit))
        bit *= 2
    return tuple(bits)


def plan_total(sizes, rows, order, merge=False):
    shards = sizes[1]
    count, full, stages, shares = rows // shards, True, [], []
    for group in order:
        across = tuple(b for b in group if b[0] == "shard")
        along = tuple(b for b in group if b[0] == "stream")
        if along and count % (16 * 2 ** len(along)):
            groups = ([(across, ())] if across else []) + [((), (b,)) for b in along]
        else:
            groups = [(across, along)]
        for across, along in groups:
            scatter = count % (16 * 2 ** len(along)) == 0
            if scatter:
                count //= 2 ** len(along)
            full = full and not across
            stages.append((across + along, along if scatter else (), bool(across), shards if full else 1, count))
            if scatter and along:
                shares.insert(0, along)
    if merge and len(shares) > 2:
        shares = [tuple(b for group in shares[-2::-1] for b in group), shares[-1]]
    return stages, shares


class Total:
    def __init__(self, place, grad, total, slots, take, plan):
        self.p, self.grad, self.total, self.take = place, grad, total, take
        self.slots = slots
        self.stages, self.shares = plan
        self.rows = grad.shape[1]
        self.off, self.count, self.full = 0, self.rows, True
        self.live, self.done = [], []
        self.at = 0

    def begin(self):
        bits, along, across, blocks, piece = self.stages[self.at]
        slot = self.slots[self.at]
        self.live = []
        for n, delta in enumerate(subsets(bits)):
            s, y = who = self.p.flip(delta)
            rows = rows_at(self.off + self.p.index(along, delta) * piece, piece)
            if across:
                src = self.grad.at[pl.ds(y, 1), rows, :]
            elif self.full:
                src = self.grad.at[:, rows, :]
            else:
                src = self.grad.at[pl.ds(self.p.y, 1), rows, :]
            self.live.append(remote(src, slot.at[n], self.take(), who))
        self.off = self.off + self.p.index(along) * piece
        self.count = piece
        self.full = self.full and not across

    def add(self, last):
        slot = self.slots[self.at]
        rows = rows_at(self.off, self.count)
        here = slice(None) if self.full else pl.ds(self.p.y, 1)
        value = self.grad[here, rows, :].astype(F32)
        for n, copy in enumerate(self.live):
            copy.wait_recv()
            value = value + slot[n].astype(F32)
        if last:
            self.total[rows, :] = value[0].astype(BF)
        else:
            self.grad[here, rows, :] = value.astype(BF)
        self.done += self.live
        self.at += 1

    def share(self, bits):
        v = self.total.at[rows_at(self.off, self.count), :]
        self.live = [remote(v, v, self.take(), self.p.flip(delta)) for delta in subsets(bits)]
        self.off = self.off - self.p.index(bits) * self.count
        self.count *= 2 ** len(bits)

    def arrive(self):
        for copy in self.live:
            copy.wait_recv()
        self.done += self.live

    def steps(self):
        def middle():
            self.add(False)
            self.begin()

        def turn():
            self.add(True)
            self.share(self.shares[0])

        def later(bits):
            self.arrive()
            self.share(bits)

        out = [self.begin] + [middle] * (len(self.stages) - 1) + [turn]
        return out + [functools.partial(later, bits) for bits in self.shares[1:]] + [self.arrive]

    def sent(self):
        for copy in self.done:
            copy.wait_send()


class Everywhere:
    def __init__(self, place, table, slots, take, groups):
        self.p, self.table, self.slots, self.take, self.groups = place, table, slots, take, groups
        self.live, self.done, self.at = [], [], 0

    def begin(self):
        group, slot = self.groups[self.at], self.slots[self.at]
        mine = pl.ds(self.p.index(group), 1)
        slot[mine] = self.table[...][None]
        self.live = [remote(slot.at[mine], slot.at[mine], self.take(), self.p.flip(d)) for d in subsets(group)]

    def add(self):
        for copy in self.live:
            copy.wait_recv()
        self.done += self.live
        slot = self.slots[self.at]
        total = slot[0]
        for n in range(1, slot.shape[0]):
            total = total + slot[n]
        self.table[...] = total
        self.at += 1

    def steps(self):
        def middle():
            self.add()
            self.begin()

        return [self.begin] + [middle] * (len(self.groups) - 1) + [self.add]

    def sent(self):
        for copy in self.done:
            copy.wait_send()


GRADS = ("d0", "d1", "u0", "u1", "o", "qa", "qb")
WAYS = {"d0": "yx.z", "d1": "yx.z", "u0": "z.y.x", "u1": "y.x.z", "o": "x.y.z", "qa": "yx.z", "qb": "yx.z"}
RING = 4
TICKS = (
    ("d0",),
    ("d0",),
    ("u0",),
    ("u1", "d1", "u0"),
    (),
    (),
    ("d1",),
    (),
    (),
    (),
    (),
    (),
    ("o",),
    ("u1", "o", "d0"),
    (),
    (),
    (),
    ("qa", "d1"),
    ("qa",),
    (),
    ("d0", "u0"),
    ("u1",),
    ("d1",),
    ("o",),
    ("qb",),
    ("qa", "u0", "qb", "o"),
    (),
    (),
    (),
    ("u1",),
    (),
    ("d1",),
    (),
    ("o", "qa"),
    (),
    (),
    ("qb",),
    (),
    (),
    (),
    (),
    ("u0", "n", "d0", "u1", "n"),
    (),
    (),
    (),
    (),
    ("qa", "qb"),
    (),
    (),
    ("u0", "d0", "n"),
    ("o",),
    ("d0", "u1"),
    (),
    (),
    (),
    ("d1", "qa"),
    (),
    (),
    ("qa", "o", "d1", "qb", "u1", "o", "u1", "u0", "qb", "u0", "qb"),
)


def layer_kernel(
    sizes, plan, tok, mem, old, docs, cot, wqkv, wo, wu, wd, wc, norms, *rest
):
    moments, averages, rest = rest[:4], rest[4:8], rest[8:]
    xs, ct, lifted, newold, norm_total, kept, dK, dV, seen_at, gl, gres, res, *rest = rest
    tbuf, rest = rest[:7], rest[7:]
    (N, Q, K, V, PT, OT, act, gh, Dv, Wq, Wk, Wv, Wo, Wu, Wd, Wc, nblocks, ngrad, *rest) = rest
    gbuf, rest = rest[:7], rest[7:]
    gr, dO = gh.at[:, pl.ds(0, Wo.shape[1])], gh.at[:, pl.ds(Wo.shape[1], Wo.shape[1])]
    slots = []
    for stages, _ in plan["totals"]:
        slots.append(rest[: len(stages)])
        rest = rest[len(stages) :]
    nslots, rest = rest[: len(plan["groups"])], rest[len(plan["groups"]) :]
    send_ref, recv_ref, local_ref = rest
    place = Place(*sizes)
    send, recv, local = Sems(send_ref, plan["sems"]), Sems(recv_ref, plan["sems"]), Sems(local_ref, plan["local"])

    def pair():
        return send.take(), recv.take()

    shards = place.shards
    S, D = tok.shape
    M = mem.shape[0]
    H0 = M - REACH
    L = REACH + S
    T0 = REACH
    W = REACH + 128
    FF = Wu.shape[1]
    n_q = S // 128

    barrier = pltpu.get_barrier_semaphore()
    for bits in plan["partners"]:
        pl.semaphore_signal(barrier, inc=1, device_id=place.flip(bits), device_id_type=MESH)

    def fetch(src, dst):
        copy = pltpu.make_async_copy(src, dst, local.take())
        copy.start()
        return copy

    jobs = {}

    def bring(name, pieces, target, unit, ref):
        for n, (src, row, col) in enumerate(pieces):
            stage = ref.at[pl.ds((unit + n) * r1, r1), :]
            jobs.setdefault(name, []).append((fetch(src, stage), stage, target, row, col))

    r1 = wqkv.shape[0]
    pieces = unit_list(wqkv, wo, wu, wd)
    bring("k", [(pieces[1][0], 0, 0)], Wk, 1, kept)
    bring("v", [(pieces[2][0], 0, 0)], Wv, 2, kept)
    bring("q", pieces[0:1], Wq, 0, kept)
    tok_in = fetch(tok, xs.at[pl.ds(M, S), :])
    mem_in = fetch(mem, xs.at[pl.ds(0, M), :])
    bring("o", pieces[3:4], Wo, 3, kept)
    bring("u", pieces[4 : 4 + FF // D], Wu, 0, dV)
    bring("d", pieces[4 + FF // D :], Wd, 0, dK)
    stage = gl.at[pl.ds(0, wc.shape[0]), :]
    jobs["c"] = [(fetch(wc, stage), stage, Wc, 0, 0)]
    cot_in = fetch(cot, ct)
    old_in = fetch(old.at[pl.ds(S // 3, old.shape[0] - S // 3), :], newold.at[pl.ds(0, old.shape[0] - S // 3), :])

    nblocks[pl.ds(place.y, 1)] = jnp.concatenate(
        [norms[...].astype(BF).astype(F32), jnp.zeros((4, norms.shape[1]), F32)], axis=0
    )[None]

    def cast(name):
        for copy, stage, target, row, col in jobs[name]:
            copy.wait()
            here = rows_at(place.y * (target.shape[0] // shards) + row, stage.shape[0])
            target[here, pl.ds(col, 512)] = stage[...].astype(BF)

    cast("k")
    pl.semaphore_wait(barrier, len(plan["partners"]))
    own = nblocks.at[pl.ds(place.y, 1)]
    norm_copies = [remote(own, own, pair(), place.flip(delta)) for delta in subsets(shard_bits(shards))]
    gathers = {}

    def launch(name, buf, **piece):
        gathers[name] = Gather(place, buf, pair, plan["split"], **piece)
        gathers[name].start()

    launch("k", Wk)
    cast("v")
    launch("v", Wv)
    cast("q")
    launch("q", Wq)
    cast("o")
    launch("o", Wo)

    ids = docs[...].astype(F32)
    column = jnp.transpose(jnp.broadcast_to(ids, (8, ids.shape[1])))
    base = ids.shape[1] - L

    def see(b):
        key = column[base + 128 * b : base + 128 * b + W, 0:1]
        query = ids[:, base + T0 + 128 * b : base + T0 + 128 * b + 128]
        k = lax.broadcasted_iota(jnp.int32, (W, 128), 0)
        q = lax.broadcasted_iota(jnp.int32, (W, 128), 1) + T0
        seen_at[pl.ds(b // 4 * W, W), pl.ds(b % 4 * 128, 128)] = jnp.where((key == query) & (k <= q), 0.0, -1e30)

    for b in range(n_q):
        see(b)
    cast("u")
    for n in range(2):
        launch("u" + str(n), Wu, cols=pl.ds(n * FF // 2, FF // 2))
    for copy in norm_copies:
        copy.wait_recv()
    table = jnp.concatenate([nblocks[j] for j in range(shards)], axis=1)
    g1, b1, g2, b2 = table[0:1], table[1:2], table[2:3], table[3:4]

    tok_in.wait()
    mem_in.wait()

    def ln1(n):
        r = slice(n * L // 4, (n + 1) * L // 4)
        unit, _s = normalised(xs[H0 + r.start : H0 + r.stop, :].astype(F32))
        N[r, :] = (unit * g1 + b1).astype(BF)

    ln1(0)
    ln1(1)
    gathers["k"].spread()
    cast("d")
    for n in range(2):
        launch("d" + str(n), Wd, piece=(n, 2))
    gathers["v"].spread()
    ln1(2)
    ln1(3)
    gathers["q"].spread()
    cast("c")
    launch("c", Wc)
    gathers["k"].pass_on()
    gathers["o"].spread()
    gathers["v"].pass_on()
    gathers["k"].finish()
    for c in range(2):
        cs = slice(c * 256, c * 256 + 256)
        for r in (slice(0, L // 2), slice(L // 2, L)):
            K[r, cs] = nn(N[r, :], Wk[:, cs]).astype(BF)
    gathers["q"].pass_on()
    gathers["v"].finish()
    for c in range(2):
        cs = slice(c * 256, c * 256 + 256)
        for r in (slice(0, L // 2), slice(L // 2, L)):
            V[r, cs] = nn(N[r, :], Wv[:, cs]).astype(BF)
    gathers["o"].pass_on()
    gathers["q"].finish()
    for c in range(2):
        cs = slice(c * 256, c * 256 + 256)
        Q[:, cs] = (nn(N[T0:, :], Wq[:, cs]).astype(BF).astype(F32) * 0.125).astype(BF)

    def scores(i, u, slot):
        qb, p = i // 2, (i % 2) * 2 + u
        q0, l0 = rows_at(qb * 128, 128, 128), rows_at(p * 128, 128, 128)
        s = nt(K[rows_at(qb * 128, W, 128), l0], two_heads(Q[q0, l0]))
        seen = seen_at[rows_at(qb // 4 * W, W), rows_at(qb % 4 * 128, 128, 128)]
        raw[slot][0:W, u * 256 : u * 256 + 256] = s + jnp.concatenate([seen, seen], axis=1)

    def attend(i, u, slot):
        qb, p = i // 2, (i % 2) * 2 + u
        q0, l0 = rows_at(qb * 128, 128, 128), rows_at(p * 128, 128, 128)
        cs = slice(u * 256, u * 256 + 256)
        pieces = [slice(c, c + 64) for c in range(0, W, 64)]
        top, total = None, None
        for r in pieces:
            part = jnp.max(raw[slot][r, cs].reshape(8, 8, 256), axis=0)
            top = part if top is None else jnp.maximum(top, part)
        top = jnp.max(top, axis=0, keepdims=True)
        for r in pieces:
            e = jnp.exp(raw[slot][r, cs] - top)
            raw[slot][r, cs] = e
            part = jnp.sum(e.reshape(8, 8, 256), axis=0)
            total = part if total is None else total + part
        scale = 1.0 / jnp.sum(total, axis=0, keepdims=True)
        for r in pieces:
            PT[p * n_q + qb, r, :] = (raw[slot][r, cs] * scale).astype(BF)
        OT[l0, q0] = own_halves(tn(V[rows_at(qb * 128, W, 128), l0], PT[p * n_q + qb])).astype(BF)

    def attend_two(j, _):
        for slot in range(2):
            for u in range(2):
                scores(jnp.minimum(2 * j + slot + 1, 2 * n_q - 1), u, 1 - slot)
            for u in range(2):
                attend(2 * j + slot, u, slot)
        return 0

    raw = (gl, gres)
    for u in range(2):
        scores(0, u, 0)
    gathers["u0"].spread()
    lax.fori_loop(0, 2, attend_two, 0)
    gathers["u1"].spread()
    lax.fori_loop(2, 4, attend_two, 0)
    gathers["d0"].spread()
    gathers["u0"].pass_on()
    lax.fori_loop(4, n_q, attend_two, 0)
    gathers["d1"].spread()
    gathers["u1"].pass_on()
    gathers["o"].finish()

    for c in range(2):
        cs = slice(c * 256, c * 256 + 256)
        res[:, cs] = xs[M:, cs].astype(F32) + tn(OT[...], Wo[:, cs])

    for n in range(3):
        r = slice(n * S // 3, (n + 1) * S // 3)
        unit, _s = normalised(res[r, :])
        lifted[r, :] = (unit * g2 + b2).astype(BF)
    gathers["d0"].pass_on()
    cot_in.wait()
    gathers["u0"].finish()
    gathers["u1"].finish()

    tiles = FF // 256

    def tile_at(i):
        return rows_at((i + place.y * (tiles // shards)) % tiles * 256, 256, 256)

    def ffn_in(i, slot):
        here = slice(slot * 256, slot * 256 + 256)
        dK[0:S, here] = nn(lifted[...], Wu[:, tile_at(i)])
        dV[0:S, here] = nt(ct[...], Wd[tile_at(i), :])

    def ffn_out(i, slot):
        here = slice(slot * 256, slot * 256 + 256)
        for n in range(0, S, 128):
            r = slice(n, n + 128)
            h, ga = dK[r, here], dV[r, here]
            h2 = h * h
            hp = 0.5 + 0.5 * jnp.tanh(h * (GELU_C + (GELU_C * GELU_A) * h2))
            a = h * hp
            slope = hp + (a - a * hp) * (2.0 * GELU_C + (6.0 * GELU_C * GELU_A) * h2)
            act[r, tile_at(i)] = a.astype(BF)
            gh[r, tile_at(i)] = (ga * slope).astype(BF)

    def put(ref, start, value):
        rows = value.shape[0]
        if rows > ref.shape[1]:
            n = rows // ref.shape[1]
            ref[pl.ds(start // ref.shape[1], n)] = value.astype(BF).reshape(n, ref.shape[1], value.shape[1])
        else:
            ref[start // ref.shape[1], rows_at(start % ref.shape[1], rows), :] = value.astype(BF)

    def put_all(ref, cols, value):
        ref[:, :, cols] = value.astype(BF).reshape(ref.shape[0], ref.shape[1], value.shape[1])

    def grad_down(ref, col, low, high):
        def body(i, _):
            first = (2 * i + place.y * (tiles // shards)) % tiles
            put(ref, first * 256, tn(act[:, rows_at(first * 256, 512, 256)], ct[:, col : col + 256]))
            return 0

        lax.fori_loop(low // 2, high // 2, body, 0)

    own_tiles = tiles // shards
    early = own_tiles if own_tiles % 2 == 0 else 0
    ffn_in(0, 0)
    for i in range(tiles):
        if i + 1 == own_tiles:
            ffn_out(i, i % 2)
            for n in range(2):
                grad_down(gbuf[n], n * D // 2, 0, early)
            gathers["d1"].pass_on()
            gathers["d0"].finish()
            gathers["d1"].finish()
            ffn_in(i + 1, (i + 1) % 2)
            continue
        if i + 1 < tiles:
            ffn_in(i + 1, (i + 1) % 2)
        ffn_out(i, i % 2)
    gathers["c"].spread()

    homes = unit_homes(plan["work"], r1, 2 * len(pieces))
    old_units = [p[0] for p in unit_list(*moments)] + [p[0] for p in unit_list(*averages)]
    work = (dK, dV, seen_at, gl, gres, res)
    refill = []

    def bring_old(index):
        for src, (where, row) in zip(old_units, homes):
            if where == index:
                refill.append(fetch(src, work[index].at[pl.ds(row, r1), :]))

    sums = {
        name: Total(place, gbuf[i], tbuf[i], slots[i], pair, plan["totals"][i]) for i, name in enumerate(GRADS)
    }
    sums["n"] = Everywhere(place, ngrad, nslots, pair, plan["groups"])
    waiting = {name: sums[name].steps() for name in sums}
    clock = []

    def go(names):
        for name in names:
            if not waiting[name]:
                continue
            waiting[name].pop(0)()

    def tick():
        if len(clock) < len(plan["ticks"]):
            go(plan["ticks"][len(clock)])
        clock.append(0)

    for n in range(2):
        grad_down(gbuf[n], n * D // 2, early, tiles)
        tick()
    for n in range(2):
        for c in range(2):
            piece = gh[:, n * 1024 + c * 512 : n * 1024 + c * 512 + 512]
            put_all(gbuf[2 + n], slice(c * 512, c * 512 + 512), tn(lifted[...], piece))
        tick()
    for c in range(2):
        cs = slice(c * 256, c * 256 + 256)
        gl[:, cs] = nt(gh[...], Wu[cs, :])
        tick()

    def by_eight(x):
        return jnp.sum(x.reshape(x.shape[0] // 8, 8, D), axis=0)

    second = [jnp.zeros((8, D), F32)] * 2
    for n in range(3):
        r = slice(n * S // 3, (n + 1) * S // 3)
        unit, scale = normalised(res[r, :])
        gy = gl[r, :]
        x = ct[r, :].astype(F32) + norm_back(gy, unit, scale, g2)
        gres[r, :] = x
        gr[r, :] = x.astype(BF)
        second = [second[0] + by_eight(gy * unit), second[1] + by_eight(gy)]
        tick()
    put_all(gbuf[4], slice(0, D), nn(OT[...], gr[...]))
    tick()
    for c in range(2):
        cs = slice(c * 256, c * 256 + 256)
        dO[:, cs] = nt(gr[...], Wo[cs, :]).astype(BF)
    for c in range(2):
        cs = slice(c * 256, c * 256 + 256)
        dt = nt(Wo[cs, :], gr[...]).astype(BF).astype(F32) * OT[cs, :].astype(F32)
        for h in range(4):
            Dv[c * 2 + h // 2, h % 2 : h % 2 + 1, :] = jnp.sum(dt[h * 64 : h * 64 + 64], axis=0, keepdims=True)
    dK[...] = jnp.zeros_like(dK)
    dV[...] = jnp.zeros_like(dV)
    tick()

    def back_in(i, u, slot):
        qb, p = i % n_q, i // n_q * 2 + u
        q0, l0 = slice(qb * 128, qb * 128 + 128), slice(p * 128, p * 128 + 128)
        raw[slot][0:W, u * 256 : u * 256 + 256] = nt(V[qb * 128 : qb * 128 + W, l0], two_heads(dO[q0, l0]))

    def back_out(i, u, slot):
        qb, p = i % n_q, i // n_q * 2 + u
        q0, l0, keys = slice(qb * 128, qb * 128 + 128), slice(p * 128, p * 128 + 128), slice(qb * 128, qb * 128 + W)
        mean = jnp.concatenate([Dv[p, 0:1, q0], Dv[p, 1:2, q0]], axis=1)
        probs = PT[p * n_q + qb]
        ds = (probs.astype(F32) * (raw[slot][0:W, u * 256 : u * 256 + 256] - mean)).astype(BF)
        dV[keys, l0] += nn(probs, two_heads(dO[q0, l0]))
        dK[keys, l0] += nn(ds, two_heads(Q[q0, l0]))
        dq = own_halves(tn(K[keys, l0], ds)) * 0.125
        Q[q0, l0] = jnp.transpose(dq).astype(BF)

    raw = (gl, seen_at)
    for u in range(2):
        back_in(0, u, 0)
    for i in range(2 * n_q):
        if i + 1 < 2 * n_q:
            for u in range(2):
                back_in(i + 1, u, (i + 1) % 2)
        for u in range(2):
            back_out(i, u, i % 2)
        tick()
        if i % n_q == n_q - 1:
            quad = i // n_q
            cs = slice(quad * 256, quad * 256 + 256)
            K[:, cs] = dK[0:L, cs].astype(BF)
            V[:, cs] = dV[0:L, cs].astype(BF)
            g = gbuf[5 + quad]
            put_all(g, slice(0, 256), tn(N[T0:, :], Q[:, cs]))
            put_all(g, slice(256, 512), tn(N[...], K[:, cs]))
            put_all(g, slice(512, 768), tn(N[...], V[:, cs]))
            tick()

    for index in range(1, 4):
        bring_old(index)
    for c in range(2):
        cs = slice(c * 256, c * 256 + 256)
        for r in (slice(0, L // 2), slice(L // 2, L)):
            dK[r, cs] = nt(K[r, :], Wk[cs, :])
            dK[r, cs] += nt(V[r, :], Wv[cs, :])
        dK[T0:L, cs] += nt(Q[...], Wq[cs, :])
        tick()

    first = [jnp.zeros((8, D), F32)] * 2
    for low, high in [(0, T0 // 2), (T0 // 2, T0)] + [(T0 + n * S // 3, T0 + (n + 1) * S // 3) for n in range(3)]:
        unit, scale = normalised(xs[H0 + low : H0 + high, :].astype(F32))
        gy = dK[low:high, :]
        if low >= T0:
            r = slice(low - T0, high - T0)
            lifted[r, :] = (gres[r, :] + norm_back(gy, unit, scale, g1)).astype(BF)
        first = [first[0] + by_eight(gy * unit), first[1] + by_eight(gy)]
        if high == L:
            rows = [jnp.sum(x, axis=0, keepdims=True) for x in first + second]
            ngrad[...] = jnp.concatenate(rows + [jnp.zeros((4, D), F32)], axis=0)
        tick()
    bring_old(0)
    bring_old(4)

    for c in range(2):
        cs = slice(c * 256, c * 256 + 256)
        ct[:, cs] = (res[:, cs] + nn(act[...], Wd[:, cs])).astype(BF)
        tick()
    bring_old(5)
    gathers["c"].pass_on()
    gathers["c"].finish()
    squeezed = None
    for t in range(3):
        row = lax.broadcasted_iota(jnp.int32, (S // 3, S), 0) * 3 + t
        pick = jnp.where(lax.broadcasted_iota(jnp.int32, (S // 3, S), 1) == row, 1.0, 0.0).astype(BF)
        term = nn(nn(pick, xs[pl.ds(0, S), :]).astype(BF), Wc[t * D : (t + 1) * D, :])
        squeezed = term if squeezed is None else squeezed + term
        tick()
    newold[pl.ds(old.shape[0] - S // 3, S // 3), :] = squeezed.astype(BF)
    while len(clock) < len(plan["ticks"]):
        tick()
    while any(waiting.values()):
        go([name for name in waiting if waiting[name]])
    final = ngrad[...]
    width = norms.shape[1]
    mine = final[:, 0:width]
    for j in range(1, shards):
        mine = jnp.where(place.y == j, final[:, j * width : (j + 1) * width], mine)
    norm_total[...] = mine

    for copy in refill + [old_in]:
        copy.wait()
    for part in list(gathers.values()) + list(sums.values()):
        part.sent()
    for copy in norm_copies:
        copy.wait_send()


def wide_units(wu, wd, r, w):
    units = [(wu.at[:, pl.ds(c * w, w)], 0, c * w) for c in range(wu.shape[1] // w)]
    return units + [(wd.at[pl.ds(n, r), :], n, 0) for n in range(0, wd.shape[0], r)]


def unit_list(wqkv, wo, wu, wd):
    r, w = wo.shape
    return [(wqkv.at[:, pl.ds(c * w, w)], 0, 0) for c in range(3)] + [(wo, 0, 0)] + wide_units(wu, wd, r, w)


def unit_homes(work, r, count):
    homes = [(i, row) for i, rows in enumerate(work) for row in range(0, rows - r + 1, r)]
    assert len(homes) >= count
    return homes[:count]


def work_rows(S):
    big = -(-(REACH + S) // 256) * 256
    return (big, big, big, S, S, S)


def run_layer(sizes, tokens, memory, cmemory, docs, cotangent, wqkv, wo, wu, wd, wc, norms, moments, averages):
    streams, shards = sizes
    S, D = tokens.shape
    M = memory.shape[0]
    L = REACH + S
    W = REACH + 128
    FF = wu.shape[1]
    n_q = S // 128
    shapes = [(FF, D // 2)] * 2 + [(D, FF // 2)] * 2 + [(D, D)] + [(D, 3 * D // 2)] * 2
    shapes = [(shards, rows // shards, cols) for rows, cols in shapes]
    across, along = shard_bits(shards), stream_bits(streams)
    far = [along[i : i + 2] for i in range(2, len(along), 2)]
    axes = {"c": [(CORE,)], "y": [across], "x": [(NEAR,)], "yx": [across + (NEAR,)], "z": far}
    totals = []
    for i, name in enumerate(GRADS):
        way = WAYS[name].rstrip("+")
        order = [group for axis in ["c"] + way.split(".") for group in axes[axis]]
        totals.append(plan_total(sizes, FF if i < 2 else D, order, WAYS[name].endswith("+")))
    groups = [across + (NEAR, CORE)] + far
    used = [subsets(across), subsets((NEAR, CORE))] + [subsets(g) for g in groups]
    for stages, shares in totals:
        used += [subsets(stage[0]) for stage in stages] + [subsets(bits) for bits in shares]
    partners = sorted({tuple(sorted(delta)) for some in used for delta in some})
    sems = 9 * 4 * (shards - 1) + len(subsets(across)) + sum(len(subsets(g)) for g in groups)
    for stages, shares in totals:
        sems += sum(len(subsets(stage[0])) for stage in stages) + sum(len(subsets(bits)) for bits in shares)
    plan = {
        "totals": totals,
        "groups": groups,
        "partners": partners,
        "ticks": TICKS,
        "sems": sems,
        "local": 64,
        "work": work_rows(S),
        "split": True,
    }
    f32, bf = (lambda *s: pltpu.VMEM(s, F32)), (lambda *s: pltpu.VMEM(s, BF))
    scratch = [
        bf(L, D), bf(S, D), bf(L, D), bf(L, D), bf((HEADS // 2) * n_q, W, 256), bf(D, S), bf(S, FF), bf(S, FF),
        f32(HEADS // 2, 2, S), bf(D, D), bf(D, D), bf(D, D), bf(D, D), bf(D, FF), bf(FF, D), bf(3 * D, D),
        f32(shards, 8, norms.shape[1]), f32(8, D),
    ]
    scratch += [bf(*s) for s in shapes]
    for (stages, _), s in zip(totals, shapes):
        scratch += [bf(len(subsets(bits)), blocks, piece, s[2]) for bits, _b, _a, blocks, piece in stages]
    scratch += [f32(2 ** len(g), 8, D) for g in groups]
    scratch += [pltpu.SemaphoreType.DMA((sems,)), pltpu.SemaphoreType.DMA((sems,)), pltpu.SemaphoreType.DMA((64,))]
    anywhere = pl.BlockSpec(memory_space=pl.ANY)
    vmem = pl.BlockSpec(memory_space=pltpu.VMEM)
    units = 3 + 1
    out_shape = [bf(M + S, D), bf(S, D), bf(S, D), bf(*cmemory.shape), f32(8, norms.shape[1]), f32(units * wo.shape[0], D)]
    out_shape += [f32(rows, D) for rows in plan["work"]]
    out_shape += [bf(s[1], s[2]) for s in shapes]
    room = 253 * 256 * 1024 - sum(x.inner_aval.size * x.inner_aval.dtype.itemsize for x in out_shape)
    big = [pltpu.with_memory_space_constraint(x, pltpu.HBM) for x in (tokens, memory, cmemory)]
    more = [pltpu.with_memory_space_constraint(x, pltpu.HBM) for x in (cotangent, wqkv, wo, wu, wd, wc)]
    later = [pltpu.with_memory_space_constraint(x, pltpu.HBM) for x in (*moments, *averages)]
    return pl.pallas_call(
        functools.partial(layer_kernel, sizes, plan),
        out_shape=out_shape,
        in_specs=[anywhere] * 3 + [vmem] + [anywhere] * 6 + [vmem] + [anywhere] * 8,
        out_specs=[vmem] * len(out_shape),
        scratch_shapes=scratch,
        compiler_params=pltpu.CompilerParams(
            collective_id=0, has_side_effects=True, vmem_limit_bytes=room
        ),
        name="layer",
    )(*big, docs, *more, norms, *later)


def renew(grad, moment, average, master):
    momentum = MOMENTUM * moment + (1.0 - MOMENTUM) * grad
    updated = master - RATE * ((1.0 - MOMENTUM) * grad + MOMENTUM * momentum)
    smooth = SMOOTH * average + (1.0 - SMOOTH) * updated
    return momentum, smooth, updated


def update_kernel(
    wu, wd, xs, output, tgrad, newold, norm_grad, kept, dK, dV, seen_at, gl, gres, res, d0, d1, u0, u1, o, qa, qb, w_norm, v_norm, a_norm,
    *rest
):
    work = (dK, dV, seen_at, gl, gres, res)
    results, rest = [rest[n * 4 : n * 4 + 4] for n in range(4)], rest[16:]
    norm_out, lifted_out, rest = rest[:4], rest[4], rest[5:]
    out_to, memory_to, cmemory_to, tgrad_to, stage, late, sems = rest
    sem = iter(range(sems.shape[0]))
    copies = []

    def store(src, dst):
        copies.append(pltpu.make_async_copy(src, dst, sems.at[next(sem)]))
        copies[-1].start()

    r, D = o.shape
    late_in = []
    for n, (src, _r, _c) in enumerate(wide_units(wu, wd, r, D)):
        late_in.append(pltpu.make_async_copy(src, late.at[pl.ds(n * r, r), :], sems.at[next(sem)]))
        late_in[-1].start()
    g = norm_grad[0:4, :]
    norm_out[0][...] = g
    lifted_out[...] = g[2:4]
    for ref, value in zip(norm_out[1:], renew(g, v_norm[...], a_norm[...], w_norm[...])):
        ref[...] = value

    places = list(zip(*[[p[0] for p in unit_list(*arrays)] for arrays in results]))
    homes = unit_homes([ref.shape[0] for ref in work], r, 2 * len(places))
    half = D // 2

    def total(n):
        if n < 3:
            return jnp.concatenate([t[:, n * half : n * half + half] for t in (qa, qb)], axis=1)
        if n == 3:
            return o[...]
        n -= 4
        if n < 2 * u0.shape[1] // D:
            per = u0.shape[1] // D
            return (u0, u1)[n // per][:, n % per * D : n % per * D + D]
        n -= 2 * u0.shape[1] // D
        return jnp.concatenate([t[n * r : n * r + r, :] for t in (d0, d1)], axis=1)

    def old(n):
        where, row = homes[n]
        return work[where][pl.ds(row, r), :]

    here = kept.shape[0] // r
    for n in range(len(places)):
        if n >= here:
            late_in[n - here].wait()
        master = kept[pl.ds(n * r, r), :] if n < here else late[pl.ds((n - here) * r, r), :]
        grad = total(n).astype(F32)
        new = (grad,) + renew(grad, old(n), old(len(places) + n), master)
        for m, value in enumerate(new):
            if n >= RING:
                copies[(n - RING) * 4 + m].wait()
            slot = stage.at[n % RING * 4 + m]
            slot[...] = value
            store(slot, places[n][m])
    store(output, out_to)
    store(xs.at[pl.ds(xs.shape[0] - memory_to.shape[0], memory_to.shape[0]), :], memory_to)
    store(newold, cmemory_to)
    store(tgrad, tgrad_to)
    for copy in copies[max(0, len(places) - RING) * 4 :]:
        copy.wait()


def run_update(from_layer, masters, norm_old, memory):
    r, w = masters[1].shape
    units = sum(m.size for m in masters) // (r * w)
    anywhere = pl.BlockSpec(memory_space=pl.ANY)
    vmem = pl.BlockSpec(memory_space=pltpu.VMEM)
    same = [jax.ShapeDtypeStruct(m.shape, F32) for m in masters]
    small = jax.ShapeDtypeStruct(norm_old[0].shape, F32)
    lifted = jax.ShapeDtypeStruct((2, small.shape[1]), F32)
    bf = lambda x: jax.ShapeDtypeStruct(x.shape, BF)
    keep = [bf(from_layer[1]), bf(memory), bf(from_layer[3]), bf(from_layer[2])]
    held = [pltpu.with_memory_space_constraint(x, pltpu.VMEM) for x in from_layer]
    return pl.pallas_call(
        update_kernel,
        out_shape=same * 4 + [small] * 4 + [lifted] + keep,
        in_specs=[anywhere] * 2 + [vmem] * (len(held) + 3),
        out_specs=[anywhere] * 16 + [vmem] * 5 + [anywhere] * 4,
        scratch_shapes=[
            pltpu.VMEM((RING * 4, r, w), F32),
            pltpu.VMEM(((units - 4) * r, w), F32),
            pltpu.SemaphoreType.DMA((units * 5,)),
        ],
        compiler_params=pltpu.CompilerParams(vmem_limit_bytes=18 * 1024 * 1024),
        name="update",
    )(*[pltpu.with_memory_space_constraint(x, pltpu.HBM) for x in masters[2:]], *held, *[pltpu.with_memory_space_constraint(x, pltpu.HBM) for x in norm_old])


def on_device(
    sizes, tokens, memory, cmemory, doc_ids, cotangent,
    qkv_weight, out_weight, up_weight, down_weight, conv_weight, norm_params,
    qkv_moment, out_moment, up_moment, down_moment, norm_moment,
    qkv_average, out_average, up_average, down_average, norm_average,
):
    masters = (qkv_weight, out_weight, up_weight, down_weight)
    from_layer = run_layer(
        sizes, tokens[0], memory[0], cmemory[0], doc_ids, cotangent[0], *masters, conv_weight, norm_params.T,
        (qkv_moment, out_moment, up_moment, down_moment), (qkv_average, out_average, up_average, down_average),
    )
    new = run_update(from_layer, masters, (norm_params.T, norm_moment.T, norm_average.T), memory[0])
    grads, momenta, smooths, updates = new[0:4], new[4:8], new[8:12], new[12:16]
    norms = [x.T for x in new[16:20]]
    lifted = new[20].T
    out, new_memory, new_cmemory, token_grad = new[21:25]
    return (
        out[None], new_memory[None], new_cmemory[None], token_grad[None],
        *grads, norms[0], *momenta, norms[1], *smooths, norms[2], *updates, norms[3], lifted,
    )


def solution(mesh):
    sizes = (mesh.shape["stream"], mesh.shape["shard"])
    both = ("stream", "shard")
    wide = P(both, None, None)
    rows = P("shard", None)
    return jax.shard_map(
        functools.partial(on_device, sizes),
        mesh=mesh,
        in_specs=(wide, wide, wide, P(both, None), wide) + (rows,) * 16,
        out_specs=(wide,) * 4 + (rows,) * 21,
        check_vma=False,
    )
```

```python
import functools

import jax
import jax.numpy as jnp
from jax import lax
from jax.experimental import pallas as pl
from jax.experimental.pallas import tpu as pltpu
from jax.sharding import PartitionSpec as P

HEADS = 8
MOMENTUM = 0.9
RATE = 0.0025
SMOOTH = 0.8
REACH = 448
BF = jnp.bfloat16
F32 = jnp.float32
MESH = pl.DeviceIdType.MESH
GELU_C = 0.7978845608028654
GELU_A = 0.044715


def nn(a, b):
    return lax.dot_general(a, b, (((1,), (0,)), ((), ())), preferred_element_type=F32)


def nt(a, b):
    return lax.dot_general(a, b, (((1,), (1,)), ((), ())), preferred_element_type=F32)


def tn(a, b):
    return lax.dot_general(a, b, (((0,), (0,)), ((), ())), preferred_element_type=F32)


def normalised(x):
    center = x - jnp.mean(x, axis=-1, keepdims=True)
    scale = lax.rsqrt(jnp.mean(center * center, axis=-1, keepdims=True) + 1e-5)
    return center * scale, scale


def norm_back(grad, unit, scale, gain):
    inner = grad * gain
    first = jnp.mean(inner, axis=-1, keepdims=True)
    second = jnp.mean(inner * unit, axis=-1, keepdims=True)
    return (inner - first - unit * second) * scale


def two_heads(block):
    lane = lax.broadcasted_iota(jnp.int32, block.shape, 1)
    zero = jnp.zeros_like(block)
    low = lane < 64
    return jnp.concatenate([jnp.where(low, block, zero), jnp.where(low, zero, block)], axis=0)


def own_halves(block):
    return jnp.concatenate([block[0:64, 0:128], block[64:128, 128:256]], axis=0)


def rows_at(start, count, by=16):
    return pl.ds(pl.multiple_of(start, by), count)


class Sems:
    def __init__(self, ref, size):
        self.ref, self.size, self.used = ref, size, 0

    def take(self):
        self.used += 1
        assert self.used <= self.size
        return self.ref.at[self.used - 1]


def subsets(bits):
    found = [()]
    for bit in bits:
        found += [f + (bit,) for f in found]
    return found[1:]


class Place:
    def __init__(self, streams, shards):
        self.streams, self.shards = streams, shards
        self.s = lax.axis_index("stream")
        self.y = lax.axis_index("shard")

    def value(self, axis, bit, flipped=False):
        v = ((self.s if axis == "stream" else self.y) // bit) % 2
        return 1 - v if flipped else v

    def flip(self, bits):
        s, y = self.s, self.y
        for axis, bit in bits:
            step = bit * (1 - 2 * self.value(axis, bit))
            if axis == "stream":
                s = s + step
            else:
                y = y + step
        return s, y

    def index(self, bits, flipped=()):
        total = 0
        for axis, bit in bits:
            total = total * 2 + self.value(axis, bit, (axis, bit) in flipped)
        return total


def remote(src, dst, sems, who):
    copy = pltpu.make_async_remote_copy(
        src_ref=src, dst_ref=dst, send_sem=sems[0], recv_sem=sems[1], device_id=who, device_id_type=MESH
    )
    copy.start()
    return copy


CORE, NEAR = ("stream", 1), ("stream", 2)


class Gather:
    def __init__(self, place, buf, take, split, piece=(0, 1), cols=None):
        self.p, self.buf, self.take = place, buf, take
        self.block = buf.shape[0] // place.shards
        self.rows = self.block // piece[1]
        self.first_row = piece[0] * self.rows
        self.cols = cols or pl.ds(0, buf.shape[1])
        self.split = split
        self.parts = (NEAR, CORE) if split else (CORE,)
        self.count = self.rows // 2 ** len(self.parts)
        self.deltas = subsets(shard_bits(place.shards))
        self.part = place.index(self.parts)
        self.first, self.second, self.third = [], [], []

    def view(self, owner, part):
        start = owner * self.block + self.first_row + part * self.count
        return self.buf.at[rows_at(start, self.count), self.cols]

    def start(self):
        for delta in self.deltas:
            v = self.view(self.p.y, self.part)
            self.first.append(remote(v, v, self.take(), self.p.flip(delta)))

    def spread(self):
        for n, delta in enumerate(self.deltas):
            self.first[n].wait_recv()
            v = self.view(self.p.flip(delta)[1], self.part)
            if self.split:
                self.second.append(remote(v, v, self.take(), self.p.flip((NEAR,))))
            self.third.append(remote(v, v, self.take(), self.p.flip((CORE,))))

    def pass_on(self):
        if self.split:
            for n, delta in enumerate(self.deltas):
                self.second[n].wait_recv()
                v = self.view(self.p.flip(delta)[1], self.p.index(self.parts, (NEAR,)))
                self.third.append(remote(v, v, self.take(), self.p.flip((CORE,))))

    def finish(self):
        for copy in self.third:
            copy.wait_recv()

    def sent(self):
        for copy in self.first + self.second + self.third:
            copy.wait_send()


def shard_bits(shards):
    bits, bit = [], shards // 2
    while bit >= 1:
        bits.append(("shard", bit))
        bit //= 2
    return tuple(bits)


def stream_bits(streams):
    bits, bit = [], 1
    while bit < streams:
        bits.append(("stream", bit))
        bit *= 2
    return tuple(bits)


def plan_total(sizes, rows, order, merge=False):
    shards = sizes[1]
    count, full, stages, shares = rows // shards, True, [], []
    for group in order:
        across = tuple(b for b in group if b[0] == "shard")
        along = tuple(b for b in group if b[0] == "stream")
        if along and count % (16 * 2 ** len(along)):
            groups = ([(across, ())] if across else []) + [((), (b,)) for b in along]
        else:
            groups = [(across, along)]
        for across, along in groups:
            scatter = count % (16 * 2 ** len(along)) == 0
            if scatter:
                count //= 2 ** len(along)
            full = full and not across
            stages.append((across + along, along if scatter else (), bool(across), shards if full else 1, count))
            if scatter and along:
                shares.insert(0, along)
    if merge and len(shares) > 2:
        shares = [tuple(b for group in shares[-2::-1] for b in group), shares[-1]]
    return stages, shares


class Total:
    def __init__(self, place, grad, total, slots, take, plan):
        self.p, self.grad, self.total, self.take = place, grad, total, take
        self.slots = slots
        self.stages, self.shares = plan
        self.rows = grad.shape[1]
        self.off, self.count, self.full = 0, self.rows, True
        self.live, self.done = [], []
        self.at = 0

    def begin(self):
        bits, along, across, blocks, piece = self.stages[self.at]
        slot = self.slots[self.at]
        self.live = []
        for n, delta in enumerate(subsets(bits)):
            s, y = who = self.p.flip(delta)
            rows = rows_at(self.off + self.p.index(along, delta) * piece, piece)
            if across:
                src = self.grad.at[pl.ds(y, 1), rows, :]
            elif self.full:
                src = self.grad.at[:, rows, :]
            else:
                src = self.grad.at[pl.ds(self.p.y, 1), rows, :]
            self.live.append(remote(src, slot.at[n], self.take(), who))
        self.off = self.off + self.p.index(along) * piece
        self.count = piece
        self.full = self.full and not across

    def add(self, last):
        slot = self.slots[self.at]
        rows = rows_at(self.off, self.count)
        here = slice(None) if self.full else pl.ds(self.p.y, 1)
        value = self.grad[here, rows, :].astype(F32)
        for n, copy in enumerate(self.live):
            copy.wait_recv()
            value = value + slot[n].astype(F32)
        if last:
            self.total[rows, :] = value[0].astype(BF)
        else:
            self.grad[here, rows, :] = value.astype(BF)
        self.done += self.live
        self.at += 1

    def share(self, bits):
        v = self.total.at[rows_at(self.off, self.count), :]
        self.live = [remote(v, v, self.take(), self.p.flip(delta)) for delta in subsets(bits)]
        self.off = self.off - self.p.index(bits) * self.count
        self.count *= 2 ** len(bits)

    def arrive(self):
        for copy in self.live:
            copy.wait_recv()
        self.done += self.live

    def steps(self):
        def middle():
            self.add(False)
            self.begin()

        def turn():
            self.add(True)
            self.share(self.shares[0])

        def later(bits):
            self.arrive()
            self.share(bits)

        out = [self.begin] + [middle] * (len(self.stages) - 1) + [turn]
        return out + [functools.partial(later, bits) for bits in self.shares[1:]] + [self.arrive]

    def sent(self):
        for copy in self.done:
            copy.wait_send()


class Everywhere:
    def __init__(self, place, table, slots, take, groups):
        self.p, self.table, self.slots, self.take, self.groups = place, table, slots, take, groups
        self.live, self.done, self.at = [], [], 0

    def begin(self):
        group, slot = self.groups[self.at], self.slots[self.at]
        mine = pl.ds(self.p.index(group), 1)
        slot[mine] = self.table[...][None]
        self.live = [remote(slot.at[mine], slot.at[mine], self.take(), self.p.flip(d)) for d in subsets(group)]

    def add(self):
        for copy in self.live:
            copy.wait_recv()
        self.done += self.live
        slot = self.slots[self.at]
        total = slot[0]
        for n in range(1, slot.shape[0]):
            total = total + slot[n]
        self.table[...] = total
        self.at += 1

    def steps(self):
        def middle():
            self.add()
            self.begin()

        return [self.begin] + [middle] * (len(self.groups) - 1) + [self.add]

    def sent(self):
        for copy in self.done:
            copy.wait_send()


GRADS = ("d0", "d1", "u0", "u1", "o", "qa", "qb")
WAYS = {"d0": "yx.z", "d1": "yx.z", "u0": "z.y.x", "u1": "y.x.z", "o": "x.y.z", "qa": "yx.z", "qb": "yx.z"}
RING = 4
TICKS = (
    ("d0",),
    ("d0",),
    ("u0",),
    ("u1", "d1", "u0"),
    (),
    (),
    ("d1",),
    (),
    (),
    (),
    (),
    (),
    ("o",),
    ("u1", "o", "d0"),
    (),
    (),
    (),
    ("qa", "d1"),
    ("qa",),
    (),
    ("d0", "u0"),
    ("u1",),
    ("d1",),
    ("o",),
    ("qb",),
    ("qa", "u0", "qb", "o"),
    (),
    (),
    (),
    ("u1",),
    (),
    ("d1",),
    (),
    ("o", "qa"),
    (),
    (),
    ("qb",),
    (),
    (),
    (),
    (),
    ("u0", "n", "d0", "u1", "n"),
    (),
    (),
    (),
    (),
    ("qa", "qb"),
    (),
    (),
    ("u0", "d0", "n"),
    ("o",),
    ("d0", "u1"),
    (),
    (),
    (),
    ("d1", "qa"),
    (),
    (),
    ("qa", "o", "d1", "qb", "u1", "o", "u1", "u0", "qb", "u0", "qb"),
)


def layer_kernel(
    sizes, plan, tok, mem, old, docs, cot, wqkv, wo, wu, wd, wc, norms, *rest
):
    moments, averages, rest = rest[:4], rest[4:8], rest[8:]
    xs, ct, lifted, newold, norm_total, kept, dK, dV, seen_at, gl, gres, res, *rest = rest
    tbuf, rest = rest[:7], rest[7:]
    (N, Q, K, V, PT, OT, act, gh, Dv, Wq, Wk, Wv, Wo, Wu, Wd, Wc, nblocks, ngrad, *rest) = rest
    gbuf, rest = rest[:7], rest[7:]
    gr, dO = gh.at[:, pl.ds(0, Wo.shape[1])], gh.at[:, pl.ds(Wo.shape[1], Wo.shape[1])]
    slots = []
    for stages, _ in plan["totals"]:
        slots.append(rest[: len(stages)])
        rest = rest[len(stages) :]
    nslots, rest = rest[: len(plan["groups"])], rest[len(plan["groups"]) :]
    send_ref, recv_ref, local_ref = rest
    place = Place(*sizes)
    send, recv, local = Sems(send_ref, plan["sems"]), Sems(recv_ref, plan["sems"]), Sems(local_ref, plan["local"])

    def pair():
        return send.take(), recv.take()

    shards = place.shards
    S, D = tok.shape
    M = mem.shape[0]
    H0 = M - REACH
    L = REACH + S
    T0 = REACH
    W = REACH + 128
    FF = Wu.shape[1]
    n_q = S // 128

    barrier = pltpu.get_barrier_semaphore()
    for bits in plan["partners"]:
        pl.semaphore_signal(barrier, inc=1, device_id=place.flip(bits), device_id_type=MESH)

    def fetch(src, dst):
        copy = pltpu.make_async_copy(src, dst, local.take())
        copy.start()
        return copy

    jobs = {}

    def bring(name, pieces, target, unit, ref):
        for n, (src, row, col) in enumerate(pieces):
            stage = ref.at[pl.ds((unit + n) * r1, r1), :]
            jobs.setdefault(name, []).append((fetch(src, stage), stage, target, row, col))

    r1 = wqkv.shape[0]
    pieces = unit_list(wqkv, wo, wu, wd)
    bring("k", [(pieces[1][0], 0, 0)], Wk, 1, kept)
    bring("v", [(pieces[2][0], 0, 0)], Wv, 2, kept)
    bring("q", pieces[0:1], Wq, 0, kept)
    tok_in = fetch(tok, xs.at[pl.ds(M, S), :])
    mem_in = fetch(mem, xs.at[pl.ds(0, M), :])
    bring("o", pieces[3:4], Wo, 3, kept)
    bring("u", pieces[4 : 4 + FF // D], Wu, 0, dV)
    bring("d", pieces[4 + FF // D :], Wd, 0, dK)
    stage = gl.at[pl.ds(0, wc.shape[0]), :]
    jobs["c"] = [(fetch(wc, stage), stage, Wc, 0, 0)]
    cot_in = fetch(cot, ct)
    old_in = fetch(old.at[pl.ds(S // 3, old.shape[0] - S // 3), :], newold.at[pl.ds(0, old.shape[0] - S // 3), :])

    nblocks[pl.ds(place.y, 1)] = jnp.concatenate(
        [norms[...].astype(BF).astype(F32), jnp.zeros((4, norms.shape[1]), F32)], axis=0
    )[None]

    def cast(name):
        for copy, stage, target, row, col in jobs[name]:
            copy.wait()
            here = rows_at(place.y * (target.shape[0] // shards) + row, stage.shape[0])
            target[here, pl.ds(col, 512)] = stage[...].astype(BF)

    cast("k")
    pl.semaphore_wait(barrier, len(plan["partners"]))
    own = nblocks.at[pl.ds(place.y, 1)]
    norm_copies = [remote(own, own, pair(), place.flip(delta)) for delta in subsets(shard_bits(shards))]
    gathers = {}

    def launch(name, buf, **piece):
        gathers[name] = Gather(place, buf, pair, plan["split"], **piece)
        gathers[name].start()

    launch("k", Wk)
    cast("v")
    launch("v", Wv)
    cast("q")
    launch("q", Wq)
    cast("o")
    launch("o", Wo)

    ids = docs[...].astype(F32)
    column = jnp.transpose(jnp.broadcast_to(ids, (8, ids.shape[1])))
    base = ids.shape[1] - L

    def see(b):
        key = column[base + 128 * b : base + 128 * b + W, 0:1]
        query = ids[:, base + T0 + 128 * b : base + T0 + 128 * b + 128]
        k = lax.broadcasted_iota(jnp.int32, (W, 128), 0)
        q = lax.broadcasted_iota(jnp.int32, (W, 128), 1) + T0
        seen_at[pl.ds(b // 4 * W, W), pl.ds(b % 4 * 128, 128)] = jnp.where((key == query) & (k <= q), 0.0, -1e30)

    for b in range(n_q):
        see(b)
    cast("u")
    for n in range(2):
        launch("u" + str(n), Wu, cols=pl.ds(n * FF // 2, FF // 2))
    for copy in norm_copies:
        copy.wait_recv()
    table = jnp.concatenate([nblocks[j] for j in range(shards)], axis=1)
    g1, b1, g2, b2 = table[0:1], table[1:2], table[2:3], table[3:4]

    tok_in.wait()
    mem_in.wait()

    def ln1(n):
        r = slice(n * L // 4, (n + 1) * L // 4)
        unit, _s = normalised(xs[H0 + r.start : H0 + r.stop, :].astype(F32))
        N[r, :] = (unit * g1 + b1).astype(BF)

    ln1(0)
    ln1(1)
    gathers["k"].spread()
    cast("d")
    for n in range(2):
        launch("d" + str(n), Wd, piece=(n, 2))
    gathers["v"].spread()
    ln1(2)
    ln1(3)
    gathers["q"].spread()
    cast("c")
    launch("c", Wc)
    gathers["k"].pass_on()
    gathers["o"].spread()
    gathers["v"].pass_on()
    gathers["k"].finish()
    for c in range(2):
        cs = slice(c * 256, c * 256 + 256)
        for r in (slice(0, L // 2), slice(L // 2, L)):
            K[r, cs] = nn(N[r, :], Wk[:, cs]).astype(BF)
    gathers["q"].pass_on()
    gathers["v"].finish()
    for c in range(2):
        cs = slice(c * 256, c * 256 + 256)
        for r in (slice(0, L // 2), slice(L // 2, L)):
            V[r, cs] = nn(N[r, :], Wv[:, cs]).astype(BF)
    gathers["o"].pass_on()
    gathers["q"].finish()
    for c in range(2):
        cs = slice(c * 256, c * 256 + 256)
        Q[:, cs] = (nn(N[T0:, :], Wq[:, cs]).astype(BF).astype(F32) * 0.125).astype(BF)

    def scores(i, u, slot):
        qb, p = i // 2, (i % 2) * 2 + u
        q0, l0 = rows_at(qb * 128, 128, 128), rows_at(p * 128, 128, 128)
        s = nt(K[rows_at(qb * 128, W, 128), l0], two_heads(Q[q0, l0]))
        seen = seen_at[rows_at(qb // 4 * W, W), rows_at(qb % 4 * 128, 128, 128)]
        raw[slot][0:W, u * 256 : u * 256 + 256] = s + jnp.concatenate([seen, seen], axis=1)

    def attend(i, u, slot):
        qb, p = i // 2, (i % 2) * 2 + u
        q0, l0 = rows_at(qb * 128, 128, 128), rows_at(p * 128, 128, 128)
        cs = slice(u * 256, u * 256 + 256)
        pieces = [slice(c, c + 64) for c in range(0, W, 64)]
        top, total = None, None
        for r in pieces:
            part = jnp.max(raw[slot][r, cs].reshape(8, 8, 256), axis=0)
            top = part if top is None else jnp.maximum(top, part)
        top = jnp.max(top, axis=0, keepdims=True)
        for r in pieces:
            e = jnp.exp(raw[slot][r, cs] - top)
            raw[slot][r, cs] = e
            part = jnp.sum(e.reshape(8, 8, 256), axis=0)
            total = part if total is None else total + part
        scale = 1.0 / jnp.sum(total, axis=0, keepdims=True)
        for r in pieces:
            PT[p * n_q + qb, r, :] = (raw[slot][r, cs] * scale).astype(BF)
        OT[l0, q0] = own_halves(tn(V[rows_at(qb * 128, W, 128), l0], PT[p * n_q + qb])).astype(BF)

    def attend_two(j, _):
        for slot in range(2):
            for u in range(2):
                scores(jnp.minimum(2 * j + slot + 1, 2 * n_q - 1), u, 1 - slot)
            for u in range(2):
                attend(2 * j + slot, u, slot)
        return 0

    raw = (gl, gres)
    for u in range(2):
        scores(0, u, 0)
    gathers["u0"].spread()
    lax.fori_loop(0, 2, attend_two, 0)
    gathers["u1"].spread()
    lax.fori_loop(2, 4, attend_two, 0)
    gathers["d0"].spread()
    gathers["u0"].pass_on()
    lax.fori_loop(4, n_q, attend_two, 0)
    gathers["d1"].spread()
    gathers["u1"].pass_on()
    gathers["o"].finish()

    for c in range(2):
        cs = slice(c * 256, c * 256 + 256)
        res[:, cs] = xs[M:, cs].astype(F32) + tn(OT[...], Wo[:, cs])

    for n in range(3):
        r = slice(n * S // 3, (n + 1) * S // 3)
        unit, _s = normalised(res[r, :])
        lifted[r, :] = (unit * g2 + b2).astype(BF)
    gathers["d0"].pass_on()
    cot_in.wait()
    gathers["u0"].finish()
    gathers["u1"].finish()

    tiles = FF // 256

    def tile_at(i):
        return rows_at((i + place.y * (tiles // shards)) % tiles * 256, 256, 256)

    def ffn_in(i, slot):
        here = slice(slot * 256, slot * 256 + 256)
        dK[0:S, here] = nn(lifted[...], Wu[:, tile_at(i)])
        dV[0:S, here] = nt(ct[...], Wd[tile_at(i), :])

    def ffn_out(i, slot):
        here = slice(slot * 256, slot * 256 + 256)
        for n in range(0, S, 128):
            r = slice(n, n + 128)
            h, ga = dK[r, here], dV[r, here]
            h2 = h * h
            hp = 0.5 + 0.5 * jnp.tanh(h * (GELU_C + (GELU_C * GELU_A) * h2))
            a = h * hp
            slope = hp + (a - a * hp) * (2.0 * GELU_C + (6.0 * GELU_C * GELU_A) * h2)
            act[r, tile_at(i)] = a.astype(BF)
            gh[r, tile_at(i)] = (ga * slope).astype(BF)

    def put(ref, start, value):
        rows = value.shape[0]
        if rows > ref.shape[1]:
            n = rows // ref.shape[1]
            ref[pl.ds(start // ref.shape[1], n)] = value.astype(BF).reshape(n, ref.shape[1], value.shape[1])
        else:
            ref[start // ref.shape[1], rows_at(start % ref.shape[1], rows), :] = value.astype(BF)

    def put_all(ref, cols, value):
        ref[:, :, cols] = value.astype(BF).reshape(ref.shape[0], ref.shape[1], value.shape[1])

    def grad_down(ref, col, low, high):
        def body(i, _):
            first = (2 * i + place.y * (tiles // shards)) % tiles
            put(ref, first * 256, tn(act[:, rows_at(first * 256, 512, 256)], ct[:, col : col + 256]))
            return 0

        lax.fori_loop(low // 2, high // 2, body, 0)

    own_tiles = tiles // shards
    early = own_tiles if own_tiles % 2 == 0 else 0
    ffn_in(0, 0)
    for i in range(tiles):
        if i + 1 == own_tiles:
            ffn_out(i, i % 2)
            for n in range(2):
                grad_down(gbuf[n], n * D // 2, 0, early)
            gathers["d1"].pass_on()
            gathers["d0"].finish()
            gathers["d1"].finish()
            ffn_in(i + 1, (i + 1) % 2)
            continue
        if i + 1 < tiles:
            ffn_in(i + 1, (i + 1) % 2)
        ffn_out(i, i % 2)
    gathers["c"].spread()

    homes = unit_homes(plan["work"], r1, 2 * len(pieces))
    old_units = [p[0] for p in unit_list(*moments)] + [p[0] for p in unit_list(*averages)]
    work = (dK, dV, seen_at, gl, gres, res)
    refill = []

    def bring_old(index):
        for src, (where, row) in zip(old_units, homes):
            if where == index:
                refill.append(fetch(src, work[index].at[pl.ds(row, r1), :]))

    sums = {
        name: Total(place, gbuf[i], tbuf[i], slots[i], pair, plan["totals"][i]) for i, name in enumerate(GRADS)
    }
    sums["n"] = Everywhere(place, ngrad, nslots, pair, plan["groups"])
    waiting = {name: sums[name].steps() for name in sums}
    clock = []

    def go(names):
        for name in names:
            if not waiting[name]:
                continue
            waiting[name].pop(0)()

    def tick():
        if len(clock) < len(plan["ticks"]):
            go(plan["ticks"][len(clock)])
        clock.append(0)

    for n in range(2):
        grad_down(gbuf[n], n * D // 2, early, tiles)
        tick()
    for n in range(2):
        for c in range(2):
            piece = gh[:, n * 1024 + c * 512 : n * 1024 + c * 512 + 512]
            put_all(gbuf[2 + n], slice(c * 512, c * 512 + 512), tn(lifted[...], piece))
        tick()
    for c in range(2):
        cs = slice(c * 256, c * 256 + 256)
        gl[:, cs] = nt(gh[...], Wu[cs, :])
        tick()

    def by_eight(x):
        return jnp.sum(x.reshape(x.shape[0] // 8, 8, D), axis=0)

    second = [jnp.zeros((8, D), F32)] * 2
    for n in range(3):
        r = slice(n * S // 3, (n + 1) * S // 3)
        unit, scale = normalised(res[r, :])
        gy = gl[r, :]
        x = ct[r, :].astype(F32) + norm_back(gy, unit, scale, g2)
        gres[r, :] = x
        gr[r, :] = x.astype(BF)
        second = [second[0] + by_eight(gy * unit), second[1] + by_eight(gy)]
        tick()
    put_all(gbuf[4], slice(0, D), nn(OT[...], gr[...]))
    tick()
    for c in range(2):
        cs = slice(c * 256, c * 256 + 256)
        dO[:, cs] = nt(gr[...], Wo[cs, :]).astype(BF)
    for c in range(2):
        cs = slice(c * 256, c * 256 + 256)
        dt = nt(Wo[cs, :], gr[...]).astype(BF).astype(F32) * OT[cs, :].astype(F32)
        for h in range(4):
            Dv[c * 2 + h // 2, h % 2 : h % 2 + 1, :] = jnp.sum(dt[h * 64 : h * 64 + 64], axis=0, keepdims=True)
    dK[...] = jnp.zeros_like(dK)
    dV[...] = jnp.zeros_like(dV)
    tick()

    def back_in(i, u, slot):
        qb, p = i % n_q, i // n_q * 2 + u
        q0, l0 = slice(qb * 128, qb * 128 + 128), slice(p * 128, p * 128 + 128)
        raw[slot][0:W, u * 256 : u * 256 + 256] = nt(V[qb * 128 : qb * 128 + W, l0], two_heads(dO[q0, l0]))

    def back_out(i, u, slot):
        qb, p = i % n_q, i // n_q * 2 + u
        q0, l0, keys = slice(qb * 128, qb * 128 + 128), slice(p * 128, p * 128 + 128), slice(qb * 128, qb * 128 + W)
        mean = jnp.concatenate([Dv[p, 0:1, q0], Dv[p, 1:2, q0]], axis=1)
        probs = PT[p * n_q + qb]
        ds = (probs.astype(F32) * (raw[slot][0:W, u * 256 : u * 256 + 256] - mean)).astype(BF)
        dV[keys, l0] += nn(probs, two_heads(dO[q0, l0]))
        dK[keys, l0] += nn(ds, two_heads(Q[q0, l0]))
        dq = own_halves(tn(K[keys, l0], ds)) * 0.125
        Q[q0, l0] = jnp.transpose(dq).astype(BF)

    raw = (gl, seen_at)
    for u in range(2):
        back_in(0, u, 0)
    for i in range(2 * n_q):
        if i + 1 < 2 * n_q:
            for u in range(2):
                back_in(i + 1, u, (i + 1) % 2)
        for u in range(2):
            back_out(i, u, i % 2)
        tick()
        if i % n_q == n_q - 1:
            quad = i // n_q
            cs = slice(quad * 256, quad * 256 + 256)
            K[:, cs] = dK[0:L, cs].astype(BF)
            V[:, cs] = dV[0:L, cs].astype(BF)
            g = gbuf[5 + quad]
            put_all(g, slice(0, 256), tn(N[T0:, :], Q[:, cs]))
            put_all(g, slice(256, 512), tn(N[...], K[:, cs]))
            put_all(g, slice(512, 768), tn(N[...], V[:, cs]))
            tick()

    for index in range(1, 4):
        bring_old(index)
    for c in range(2):
        cs = slice(c * 256, c * 256 + 256)
        for r in (slice(0, L // 2), slice(L // 2, L)):
            dK[r, cs] = nt(K[r, :], Wk[cs, :])
            dK[r, cs] += nt(V[r, :], Wv[cs, :])
        dK[T0:L, cs] += nt(Q[...], Wq[cs, :])
        tick()

    first = [jnp.zeros((8, D), F32)] * 2
    for low, high in [(0, T0 // 2), (T0 // 2, T0)] + [(T0 + n * S // 3, T0 + (n + 1) * S // 3) for n in range(3)]:
        unit, scale = normalised(xs[H0 + low : H0 + high, :].astype(F32))
        gy = dK[low:high, :]
        if low >= T0:
            r = slice(low - T0, high - T0)
            lifted[r, :] = (gres[r, :] + norm_back(gy, unit, scale, g1)).astype(BF)
        first = [first[0] + by_eight(gy * unit), first[1] + by_eight(gy)]
        if high == L:
            rows = [jnp.sum(x, axis=0, keepdims=True) for x in first + second]
            ngrad[...] = jnp.concatenate(rows + [jnp.zeros((4, D), F32)], axis=0)
        tick()
    bring_old(0)
    bring_old(4)

    for c in range(2):
        cs = slice(c * 256, c * 256 + 256)
        ct[:, cs] = (res[:, cs] + nn(act[...], Wd[:, cs])).astype(BF)
        tick()
    bring_old(5)
    gathers["c"].pass_on()
    gathers["c"].finish()
    squeezed = None
    for t in range(3):
        row = lax.broadcasted_iota(jnp.int32, (S // 3, S), 0) * 3 + t
        pick = jnp.where(lax.broadcasted_iota(jnp.int32, (S // 3, S), 1) == row, 1.0, 0.0).astype(BF)
        term = nn(nn(pick, xs[pl.ds(0, S), :]).astype(BF), Wc[t * D : (t + 1) * D, :])
        squeezed = term if squeezed is None else squeezed + term
        tick()
    newold[pl.ds(old.shape[0] - S // 3, S // 3), :] = squeezed.astype(BF)
    while len(clock) < len(plan["ticks"]):
        tick()
    while any(waiting.values()):
        go([name for name in waiting if waiting[name]])
    final = ngrad[...]
    width = norms.shape[1]
    mine = final[:, 0:width]
    for j in range(1, shards):
        mine = jnp.where(place.y == j, final[:, j * width : (j + 1) * width], mine)
    norm_total[...] = mine

    for copy in refill + [old_in]:
        copy.wait()
    for part in list(gathers.values()) + list(sums.values()):
        part.sent()
    for copy in norm_copies:
        copy.wait_send()


def wide_units(wu, wd, r, w):
    units = [(wu.at[:, pl.ds(c * w, w)], 0, c * w) for c in range(wu.shape[1] // w)]
    return units + [(wd.at[pl.ds(n, r), :], n, 0) for n in range(0, wd.shape[0], r)]


def unit_list(wqkv, wo, wu, wd):
    r, w = wo.shape
    return [(wqkv.at[:, pl.ds(c * w, w)], 0, 0) for c in range(3)] + [(wo, 0, 0)] + wide_units(wu, wd, r, w)


def unit_homes(work, r, count):
    homes = [(i, row) for i, rows in enumerate(work) for row in range(0, rows - r + 1, r)]
    assert len(homes) >= count
    return homes[:count]


def work_rows(S):
    big = -(-(REACH + S) // 256) * 256
    return (big, big, big, S, S, S)


def run_layer(sizes, tokens, memory, cmemory, docs, cotangent, wqkv, wo, wu, wd, wc, norms, moments, averages):
    streams, shards = sizes
    S, D = tokens.shape
    M = memory.shape[0]
    L = REACH + S
    W = REACH + 128
    FF = wu.shape[1]
    n_q = S // 128
    shapes = [(FF, D // 2)] * 2 + [(D, FF // 2)] * 2 + [(D, D)] + [(D, 3 * D // 2)] * 2
    shapes = [(shards, rows // shards, cols) for rows, cols in shapes]
    across, along = shard_bits(shards), stream_bits(streams)
    far = [along[i : i + 2] for i in range(2, len(along), 2)]
    axes = {"c": [(CORE,)], "y": [across], "x": [(NEAR,)], "yx": [across + (NEAR,)], "z": far}
    totals = []
    for i, name in enumerate(GRADS):
        way = WAYS[name].rstrip("+")
        order = [group for axis in ["c"] + way.split(".") for group in axes[axis]]
        totals.append(plan_total(sizes, FF if i < 2 else D, order, WAYS[name].endswith("+")))
    groups = [across + (NEAR, CORE)] + far
    used = [subsets(across), subsets((NEAR, CORE))] + [subsets(g) for g in groups]
    for stages, shares in totals:
        used += [subsets(stage[0]) for stage in stages] + [subsets(bits) for bits in shares]
    partners = sorted({tuple(sorted(delta)) for some in used for delta in some})
    sems = 9 * 4 * (shards - 1) + len(subsets(across)) + sum(len(subsets(g)) for g in groups)
    for stages, shares in totals:
        sems += sum(len(subsets(stage[0])) for stage in stages) + sum(len(subsets(bits)) for bits in shares)
    plan = {
        "totals": totals,
        "groups": groups,
        "partners": partners,
        "ticks": TICKS,
        "sems": sems,
        "local": 64,
        "work": work_rows(S),
        "split": True,
    }
    f32, bf = (lambda *s: pltpu.VMEM(s, F32)), (lambda *s: pltpu.VMEM(s, BF))
    scratch = [
        bf(L, D), bf(S, D), bf(L, D), bf(L, D), bf((HEADS // 2) * n_q, W, 256), bf(D, S), bf(S, FF), bf(S, FF),
        f32(HEADS // 2, 2, S), bf(D, D), bf(D, D), bf(D, D), bf(D, D), bf(D, FF), bf(FF, D), bf(3 * D, D),
        f32(shards, 8, norms.shape[1]), f32(8, D),
    ]
    scratch += [bf(*s) for s in shapes]
    for (stages, _), s in zip(totals, shapes):
        scratch += [bf(len(subsets(bits)), blocks, piece, s[2]) for bits, _b, _a, blocks, piece in stages]
    scratch += [f32(2 ** len(g), 8, D) for g in groups]
    scratch += [pltpu.SemaphoreType.DMA((sems,)), pltpu.SemaphoreType.DMA((sems,)), pltpu.SemaphoreType.DMA((64,))]
    anywhere = pl.BlockSpec(memory_space=pl.ANY)
    vmem = pl.BlockSpec(memory_space=pltpu.VMEM)
    units = 3 + 1
    out_shape = [bf(M + S, D), bf(S, D), bf(S, D), bf(*cmemory.shape), f32(8, norms.shape[1]), f32(units * wo.shape[0], D)]
    out_shape += [f32(rows, D) for rows in plan["work"]]
    out_shape += [bf(s[1], s[2]) for s in shapes]
    room = 253 * 256 * 1024 - sum(x.inner_aval.size * x.inner_aval.dtype.itemsize for x in out_shape)
    big = [pltpu.with_memory_space_constraint(x, pltpu.HBM) for x in (tokens, memory, cmemory)]
    more = [pltpu.with_memory_space_constraint(x, pltpu.HBM) for x in (cotangent, wqkv, wo, wu, wd, wc)]
    later = [pltpu.with_memory_space_constraint(x, pltpu.HBM) for x in (*moments, *averages)]
    return pl.pallas_call(
        functools.partial(layer_kernel, sizes, plan),
        out_shape=out_shape,
        in_specs=[anywhere] * 3 + [vmem] + [anywhere] * 6 + [vmem] + [anywhere] * 8,
        out_specs=[vmem] * len(out_shape),
        scratch_shapes=scratch,
        compiler_params=pltpu.CompilerParams(
            collective_id=0, has_side_effects=True, vmem_limit_bytes=room
        ),
        name="layer",
    )(*big, docs, *more, norms, *later)


def renew(grad, moment, average, master):
    momentum = MOMENTUM * moment + (1.0 - MOMENTUM) * grad
    updated = master - RATE * ((1.0 - MOMENTUM) * grad + MOMENTUM * momentum)
    smooth = SMOOTH * average + (1.0 - SMOOTH) * updated
    return momentum, smooth, updated


def update_kernel(
    wu, wd, xs, output, tgrad, newold, norm_grad, kept, dK, dV, seen_at, gl, gres, res, d0, d1, u0, u1, o, qa, qb, w_norm, v_norm, a_norm,
    *rest
):
    work = (dK, dV, seen_at, gl, gres, res)
    results, rest = [rest[n * 4 : n * 4 + 4] for n in range(4)], rest[16:]
    norm_out, lifted_out, rest = rest[:4], rest[4], rest[5:]
    out_to, memory_to, cmemory_to, tgrad_to, stage, late, small_in, small_out, lifted_stage, sems = rest
    sem = iter(range(sems.shape[0]))
    copies = []

    def store(src, dst):
        copies.append(pltpu.make_async_copy(src, dst, sems.at[next(sem)]))
        copies[-1].start()

    r, D = o.shape
    late_in = []
    for n, (src, _r, _c) in enumerate(wide_units(wu, wd, r, D)):
        late_in.append(pltpu.make_async_copy(src, late.at[pl.ds(n * r, r), :], sems.at[next(sem)]))
        late_in[-1].start()
    store(output, out_to)
    store(xs.at[pl.ds(xs.shape[0] - memory_to.shape[0], memory_to.shape[0]), :], memory_to)
    store(newold, cmemory_to)
    store(tgrad, tgrad_to)
    small = []
    for n, src in enumerate((w_norm, v_norm, a_norm)):
        small.append(pltpu.make_async_copy(src, small_in.at[n], sems.at[next(sem)]))
        small[-1].start()
    for copy in small:
        copy.wait()
    g = norm_grad[0:4, :]
    lifted_stage[...] = g[2:4]
    store(lifted_stage, lifted_out)
    for n, value in enumerate((g,) + renew(g, small_in[1], small_in[2], small_in[0])):
        small_out[n] = value
        store(small_out.at[n], norm_out[n])
    before = len(copies)

    places = list(zip(*[[p[0] for p in unit_list(*arrays)] for arrays in results]))
    homes = unit_homes([ref.shape[0] for ref in work], r, 2 * len(places))
    half = D // 2

    def total(n):
        if n < 3:
            return jnp.concatenate([t[:, n * half : n * half + half] for t in (qa, qb)], axis=1)
        if n == 3:
            return o[...]
        n -= 4
        if n < 2 * u0.shape[1] // D:
            per = u0.shape[1] // D
            return (u0, u1)[n // per][:, n % per * D : n % per * D + D]
        n -= 2 * u0.shape[1] // D
        return jnp.concatenate([t[n * r : n * r + r, :] for t in (d0, d1)], axis=1)

    def old(n):
        where, row = homes[n]
        return work[where][pl.ds(row, r), :]

    here = kept.shape[0] // r
    for n in range(len(places)):
        if n >= here:
            late_in[n - here].wait()
        master = kept[pl.ds(n * r, r), :] if n < here else late[pl.ds((n - here) * r, r), :]
        grad = total(n).astype(F32)
        new = (grad,) + renew(grad, old(n), old(len(places) + n), master)
        for m, value in enumerate(new):
            if n >= RING:
                copies[before + (n - RING) * 4 + m].wait()
            slot = stage.at[n % RING * 4 + m]
            slot[...] = value
            store(slot, places[n][m])
    for copy in copies[:before] + copies[before + max(0, len(places) - RING) * 4 :]:
        copy.wait()


def run_update(from_layer, masters, norm_old, memory):
    r, w = masters[1].shape
    units = sum(m.size for m in masters) // (r * w)
    anywhere = pl.BlockSpec(memory_space=pl.ANY)
    vmem = pl.BlockSpec(memory_space=pltpu.VMEM)
    same = [jax.ShapeDtypeStruct(m.shape, F32) for m in masters]
    small = jax.ShapeDtypeStruct(norm_old[0].shape, F32)
    lifted = jax.ShapeDtypeStruct((2, small.shape[1]), F32)
    bf = lambda x: jax.ShapeDtypeStruct(x.shape, BF)
    keep = [bf(from_layer[1]), bf(memory), bf(from_layer[3]), bf(from_layer[2])]
    held = [pltpu.with_memory_space_constraint(x, pltpu.VMEM) for x in from_layer]
    return pl.pallas_call(
        update_kernel,
        out_shape=same * 4 + [small] * 4 + [lifted] + keep,
        in_specs=[anywhere] * 2 + [vmem] * len(held) + [anywhere] * 3,
        out_specs=[anywhere] * 25,
        scratch_shapes=[
            pltpu.VMEM((RING * 4, r, w), F32),
            pltpu.VMEM(((units - 4) * r, w), F32),
            pltpu.VMEM((3, *small.shape), F32),
            pltpu.VMEM((4, *small.shape), F32),
            pltpu.VMEM(lifted.shape, F32),
            pltpu.SemaphoreType.DMA((units * 5 + 12,)),
        ],
        compiler_params=pltpu.CompilerParams(vmem_limit_bytes=18 * 1024 * 1024),
        name="update",
    )(*[pltpu.with_memory_space_constraint(x, pltpu.HBM) for x in masters[2:]], *held, *[pltpu.with_memory_space_constraint(x, pltpu.HBM) for x in norm_old])


def on_device(
    sizes, tokens, memory, cmemory, doc_ids, cotangent,
    qkv_weight, out_weight, up_weight, down_weight, conv_weight, norm_params,
    qkv_moment, out_moment, up_moment, down_moment, norm_moment,
    qkv_average, out_average, up_average, down_average, norm_average,
):
    masters = (qkv_weight, out_weight, up_weight, down_weight)
    from_layer = run_layer(
        sizes, tokens[0], memory[0], cmemory[0], doc_ids, cotangent[0], *masters, conv_weight, norm_params.T,
        (qkv_moment, out_moment, up_moment, down_moment), (qkv_average, out_average, up_average, down_average),
    )
    new = run_update(from_layer, masters, (norm_params.T, norm_moment.T, norm_average.T), memory[0])
    grads, momenta, smooths, updates = new[0:4], new[4:8], new[8:12], new[12:16]
    norms = [x.T for x in new[16:20]]
    lifted = new[20].T
    out, new_memory, new_cmemory, token_grad = new[21:25]
    return (
        out[None], new_memory[None], new_cmemory[None], token_grad[None],
        *grads, norms[0], *momenta, norms[1], *smooths, norms[2], *updates, norms[3], lifted,
    )


def solution(mesh):
    sizes = (mesh.shape["stream"], mesh.shape["shard"])
    both = ("stream", "shard")
    wide = P(both, None, None)
    rows = P("shard", None)
    return jax.shard_map(
        functools.partial(on_device, sizes),
        mesh=mesh,
        in_specs=(wide, wide, wide, P(both, None), wide) + (rows,) * 16,
        out_specs=(wide,) * 4 + (rows,) * 21,
        check_vma=False,
    )
```
